32 devices in a mesh: dp: 16 (over z, y, x), tensor: 2 (over core).
Axes of the slice: x: 2, y: 2, z: 4, core: 2. Of those that a mesh axis runs over, the one named last changes fastest.
Arguments:
- tokens: bfloat16 [2, 2048, 1024], P(None, 'dp'), may hold values from -6 to 6
- cu_seqlens: int32 [2, 32], replicated, may hold values from 0 to 2048, as said below
- attn_gain: bfloat16 [2, 1024], P(None, 'dp'), may hold values from 0.5 to 1.5
- mlp_gain: bfloat16 [2, 1024], P(None, 'dp'), may hold values from 0.5 to 1.5
- w_qkv: bfloat16 [2, 3, 1024, 1024], P(None, None, 'dp', 'tensor'), may hold values from -0.1875 to 0.1875
- w_attn_out: bfloat16 [2, 1024, 1024], P(None, 'dp', 'tensor'), may hold values from -2 to 2
- w_ffn_in: bfloat16 [2, 2, 1024, 2624], P(None, None, 'dp', 'tensor'), may hold values from -0.1875 to 0.1875
- w_ffn_out: bfloat16 [2, 1024, 2624], P(None, 'dp', 'tensor'), may hold values from -0.125 to 0.125
- out_grad: bfloat16 [2, 2048, 1024], P(None, 'dp'), may hold values from -6 to 6
Outputs:
- hidden_out: bfloat16 [2, 2048, 1024], P(None, 'dp')
- input_grad: float32 [2, 2048, 1024], P(None, 'dp')
- attn_gain_grad: float32 [2, 1024], P(None, 'dp')
- mlp_gain_grad: float32 [2, 1024], P(None, 'dp')
- w_qkv_grad: float32 [2, 3, 1024, 1024], P(None, None, 'dp', 'tensor')
- w_attn_out_grad: float32 [2, 1024, 1024], P(None, 'dp', 'tensor')
- w_ffn_in_grad: float32 [2, 2, 1024, 2624], P(None, None, 'dp', 'tensor')
- w_ffn_out_grad: float32 [2, 1024, 2624], P(None, 'dp', 'tensor')
The draws below stay inside these ranges and needn't reach their ends.
Inputs may be any that keep to these rules, and one draw needn't show every extreme that they name: `cu_seqlens`: in each micro-batch the 32 boundaries rise strictly from 0 to 2048; no document has more than 128 tokens and some document has exactly 128; no interior boundary is a multiple of 128, and every aligned block of 128 tokens holds one or two interior boundaries.
All inputs are finite; a program needn't handle non-finite values.
Results may differ from the reference program's by a relative error of at most 0.025.
Values may be sent and summed in bfloat16 or wider, within the bound.
No kernel may reach another device: no remote copies, remote signals or barrier semaphores. Data moves between devices by JAX's collectives and lax.ppermute only.
A program may use at most 256 MiB of HBM per device.

```python
import math
import jax
import jax.numpy as jnp
from jax import lax

D = 1024
H = 16
HD = 64
FF = 2624
HALF = 64
LAYERS = 2
MB = 2
TOK_DEV = 128
TOKENS = 2048
DOCS = 31


def bounds_one(key):
    key_left, key_right, key_long = jax.random.split(key, 3)
    edge_count = (DOCS - 1) // 2
    lowest = TOK_DEV // 16
    highest = 7 * TOK_DEV // 16 + 1
    left_part = jax.random.randint(key_left, (edge_count,), lowest, highest, dtype=jnp.int32)
    right_part = jax.random.randint(key_right, (edge_count,), lowest, highest, dtype=jnp.int32)
    longest = jax.random.randint(key_long, (), 0, edge_count, dtype=jnp.int32)
    picked = jnp.arange(edge_count, dtype=jnp.int32) == longest
    left_part = jnp.where(picked, TOK_DEV // 2, left_part)
    right_part = jnp.where(picked, TOK_DEV // 2, right_part)
    edges = (jnp.arange(edge_count, dtype=jnp.int32) + 1) * TOK_DEV
    inner = jnp.stack([edges - left_part, edges + right_part], axis=1).reshape(-1)
    first = jnp.zeros((1,), jnp.int32)
    final = jnp.full((1,), TOKENS, jnp.int32)
    return jnp.concatenate([first, inner, final]).astype(jnp.int32)


def draw_cu_seqlens(key, part):
    key = jax.random.fold_in(key, 7)
    return jax.vmap(bounds_one)(jax.random.split(key, MB))


def levels(key, extent, cuts, low, largest):
    def one(position, parts):
        steps = jax.random.uniform(jax.random.fold_in(jax.random.fold_in(key, 6), position), (parts,), jnp.float32, low / len(cuts), largest / len(cuts))
        return jnp.repeat(jnp.exp(steps), extent[position] // parts).reshape((-1,) + (1,) * (len(extent) - position - 1))

    level = one(*cuts[0])
    for cut in cuts[1:]:
        level = level * one(*cut)
    return level


def normal_values(rng, shape, width, most, shards=(), held_as=jnp.bfloat16):
    entries = width * jax.random.normal(rng, shape, jnp.float32)
    if shards:
        entries = entries * levels(rng, shape, shards, -0.22, 0.18)
    return jnp.clip(entries, -most, most).astype(held_as)


def setup_inputs(seed: int = 0) -> dict:
    arg_keys = jax.random.split(jax.random.key(seed), 10)
    return {
        "tokens": normal_values(arg_keys[0], (MB, TOKENS, D), 1.0, 6.0, ((1, 16),)),
        "cu_seqlens": draw_cu_seqlens(jax.random.fold_in(arg_keys[9], 71), 0),
        "attn_gain": jnp.clip(1.0 + 0.1 * jax.random.normal(arg_keys[2], (LAYERS, D), jnp.float32), 0.5, 1.5).astype(jnp.bfloat16),
        "mlp_gain": jnp.clip(1.0 + 0.1 * jax.random.normal(arg_keys[3], (LAYERS, D), jnp.float32), 0.5, 1.5).astype(jnp.bfloat16),
        "w_qkv": normal_values(arg_keys[4], (LAYERS, 3, D, H * HD), D ** -0.5, 0.1875, ((2, 16), (3, 2))),
        "w_attn_out": normal_values(arg_keys[5], (LAYERS, D, H * HD), 8 ** -0.5, 2.0, ((1, 16), (2, 2))),
        "w_ffn_in": normal_values(arg_keys[6], (LAYERS, 2, D, FF), D ** -0.5, 0.1875, ((2, 16), (3, 2))),
        "w_ffn_out": normal_values(arg_keys[7], (LAYERS, D, FF), FF ** -0.5, 0.125, ((1, 16), (2, 2))),
        "out_grad": normal_values(arg_keys[8], (MB, TOKENS, D), 1.0, 6.0, ((1, 16),)),
    }


MASKED_SCORE = -1e+30
PRECISE_DOT = lax.Precision.HIGHEST

@jax.custom_vjp
def low(v):
    return lax.optimization_barrier(v.astype(jnp.bfloat16)).astype(jnp.float32)

@jax.custom_vjp
def low_back(v):
    return v

def low_keep(v):
    return (low(v), None)

def low_pass(kept, grad):
    return (grad,)

def back_keep(v):
    return (v, None)

def back_low(kept, grad):
    return (low(grad),)
low.defvjp(low_keep, low_pass)
low_back.defvjp(back_keep, back_low)

def layer_norm(values, scale_row):
    row_mean = lax.optimization_barrier(jnp.mean(values, axis=-1, keepdims=True))
    centered = values - row_mean
    variance = lax.optimization_barrier(jnp.mean(centered * centered, axis=-1, keepdims=True))
    return centered * lax.rsqrt(variance + 1e-05) * scale_row

def rotate(values, offsets, rope_base):
    half_dim = values.shape[-1] // 2
    inv_freq = rope_base ** (-(jnp.arange(half_dim, dtype=jnp.float32) * 2.0 / values.shape[-1]))
    angles = offsets.astype(jnp.float32)[:, None] * inv_freq[None, :]
    cosine = jnp.cos(angles)[:, None, :]
    sine_part = jnp.sin(angles)[:, None, :]
    first = values[..., :half_dim]
    second = values[..., half_dim:]
    return jnp.concatenate([first * cosine - second * sine_part, second * cosine + first * sine_part], axis=-1)

def doc_info(bounds, token_index):
    inside = (token_index >= 0) & (token_index < bounds[-1])
    doc_ids = lax.optimization_barrier(jnp.sum((token_index[:, None] >= bounds[None, 1:-1]).astype(jnp.int32), axis=1)).astype(jnp.int32)
    doc_start = lax.optimization_barrier(jnp.max(jnp.where(token_index[:, None] >= bounds[None, :-1], bounds[None, :-1], 0), axis=1)).astype(jnp.int32)
    return (jnp.where(inside, doc_ids, -1).astype(jnp.int32), (token_index - doc_start).astype(jnp.int32))

def attend(queries, key_rows, value_rows, doc_ids, windowed):
    total_rows = queries.shape[0]
    block_rows = math.gcd(total_rows, 512)
    band_rows = block_rows + 2 * TOK_DEV
    token_index = jnp.arange(total_rows, dtype=jnp.int32)
    padded_keys = jnp.pad(key_rows, ((TOK_DEV, TOK_DEV), (0, 0), (0, 0)))
    padded_values = jnp.pad(value_rows, ((TOK_DEV, TOK_DEV), (0, 0), (0, 0)))
    padded_docs = jnp.pad(doc_ids, (TOK_DEV, TOK_DEV), constant_values=-1).astype(jnp.int32)
    padded_index = (jnp.arange(total_rows + 2 * TOK_DEV, dtype=jnp.int32) - TOK_DEV).astype(jnp.int32)

    def one_block(block_data):
        q_rows, q_docs, q_index = block_data
        start = q_index[0].astype(jnp.int32)
        band_keys = lax.dynamic_slice_in_dim(padded_keys, start, band_rows, 0)
        band_values = lax.dynamic_slice_in_dim(padded_values, start, band_rows, 0)
        band_docs = lax.dynamic_slice_in_dim(padded_docs, start, band_rows, 0)
        band_index = lax.dynamic_slice_in_dim(padded_index, start, band_rows, 0)
        logits = low_back(0.125 * jnp.einsum('qhd,khd->hqk', q_rows, band_keys, precision=PRECISE_DOT))
        allowed = q_docs[:, None] == band_docs[None, :]
        if windowed:
            allowed = allowed & (jnp.abs(q_index[:, None] - band_index[None, :]) <= HALF)
        masked = jnp.where(allowed[None], logits, MASKED_SCORE)
        weights_b = low(jax.nn.softmax(masked, axis=-1))
        return jnp.einsum('hqk,khd->qhd', weights_b, band_values, precision=PRECISE_DOT)
    blocks = total_rows // block_rows
    result = lax.map(jax.checkpoint(one_block), (queries.reshape(blocks, block_rows, H, HD), doc_ids.reshape(blocks, block_rows), token_index.reshape(blocks, block_rows)))
    return result.reshape(total_rows, H * HD)

def one_layer(x_in, bounds, gain_attn, gain_mlp, proj_qkv, proj_out, ffn_in, ffn_out, windowed):
    total_rows = x_in.shape[0]
    doc_ids, offsets = doc_info(bounds, jnp.arange(total_rows, dtype=jnp.int32))
    rope_base = 10000.0 if windowed else 160000.0
    normed = low(layer_norm(x_in, gain_attn))
    qkv = low_back(jnp.einsum('td,sdc->stc', normed, proj_qkv, precision=PRECISE_DOT))
    queries = low(rotate(qkv[0].reshape(total_rows, H, HD), offsets, rope_base))
    key_rows = low(rotate(qkv[1].reshape(total_rows, H, HD), offsets, rope_base))
    value_rows = low(qkv[2].reshape(total_rows, H, HD))
    context = low_back(low(attend(queries, key_rows, value_rows, doc_ids, windowed)))
    x_mid = x_in + low_back(jnp.einsum('tc,dc->td', context, proj_out, precision=PRECISE_DOT))
    hidden_in = low(layer_norm(x_mid, gain_mlp))
    gate_up = low_back(jnp.einsum('td,sdf->stf', hidden_in, ffn_in, precision=PRECISE_DOT))
    hidden = low(jax.nn.gelu(gate_up[0], approximate=False) * gate_up[1])
    return x_mid + low_back(jnp.einsum('tf,df->td', hidden, ffn_out, precision=PRECISE_DOT))

def reference(tokens, cu_seqlens, attn_gain, mlp_gain, w_qkv, w_attn_out, w_ffn_in, w_ffn_out, out_grad):
    params = tuple((item.astype(jnp.float32) for item in (attn_gain, mlp_gain, w_qkv, w_attn_out, w_ffn_in, w_ffn_out)))

    def forward(inputs, gains_attn, gains_mlp, proj_qkv, proj_out, ffn_in, ffn_out):
        outputs = []
        for micro_idx in range(MB):
            x_rows = inputs[micro_idx]
            for layer_idx in range(LAYERS):
                x_rows = one_layer(x_rows, cu_seqlens[micro_idx], gains_attn[layer_idx], gains_mlp[layer_idx], proj_qkv[layer_idx], proj_out[layer_idx], ffn_in[layer_idx], ffn_out[layer_idx], layer_idx % 2 == 0)
            outputs.append(x_rows)
        return jnp.stack(outputs)
    result, pullback = jax.vjp(forward, tokens.astype(jnp.float32), *params)
    grads = pullback(out_grad.astype(jnp.float32))
    return (result.astype(jnp.bfloat16), grads[0], grads[1], grads[2], grads[3], grads[4], grads[5], grads[6])
```

```python
import functools

import jax
import jax.numpy as jnp
from jax import lax
from jax.experimental import pallas as pl
from jax.experimental.pallas import tpu as pltpu
from jax.sharding import Mesh
from jax.sharding import PartitionSpec as P

HD = 64
HALF = 64
BLK = 128
TEAM = 4
MASKED = -1e30
BF = jnp.bfloat16
F32 = jnp.float32


def mm(a, b, ca, cb):
    return lax.dot_general(a, b, (((ca,), (cb,)), ((), ())), preferred_element_type=F32)


def hop_team(x, k):
    return lax.ppermute(x, ("y", "x"), [(i, i ^ k) for i in range(TEAM)])


def hop_core(x):
    return lax.ppermute(x, "c", [(0, 1), (1, 0)])


def hop_z(x, s):
    n = lax.axis_size("z")
    return lax.ppermute(x, "z", [(i, (i + s) % n) for i in range(n)])


def step_z(x, by):
    n = lax.axis_size("z")
    return lax.ppermute(x, "z", [(i, i + by) for i in range(n) if 0 <= i + by < n])


def gather_rows(own):
    parts = jnp.stack([own] + [hop_team(own, k) for k in range(1, TEAM)], axis=1)
    other = hop_core(parts)
    both = jnp.stack([parts, other], axis=2)
    n, rows, width = own.shape
    return both.reshape(n, TEAM * 2 * rows, width)


def sum_rows(partial):
    n, rows, width = partial.shape
    b = partial.reshape(n, TEAM, 2, rows // (2 * TEAM), width)
    h = b[:, :, 0].astype(F32) + hop_core(b[:, :, 1]).astype(F32)
    hb = h.astype(BF)
    total = h[:, 0]
    for k in range(1, TEAM):
        total = total + hop_team(hb[:, k], k).astype(F32)
    return total


def norm_parts(v):
    mean = jnp.mean(v, axis=-1, keepdims=True)
    cent = v - mean
    rstd = lax.rsqrt(jnp.mean(cent * cent, axis=-1, keepdims=True) + 1e-05)
    return cent * rstd, rstd


def norm_back(dout, v, gain):
    xhat, rstd = norm_parts(v)
    dgain = jnp.sum(dout * xhat, axis=(0, 1))
    dx = dout * gain
    m1 = jnp.mean(dx, axis=-1, keepdims=True)
    m2 = jnp.mean(dx * xhat, axis=-1, keepdims=True)
    return rstd * (dx - m1 - xhat * m2), dgain


def swap_halves(v):
    width = v.shape[-1]
    lane = lax.broadcasted_iota(jnp.int32, v.shape, v.ndim - 1) % HD
    up = jnp.roll(v, -(HD // 2), axis=-1)
    down = jnp.roll(v, HD // 2, axis=-1)
    del width
    return jnp.where(lane < HD // 2, up, down)


def band_from(m, qkv_ref, lo_ref, hi_ref, kb, vb, width, rows):
    kb[:BLK] = lo_ref[0, :, :width]
    vb[:BLK] = lo_ref[0, :, width:]
    kb[BLK + rows :] = hi_ref[0, :, :width]
    vb[BLK + rows :] = hi_ref[0, :, width:]
    sub = rows // 8
    for j in range(8):
        src = pl.ds(pl.multiple_of((m ^ j) * sub, sub), sub)
        kb[BLK + j * sub : BLK + (j + 1) * sub] = qkv_ref[0, src, width : 2 * width]
        vb[BLK + j * sub : BLK + (j + 1) * sub] = qkv_ref[0, src, 2 * width :]


def allowed_of(i, dcol_ref, drow_ref, windowed):
    qd = dcol_ref[0, BLK + i * BLK : 2 * BLK + i * BLK, :]
    kd = drow_ref[0, :, i * BLK : (i + 3) * BLK]
    ok = qd == kd
    if windowed:
        shape = (BLK, 3 * BLK)
        gap = lax.broadcasted_iota(jnp.int32, shape, 1) - lax.broadcasted_iota(jnp.int32, shape, 0) - BLK
        ok = ok & (gap <= HALF) & (gap >= -HALF)
    return ok


def take(ref, m, i, lanes, sub):
    per = BLK // sub
    return jnp.concatenate(
        [
            ref[0, pl.ds(pl.multiple_of((m ^ (per * i + e)) * sub, sub), sub), lanes]
            for e in range(per)
        ],
        axis=0,
    )


def put(ref, m, i, lanes, sub, value):
    per = BLK // sub
    for e in range(per):
        ref[0, pl.ds(pl.multiple_of((m ^ (per * i + e)) * sub, sub), sub), lanes] = value[
            e * sub : (e + 1) * sub
        ]


def attn_fwd_kernel(m_ref, qkv_ref, lo_ref, hi_ref, dcol_ref, drow_ref, ctx_ref, kb, vb, *, windowed):
    m = m_ref[0]
    rows = qkv_ref.shape[1]
    width = qkv_ref.shape[2] // 3
    sub = rows // 8
    band_from(m, qkv_ref, lo_ref, hi_ref, kb, vb, width, rows)
    head_of = lax.broadcasted_iota(jnp.int32, (BLK, width), 1) // HD
    for i in range(rows // BLK):
        ok = allowed_of(i, dcol_ref, drow_ref, windowed)
        q = take(qkv_ref, m, i, slice(0, width), sub)
        k = kb[i * BLK : (i + 3) * BLK]
        v = vb[i * BLK : (i + 3) * BLK]
        out = jnp.zeros((BLK, width), F32)
        for h in range(width // HD):
            qh = jnp.where(head_of == h, q, jnp.zeros_like(q))
            s = jnp.where(ok, 0.125 * mm(qh, k, 1, 1), MASKED)
            e = jnp.exp(s - jnp.max(s, axis=1, keepdims=True))
            p = (e / jnp.sum(e, axis=1, keepdims=True)).astype(BF)
            out = jnp.where(head_of == h, mm(p, v, 1, 0), out)
        put(ctx_ref, m, i, slice(0, width), sub, out.astype(BF))


def attn_bwd_kernel(
    m_ref, qkv_ref, lo_ref, hi_ref, dcol_ref, drow_ref, dctx_ref, dq_ref, dk_ref, dv_ref, kb, vb, *, windowed
):
    m = m_ref[0]
    rows = qkv_ref.shape[1]
    width = qkv_ref.shape[2] // 3
    sub = rows // 8
    band_from(m, qkv_ref, lo_ref, hi_ref, kb, vb, width, rows)
    head_of = lax.broadcasted_iota(jnp.int32, (BLK, width), 1) // HD
    dk_ref[...] = jnp.zeros(dk_ref.shape, F32)
    dv_ref[...] = jnp.zeros(dv_ref.shape, F32)
    for i in range(rows // BLK):
        ok = allowed_of(i, dcol_ref, drow_ref, windowed)
        q = take(qkv_ref, m, i, slice(0, width), sub)
        do = take(dctx_ref, m, i, slice(0, width), sub)
        band = slice(i * BLK, (i + 3) * BLK)
        k = kb[band]
        v = vb[band]
        dq = jnp.zeros((BLK, width), F32)
        dk = jnp.zeros((3 * BLK, width), F32)
        dv = jnp.zeros((3 * BLK, width), F32)
        for h in range(width // HD):
            mine = head_of == h
            qh = jnp.where(mine, q, jnp.zeros_like(q))
            doh = jnp.where(mine, do, jnp.zeros_like(do))
            s = jnp.where(ok, 0.125 * mm(qh, k, 1, 1), MASKED)
            e = jnp.exp(s - jnp.max(s, axis=1, keepdims=True))
            p = e / jnp.sum(e, axis=1, keepdims=True)
            dp = mm(doh, v, 1, 1)
            ds = (p * (dp - jnp.sum(p * dp, axis=1, keepdims=True))).astype(BF)
            dq = jnp.where(mine, mm(ds, k, 1, 0), dq)
            dk = dk + mm(ds, qh, 0, 0)
            dv = dv + mm(p.astype(BF), doh, 0, 0)
        put(dq_ref, m, i, slice(0, width), sub, 0.125 * dq)
        dk_ref[0, band] = dk_ref[0, band] + 0.125 * dk
        dv_ref[0, band] = dv_ref[0, band] + dv


def whole_block(shape):
    return pl.BlockSpec((1,) + shape[1:], lambda n, m: (n,) + (0,) * (len(shape) - 1))


def call_attention(kernel, m, ins, outs, windowed):
    n, rows, width = ins[0].shape[0], ins[0].shape[1], ins[0].shape[2] // 3
    pairs = n * rows * 3 * BLK * (width // HD)
    return pl.pallas_call(
        functools.partial(kernel, windowed=windowed),
        grid_spec=pltpu.PrefetchScalarGridSpec(
            num_scalar_prefetch=1,
            grid=(n,),
            in_specs=[whole_block(a.shape) for a in ins],
            out_specs=[whole_block(o.shape) for o in outs],
            scratch_shapes=[pltpu.VMEM((rows + 2 * BLK, width), BF)] * 2,
        ),
        out_shape=outs,
        compiler_params=pltpu.CompilerParams(vmem_limit_bytes=48 * 1024 * 1024),
        cost_estimate=pl.CostEstimate(
            flops=pairs * HD * 8, bytes_accessed=n * rows * width * 12, transcendentals=pairs
        ),
    )(m, *ins)


def pad_units(w, units):
    return jnp.pad(w, [(0, 0)] * (w.ndim - 1) + [(0, units - w.shape[-1])])


def spread(pack_of, t, z):
    own = pack_of(t)
    rows, width = own.shape
    nz = lax.axis_size("z")
    plane = jnp.zeros((TEAM * rows, width), own.dtype)
    for k in range(TEAM):
        part = own if k == 0 else hop_team(pack_of(t ^ k), k)
        plane = lax.dynamic_update_slice(plane, part, ((t ^ k) * rows, 0))
    full = jnp.zeros((nz * TEAM * rows, width), own.dtype)
    for s in range(nz):
        part = plane if s == 0 else hop_z(plane, s)
        full = lax.dynamic_update_slice(full, part, (((z - s) % nz) * TEAM * rows, 0))
    return full


def collect(grad, t, z, rows):
    nz = lax.axis_size("z")
    width = grad.shape[1]
    span = TEAM * rows
    low = grad.astype(BF)
    total = lax.dynamic_slice(low, (z * span, 0), (span, width)).astype(F32)
    for s in range(1, nz):
        piece = lax.dynamic_slice(low, (((z + s) % nz) * span, 0), (span, width))
        total = total + hop_z(piece, s).astype(F32)
    out = [lax.dynamic_slice(total, (t * rows, 0), (rows, width))]
    low = total.astype(BF)
    for k in range(1, TEAM):
        piece = lax.dynamic_slice(low, ((t ^ k) * rows, 0), (rows, width))
        out.append(hop_team(piece, k).astype(F32))
    return out


def columns(parts, t, lo, width):
    rows = parts[0].shape[0]
    full = jnp.zeros((rows, TEAM * width), F32)
    for k in range(TEAM):
        full = lax.dynamic_update_slice(full, parts[k][:, lo : lo + width], (0, (t ^ k) * width))
    return full


def gelu_parts(gate):
    cdf = 0.5 * (1.0 + lax.erf(gate * 0.7071067811865476))
    return gate * cdf, cdf + gate * jnp.exp(-0.5 * gate * gate) * 0.3989422804014327


def shards(tokens, cu_seqlens, attn_gain, mlp_gain, w_qkv, w_attn_out, w_ffn_in, w_ffn_out, out_grad):
    z = lax.axis_index("z")
    t = lax.axis_index("y") * 2 + lax.axis_index("x")
    c = lax.axis_index("c")
    m = 2 * t + c
    micro, chip_rows, feat = tokens.shape
    layers = w_qkv.shape[0]
    d_rows = w_qkv.shape[2]
    head_cols = w_qkv.shape[3] // TEAM
    own_rows = chip_rows // 2
    team_rows = TEAM * chip_rows
    unit_real = w_ffn_in.shape[3]
    units = -(-unit_real // (TEAM * 128)) * 128

    ffn_in_pad = pad_units(w_ffn_in, TEAM * units)
    ffn_out_pad = pad_units(w_ffn_out, TEAM * units)
    gains_cols = jnp.pad(
        jnp.concatenate([attn_gain, mlp_gain], axis=0).T, ((0, 0), (0, 128 - 2 * layers))
    )

    def attn_pack(layer):
        def of(member):
            q3 = lax.dynamic_slice_in_dim(w_qkv[layer], member * head_cols, head_cols, axis=2)
            o = lax.dynamic_slice_in_dim(w_attn_out[layer], member * head_cols, head_cols, axis=1)
            items = [q3[0], q3[1], q3[2], o]
            if layer == 0:
                items.append(gains_cols)
            return jnp.concatenate(items, axis=1)

        return of

    def ffn_pack(layer):
        def of(member):
            gu = lax.dynamic_slice_in_dim(ffn_in_pad[layer], member * units, units, axis=2)
            dn = lax.dynamic_slice_in_dim(ffn_out_pad[layer], member * units, units, axis=1)
            return jnp.concatenate([gu[0], gu[1], dn], axis=1)

        return of

    def own_half(x):
        return lax.dynamic_slice_in_dim(x, c * own_rows, own_rows, axis=1)

    tok_own = own_half(tokens)
    grad_own = own_half(out_grad)
    tok_all = gather_rows(tok_own)

    packs = []
    for layer in range(layers):
        packs.append([spread(attn_pack(layer), t, z), None])
        packs[layer][1] = spread(ffn_pack(layer), t, z)
    gains = packs[0][0][:, 4 * head_cols : 4 * head_cols + 2 * layers].T.astype(F32)
    grad_all = gather_rows(grad_own)

    band_index = z * team_rows - BLK + jnp.arange(team_rows + 2 * BLK, dtype=jnp.int32)
    inside = (band_index >= 0) & (band_index < cu_seqlens[0, -1])
    band_docs = jnp.sum(
        (band_index[None, :, None] >= cu_seqlens[:, None, 1:-1]).astype(jnp.int32), axis=2
    )
    band_docs = jnp.where(inside[None], band_docs, -1)
    docs_col = band_docs[:, :, None]
    docs_row = band_docs[:, None, :]
    blocks = jnp.arange(2 * TEAM, dtype=jnp.int32) ^ m
    local_index = (
        z * team_rows + blocks[:, None] * own_rows + jnp.arange(own_rows, dtype=jnp.int32)[None]
    ).reshape(-1)
    start = jnp.max(
        jnp.where(
            local_index[None, :, None] >= cu_seqlens[:, None, :-1], cu_seqlens[:, None, :-1], 0
        ),
        axis=2,
    )
    offsets = (local_index[None] - start).astype(F32)
    tables = []
    for layer in range(layers):
        base = 10000.0 if layer % 2 == 0 else 160000.0
        inv = base ** (-(jnp.arange(HD // 2, dtype=F32) * 2.0 / HD))
        ang = offsets[:, :, None] * inv
        cos, sin = jnp.cos(ang), jnp.sin(ang)
        heads = head_cols // HD
        tables.append(
            (
                jnp.concatenate([cos, cos] * heads, axis=-1),
                jnp.concatenate([-sin, sin] * heads, axis=-1),
            )
        )
    m_arr = jnp.reshape(m, (1,)).astype(jnp.int32)

    def flat(x):
        return x.reshape(-1, x.shape[-1])

    def edge(kv, first):
        b = kv.reshape(micro, 2 * TEAM, own_rows, kv.shape[-1])
        picks = [0, 1] if first else [2 * TEAM - 2, 2 * TEAM - 1]
        return jnp.concatenate(
            [lax.dynamic_index_in_dim(b, m ^ j, axis=1, keepdims=False) for j in picks], axis=1
        )

    x_own = tok_own.astype(F32)
    saved = []
    for layer in range(layers):
        windowed = layer % 2 == 0
        wa, wf = packs[layer]
        w3 = wa[:, : 3 * head_cols]
        wo = wa[:, 3 * head_cols : 4 * head_cols]
        g_attn, g_mlp = gains[layer], gains[layers + layer]
        if layer == 0:
            a = (norm_parts(tok_all.astype(F32))[0] * g_attn).astype(BF)
        else:
            a = gather_rows((norm_parts(x_own)[0] * g_attn).astype(BF))
        qkv = mm(flat(a), w3, 1, 0).reshape(micro, team_rows, -1)
        cos, sin = tables[layer]
        q, k, v = (qkv[:, :, i * head_cols : (i + 1) * head_cols] for i in range(3))
        kv_b = jnp.concatenate([k * cos + swap_halves(k) * sin, v], axis=-1).astype(BF)
        lo = step_z(edge(kv_b, False), 1)
        hi = step_z(edge(kv_b, True), -1)
        qkv_b = jnp.concatenate([(q * cos + swap_halves(q) * sin).astype(BF), kv_b], axis=-1)
        ctx = call_attention(
            attn_fwd_kernel,
            m_arr,
            [qkv_b, lo, hi, docs_col, docs_row],
            [jax.ShapeDtypeStruct((micro, team_rows, head_cols), BF)],
            windowed,
        )[0]
        part = mm(flat(ctx), wo, 1, 1).astype(BF).reshape(micro, team_rows, feat)
        mid_own = x_own + sum_rows(part)
        b = gather_rows((norm_parts(mid_own)[0] * g_mlp).astype(BF))
        gu = mm(flat(b), wf[:, : 2 * units], 1, 0)
        gate, up = gu[:, :units], gu[:, units:]
        hid = (gelu_parts(gate)[0] * up).astype(BF)
        part = mm(hid, wf[:, 2 * units :], 1, 1).astype(BF).reshape(micro, team_rows, feat)
        saved.append((x_own, a, qkv_b, lo, hi, ctx, mid_own, b, gate, up, hid))
        x_own = mid_own + sum_rows(part)

    def join_core(own):
        other = hop_core(own)
        first = jnp.where(c == 0, own, other)
        second = jnp.where(c == 0, other, own)
        return jnp.concatenate([first, second], axis=1)

    hidden_out = join_core(x_own.astype(BF))

    dy_own = grad_own.astype(F32)
    dyb = grad_all
    reduced = [None] * layers
    for layer in reversed(range(layers)):
        windowed = layer % 2 == 0
        wa, wf = packs[layer]
        w3 = wa[:, : 3 * head_cols]
        wo = wa[:, 3 * head_cols : 4 * head_cols]
        g_attn, g_mlp = gains[layer], gains[layers + layer]
        x_in, a, qkv_b, lo, hi, ctx, mid_own, b, gate, up, hid = saved[layer]
        dyb2 = flat(dyb)
        dhid = mm(dyb2, wf[:, 2 * units :], 1, 0)
        act, slope = gelu_parts(gate)
        dgu = jnp.concatenate([dhid * up * slope, dhid * act], axis=1).astype(BF)
        part = mm(dgu, wf[:, : 2 * units], 1, 1).astype(BF).reshape(micro, team_rows, feat)
        db = sum_rows(part)
        d_ffn = jnp.concatenate(
            [mm(flat(b), dgu, 0, 0).astype(BF), mm(dyb2, hid, 0, 0).astype(BF)], axis=1
        )
        ffn_parts = collect(d_ffn, t, z, d_rows)
        back, dg_mlp = norm_back(db, mid_own, g_mlp)
        dmid_own = dy_own + back
        dmb = gather_rows(dmid_own.astype(BF))
        dmb2 = flat(dmb)
        dctx = mm(dmb2, wo, 1, 0).astype(BF).reshape(micro, team_rows, head_cols)
        band = team_rows + 2 * BLK
        dq, dk, dv = call_attention(
            attn_bwd_kernel,
            m_arr,
            [qkv_b, lo, hi, docs_col, docs_row, dctx],
            [
                jax.ShapeDtypeStruct((micro, team_rows, head_cols), F32),
                jax.ShapeDtypeStruct((micro, band, head_cols), F32),
                jax.ShapeDtypeStruct((micro, band, head_cols), F32),
            ],
            windowed,
        )
        dkv = jnp.concatenate([dk, dv], axis=-1)
        from_next = step_z(dkv[:, BLK + team_rows :].astype(BF), 1).astype(F32)
        from_prev = step_z(dkv[:, :BLK].astype(BF), -1).astype(F32)
        dkv = dkv[:, BLK : BLK + team_rows]
        dkv = dkv.at[:, :BLK].add(from_next).at[:, team_rows - BLK :].add(from_prev)
        true_blocks = dkv.reshape(micro, 2 * TEAM, own_rows, 2 * head_cols)
        dkv = jnp.concatenate(
            [lax.dynamic_index_in_dim(true_blocks, m ^ j, 1, False) for j in range(2 * TEAM)], axis=1
        )
        cos, sin = tables[layer]
        dk, dv = dkv[:, :, :head_cols], dkv[:, :, head_cols:]
        dqkv = jnp.concatenate(
            [dq * cos + swap_halves(dq * sin), dk * cos + swap_halves(dk * sin), dv], axis=-1
        ).astype(BF)
        dqkv2 = flat(dqkv)
        part = mm(dqkv2, w3, 1, 1).astype(BF).reshape(micro, team_rows, feat)
        da = sum_rows(part)
        back, dg_attn = norm_back(da, x_in, g_attn)
        dy_own = dmid_own + back
        if layer > 0:
            dyb = gather_rows(dy_own.astype(BF))
        d_gain = jnp.pad(jnp.stack([dg_attn, dg_mlp], axis=1), ((0, 0), (0, 126))).astype(BF)
        d_attn = jnp.concatenate(
            [mm(flat(a), dqkv2, 0, 0).astype(BF), mm(dmb2, flat(ctx), 0, 0).astype(BF), d_gain],
            axis=1,
        )
        reduced[layer] = (collect(d_attn, t, z, d_rows), ffn_parts)

    input_grad = join_core(dy_own)

    g_attn_out, g_mlp_out, g_qkv, g_out, g_in, g_down = [], [], [], [], [], []
    for layer in range(layers):
        attn_parts, ffn_parts = reduced[layer]
        g_qkv.append(jnp.stack([columns(attn_parts, t, i * head_cols, head_cols) for i in range(3)]))
        g_out.append(columns(attn_parts, t, 3 * head_cols, head_cols))
        gain_sum = sum(p[:, 4 * head_cols : 4 * head_cols + 2] for p in attn_parts)
        gain_sum = gain_sum + hop_core(gain_sum)
        g_attn_out.append(gain_sum[:, 0])
        g_mlp_out.append(gain_sum[:, 1])
        g_in.append(jnp.stack([columns(ffn_parts, t, i * units, units)[:, :unit_real] for i in range(2)]))
        g_down.append(columns(ffn_parts, t, 2 * units, units)[:, :unit_real])
    return (
        hidden_out,
        input_grad,
        jnp.stack(g_attn_out),
        jnp.stack(g_mlp_out),
        jnp.stack(g_qkv),
        jnp.stack(g_out),
        jnp.stack(g_in),
        jnp.stack(g_down),
    )


def solution(mesh):
    dp, tensor = mesh.devices.shape
    fine = Mesh(mesh.devices.reshape(dp // TEAM, 2, 2, tensor), ("z", "y", "x", "c"))
    rows = ("z", "y", "x")
    in_specs = (
        P(None, rows, None),
        P(),
        P(None, rows),
        P(None, rows),
        P(None, None, rows, "c"),
        P(None, rows, "c"),
        P(None, None, rows, "c"),
        P(None, rows, "c"),
        P(None, rows, None),
    )
    out_specs = (
        P(None, rows, None),
        P(None, rows, None),
        P(None, rows),
        P(None, rows),
        P(None, None, rows, "c"),
        P(None, rows, "c"),
        P(None, None, rows, "c"),
        P(None, rows, "c"),
    )
    return jax.shard_map(shards, mesh=fine, in_specs=in_specs, out_specs=out_specs, check_vma=False)
```

```python
import jax
import jax.numpy as jnp
from jax import lax
from jax.experimental import pallas as pl
from jax.experimental.pallas import tpu as pltpu
from jax.sharding import Mesh
from jax.sharding import PartitionSpec as P

HD = 64
HALF = 64
BLK = 128
TEAM = 4
LOCAL = 2 * TEAM
MASKED = -1e30
BF = jnp.bfloat16
F32 = jnp.float32
CHAINS = 1


def mm(a, b, ca, cb):
    return lax.dot_general(a, b, (((ca,), (cb,)), ((), ())), preferred_element_type=F32)


def hop_team(x, k):
    return lax.ppermute(x, ("y", "x"), [(i, i ^ k) for i in range(TEAM)])


def hop_core(x):
    return lax.ppermute(x, "c", [(0, 1), (1, 0)])


def hop_z(x, s):
    n = lax.axis_size("z")
    return lax.ppermute(x, "z", [(i, (i + s) % n) for i in range(n)])


def step_z(x, by):
    n = lax.axis_size("z")
    return lax.ppermute(x, "z", [(i, i + by) for i in range(n) if 0 <= i + by < n])


def out(shape, dtype):
    return jax.ShapeDtypeStruct(shape, dtype)


def call(name, body, ids, ins, outs, scratch=(), flops=0):
    def kernel(*refs):
        n_in, n_out = len(ins), len(outs)
        body(refs[0], refs[1 : 1 + n_in], refs[1 + n_in : 1 + n_in + n_out], refs[1 + n_in + n_out :])

    moved = sum(a.size * a.dtype.itemsize for a in ins) + sum(
        o.size * jnp.dtype(o.dtype).itemsize for o in outs
    )
    vmem = pl.BlockSpec(memory_space=pltpu.VMEM)
    return pl.pallas_call(
        kernel,
        name=name,
        in_specs=[pl.BlockSpec(memory_space=pltpu.SMEM)] + [vmem] * len(ins),
        out_specs=[vmem] * len(outs),
        out_shape=list(outs),
        scratch_shapes=list(scratch),
        compiler_params=pltpu.CompilerParams(vmem_limit_bytes=24 * 1024 * 1024),
        cost_estimate=pl.CostEstimate(flops=flops, bytes_accessed=moved, transcendentals=0),
    )(ids, *ins)


def aligned(start, size):
    return pl.ds(pl.multiple_of(start, size), size)


def norm_parts(v):
    cent = v - jnp.mean(v, axis=-1, keepdims=True)
    rstd = lax.rsqrt(jnp.mean(cent * cent, axis=-1, keepdims=True) + 1e-05)
    return cent * rstd, rstd


def gelu_parts(gate):
    cdf = 0.5 * (1.0 + lax.erf(gate * 0.7071067811865476))
    return gate * cdf, cdf + gate * jnp.exp(-0.5 * gate * gate) * 0.3989422804014327


def swap_halves(v):
    width = v.shape[-1]
    lane = lax.broadcasted_iota(jnp.int32, v.shape, 1) % HD
    return jnp.where(
        lane < HD // 2, pltpu.roll(v, width - HD // 2, 1), pltpu.roll(v, HD // 2, 1)
    )


def true_rows(ids, n, sub, mb, b):
    blk = (ids[2] ^ (b % 2)) * TEAM + (ids[1] ^ (b // 2))
    return aligned((blk * n + mb) * sub, sub)


def tiles_of(refs, tile):
    rows = refs[0].shape[0]
    per = max(1, tile // rows)
    for first in range(0, len(refs), per):
        group = [r[...] for r in refs[first : first + per]]
        yield slice(first * rows, (first + per) * rows), (
            group[0] if per == 1 else jnp.concatenate(group, axis=0)
        )


def store_partial(p_refs, where, value):
    half = p_refs[0].shape[0]
    which = where.start // half
    p_refs[which][where.start - which * half : where.stop - which * half, :] = value.astype(BF)


def start_body(ids, ins, outs, scratch):
    tokens, grads, w_qkv, w_out, w_in, w_down = ins
    t, c = ids[1], ids[2]
    n, half = tokens.shape[0], tokens.shape[1] // 2
    for src, dst in ((tokens, outs[0]), (grads, outs[1])):
        for mb in range(n):
            dst[mb * half : (mb + 1) * half] = src[mb, aligned(c * half, half)]
    packs = outs[2:]
    layers, hc = w_qkv.shape[0], w_qkv.shape[3] // TEAM
    real, units = w_in.shape[3], scratch[0].shape[1] // TEAM
    scratch[0][...] = jnp.zeros(scratch[0].shape, BF)
    for layer in range(layers):
        for k in range(TEAM):
            dst = packs[layer * TEAM + k]
            cols = aligned((t ^ k) * hc, hc)
            for i in range(3):
                dst[:, i * hc : (i + 1) * hc] = w_qkv[layer, i, :, cols]
            dst[:, 3 * hc : 4 * hc] = w_out[layer, :, cols]
        for i in range(3):
            scratch[0][:, :real] = w_down[layer] if i == 2 else w_in[layer, i]
            for k in range(TEAM):
                cols = pl.ds(pl.multiple_of((t ^ k) * units, 128), units)
                packs[(layers + layer) * TEAM + k][:, i * units : (i + 1) * units] = scratch[0][:, cols]


def plane_body(ids, ins, outs, scratch):
    rows = ins[0].shape[0]
    for k in range(TEAM):
        outs[0][aligned((ids[1] ^ k) * rows, rows)] = ins[k][...]


def full_body(ids, ins, outs, scratch):
    rows, nz = ins[0].shape[0], len(ins)
    for s in range(nz):
        src = lax.rem(ids[0] - s + nz, nz)
        outs[0][aligned(src * rows, rows)] = ins[s][...]


def qkv_body(row, raw, n, sub):
    def body(ids, ins, outs, scratch):
        blocks, (gains, w, cos, sin) = ins[:LOCAL], ins[LOCAL:]
        a_ref, qkv_ref, lo_ref, hi_ref = outs
        hc = w.shape[1] // 4
        for where, tile in tiles_of(blocks, 256):
            if raw:
                tile = (norm_parts(tile.astype(F32))[0] * gains[row : row + 1]).astype(BF)
            a_ref[where] = tile
            r = mm(tile, w[:, : 3 * hc], 1, 0)
            cs, sn = cos[where], sin[where]
            q, k = r[:, :hc], r[:, hc : 2 * hc]
            qkv_ref[where, :hc] = (q * cs + swap_halves(q) * sn).astype(BF)
            qkv_ref[where, hc : 2 * hc] = (k * cs + swap_halves(k) * sn).astype(BF)
            qkv_ref[where, 2 * hc :] = r[:, 2 * hc :].astype(BF)
        per = BLK // sub
        for mb in range(n):
            for i in range(per):
                dst = slice(mb * BLK + i * sub, mb * BLK + (i + 1) * sub)
                lo_ref[dst] = qkv_ref[true_rows(ids, n, sub, mb, LOCAL - per + i), hc:]
                hi_ref[dst] = qkv_ref[true_rows(ids, n, sub, mb, i), hc:]

    return body


def fill_band(ids, mb, n, sub, qkv, lo, hi, kb, vb):
    hc = kb.shape[1]
    edge = slice(mb * BLK, (mb + 1) * BLK)
    last = BLK + LOCAL * sub
    kb[:BLK], vb[:BLK] = lo[edge, :hc], lo[edge, hc:]
    kb[last:], vb[last:] = hi[edge, :hc], hi[edge, hc:]
    for b in range(LOCAL):
        src = true_rows(ids, n, sub, mb, b)
        dst = slice(BLK + b * sub, BLK + (b + 1) * sub)
        kb[dst] = qkv[src, hc : 2 * hc]
        vb[dst] = qkv[src, 2 * hc :]


def allowed_of(mb, i, col, row, windowed):
    ok = col[mb, BLK + i * BLK : 2 * BLK + i * BLK, :] == row[mb, :, i * BLK : (i + 3) * BLK]
    if windowed:
        shape = (BLK, 3 * BLK)
        gap = lax.broadcasted_iota(jnp.int32, shape, 1) - lax.broadcasted_iota(jnp.int32, shape, 0)
        ok = ok & (gap <= BLK + HALF) & (gap >= BLK - HALF)
    return ok


def take(ids, ref, n, sub, mb, i, lanes):
    per = BLK // sub
    return jnp.concatenate(
        [ref[true_rows(ids, n, sub, mb, per * i + e), lanes] for e in range(per)], axis=0
    )


def put(ids, ref, n, sub, mb, i, lanes, value):
    for e in range(BLK // sub):
        per = BLK // sub
        ref[true_rows(ids, n, sub, mb, per * i + e), lanes] = value[e * sub : (e + 1) * sub]


def probs_of(qh, k, ok):
    s = jnp.where(ok, 0.125 * mm(qh, k, 1, 1), MASKED)
    e = jnp.exp(s - jnp.max(s, axis=1, keepdims=True))
    return e / jnp.sum(e, axis=1, keepdims=True)


def attn_body(windowed, n, sub):
    def body(ids, ins, outs, scratch):
        qkv, lo, hi, col, row, w = ins
        ctx_ref = outs[0]
        kb, vb = scratch
        hc = kb.shape[1]
        head_of = lax.broadcasted_iota(jnp.int32, (BLK, hc), 1) // HD
        for mb in range(n):
            fill_band(ids, mb, n, sub, qkv, lo, hi, kb, vb)
            for i in range(LOCAL * sub // BLK):
                ok = allowed_of(mb, i, col, row, windowed)
                q = take(ids, qkv, n, sub, mb, i, slice(0, hc))
                band = slice(i * BLK, (i + 3) * BLK)
                k, v = kb[band], vb[band]
                ctx = jnp.zeros((BLK, hc), F32)
                for h in range(hc // HD):
                    qh = jnp.where(head_of == h, q, jnp.zeros_like(q))
                    p = probs_of(qh, k, ok).astype(BF)
                    ctx = jnp.where(head_of == h, mm(p, v, 1, 0), ctx)
                put(ids, ctx_ref, n, sub, mb, i, slice(0, hc), ctx.astype(BF))
        total = ctx_ref.shape[0]
        for first in range(0, total, 256):
            where = slice(first, first + 256)
            store_partial(outs[1:], where, mm(ctx_ref[where], w[:, 3 * hc :], 1, 1))

    return body


def fold_body(ids, ins, outs, scratch):
    rows = outs[0].shape[0]
    for k in range(TEAM):
        where = slice(k * rows, (k + 1) * rows)
        both = ins[0][where].astype(F32) + ins[1][where].astype(F32)
        outs[k][...] = both.astype(outs[k].dtype)


def total_of(refs):
    value = refs[0][...].astype(F32)
    for r in refs[1:]:
        value = value + r[...].astype(F32)
    return value


def resid_body(row):
    def body(ids, ins, outs, scratch):
        x = ins[0][...].astype(F32) + total_of(ins[1 : 1 + TEAM])
        if row is None:
            outs[0][...] = x.astype(BF)
        else:
            outs[0][...] = x
            outs[1][...] = (norm_parts(x)[0] * ins[-1][row : row + 1]).astype(BF)

    return body


def mlp_body(ids, ins, outs, scratch):
    blocks, w = ins[:LOCAL], ins[LOCAL]
    b_ref, gu_ref, hid_ref = outs[:3]
    units = w.shape[1] // 3
    for where, tile in tiles_of(blocks, 256):
        b_ref[where] = tile
        gu = mm(tile, w[:, : 2 * units], 1, 0)
        gu_ref[where] = gu
        hid = (gelu_parts(gu[:, :units])[0] * gu[:, units:]).astype(BF)
        hid_ref[where] = hid
        store_partial(outs[3:], where, mm(hid, w[:, 2 * units :], 1, 1))


def mlp_back_body(ids, ins, outs, scratch):
    blocks, (gu_ref, w) = ins[:LOCAL], ins[LOCAL:]
    dy_ref, dgu_ref = outs[:2]
    units = w.shape[1] // 3
    for where, tile in tiles_of(blocks, 256):
        dy_ref[where] = tile
        dhid = mm(tile, w[:, 2 * units :], 1, 0)
        act, slope = gelu_parts(gu_ref[where, :units])
        dgu_ref[where, :units] = (dhid * gu_ref[where, units:] * slope).astype(BF)
        dgu_ref[where, units:] = (dhid * act).astype(BF)
        store_partial(outs[2:], where, mm(dgu_ref[where], w[:, : 2 * units], 1, 1))


def norm_back_body(row):
    def body(ids, ins, outs, scratch):
        dout = total_of(ins[:TEAM])
        v, dy, gains = ins[TEAM:]
        xhat, rstd = norm_parts(v[...].astype(F32))
        outs[0][...] = jnp.sum(dout * xhat, axis=0, keepdims=True)
        dx = dout * gains[row : row + 1]
        m1 = jnp.mean(dx, axis=-1, keepdims=True)
        m2 = jnp.mean(dx * xhat, axis=-1, keepdims=True)
        dv = dy[...].astype(F32) + rstd * (dx - m1 - xhat * m2)
        outs[1][...] = dv
        if len(outs) > 2:
            outs[2][...] = dv.astype(BF)

    return body


def attn_back_body(windowed, n, sub):
    def body(ids, ins, outs, scratch):
        blocks, (qkv, lo, hi, col, row, w, cos, sin) = ins[:LOCAL], ins[LOCAL:]
        dm_ref, dq_ref, dkv_ref, dlo_ref, dhi_ref = outs
        kb, vb, dctx, dqs, dkb, dvb = scratch
        hc = kb.shape[1]
        for where, tile in tiles_of(blocks, 256):
            dm_ref[where] = tile
            dctx[where] = mm(tile, w[:, 3 * hc :], 1, 0).astype(BF)
        head_of = lax.broadcasted_iota(jnp.int32, (BLK, hc), 1) // HD
        last = BLK + LOCAL * sub
        for mb in range(n):
            fill_band(ids, mb, n, sub, qkv, lo, hi, kb, vb)
            dkb[...] = jnp.zeros(dkb.shape, F32)
            dvb[...] = jnp.zeros(dvb.shape, F32)
            for i in range(LOCAL * sub // BLK):
                ok = allowed_of(mb, i, col, row, windowed)
                q = take(ids, qkv, n, sub, mb, i, slice(0, hc))
                do = take(ids, dctx, n, sub, mb, i, slice(0, hc))
                band = slice(i * BLK, (i + 3) * BLK)
                k, v = kb[band], vb[band]
                dq = jnp.zeros((BLK, hc), F32)
                dk = dkb[band]
                dv = dvb[band]
                for h in range(hc // HD):
                    mine = head_of == h
                    qh = jnp.where(mine, q, jnp.zeros_like(q))
                    doh = jnp.where(mine, do, jnp.zeros_like(do))
                    p = probs_of(qh, k, ok)
                    dp = mm(doh, v, 1, 1)
                    ds = (p * (dp - jnp.sum(p * dp, axis=1, keepdims=True))).astype(BF)
                    dq = jnp.where(mine, mm(ds, k, 1, 0), dq)
                    dk = dk + mm(ds, qh, 0, 0)
                    dv = dv + mm(p.astype(BF), doh, 0, 0)
                put(ids, dqs, n, sub, mb, i, slice(0, hc), 0.125 * dq)
                dkb[band] = dk
                dvb[band] = dv
            edge = slice(mb * BLK, (mb + 1) * BLK)
            dlo_ref[edge, :hc] = (0.125 * dkb[:BLK]).astype(BF)
            dlo_ref[edge, hc:] = dvb[:BLK].astype(BF)
            dhi_ref[edge, :hc] = (0.125 * dkb[last:]).astype(BF)
            dhi_ref[edge, hc:] = dvb[last:].astype(BF)
            for b in range(LOCAL):
                src = slice(BLK + b * sub, BLK + (b + 1) * sub)
                dst = true_rows(ids, n, sub, mb, b)
                dkv_ref[dst, :hc] = 0.125 * dkb[src]
                dkv_ref[dst, hc:] = dvb[src]
        for first in range(0, dqs.shape[0], 256):
            where = slice(first, first + 256)
            g = dqs[where]
            dq_ref[where] = (g * cos[where] + swap_halves(g * sin[where])).astype(BF)

    return body


def qkv_back_body(n, sub):
    def body(ids, ins, outs, scratch):
        dq, dkv, from_next, from_prev, w, cos, sin = ins
        dqkv_ref = outs[0]
        acc = scratch[0]
        hc = w.shape[1] // 4
        acc[...] = dkv[...]
        per = BLK // sub
        for mb in range(n):
            for i in range(per):
                src = slice(mb * BLK + i * sub, mb * BLK + (i + 1) * sub)
                first = true_rows(ids, n, sub, mb, i)
                acc[first] = acc[first] + from_prev[src].astype(F32)
                end = true_rows(ids, n, sub, mb, LOCAL - per + i)
                acc[end] = acc[end] + from_next[src].astype(F32)
        for first in range(0, acc.shape[0], 256):
            where = slice(first, first + 256)
            g = acc[where, :hc]
            dqkv_ref[where, :hc] = dq[where]
            dqkv_ref[where, hc : 2 * hc] = (g * cos[where] + swap_halves(g * sin[where])).astype(BF)
            dqkv_ref[where, 2 * hc :] = acc[where, hc:].astype(BF)
            store_partial(outs[1:], where, mm(dqkv_ref[where], w[:, : 3 * hc], 1, 1))

    return body


def weight_grad_body(ids, ins, outs, scratch):
    full = scratch[0]
    chains = [ins[i : i + 4] for i in range(0, len(ins), 4)]
    cut = chains[0][1].shape[1]
    step = 256
    for first in range(0, full.shape[0], step):
        where = slice(first, first + step)
        full[where, :cut] = sum(mm(c[0][:, where], c[1][...], 0, 0) for c in chains).astype(BF)
        full[where, cut:] = sum(mm(c[2][:, where], c[3][...], 0, 0) for c in chains).astype(BF)
    nz = len(outs)
    span = outs[0].shape[0]
    for s in range(nz):
        outs[s][...] = full[aligned(lax.rem(ids[0] + s, nz) * span, span)]


def plane_sum_body(ids, ins, outs, scratch):
    scratch[0][...] = total_of(ins)
    rows = outs[0].shape[0]
    for k in range(TEAM):
        outs[k][...] = scratch[0][aligned((ids[1] ^ k) * rows, rows)].astype(outs[k].dtype)


def finish_body(ids, ins, outs, scratch):
    g_qkv, g_out, g_in, g_down = outs
    wide = scratch[0]
    layers, hc = g_qkv.shape[0], g_qkv.shape[3] // TEAM
    real, units = g_down.shape[2], wide.shape[1] // TEAM
    for layer in range(layers):
        attn = ins[layer * TEAM : (layer + 1) * TEAM]
        ffn = ins[(layers + layer) * TEAM : (layers + layer + 1) * TEAM]
        for k in range(TEAM):
            cols = aligned((ids[1] ^ k) * hc, hc)
            for i in range(3):
                g_qkv[layer, i, :, cols] = attn[k][:, i * hc : (i + 1) * hc].astype(F32)
            g_out[layer, :, cols] = attn[k][:, 3 * hc :].astype(F32)
        for i in range(3):
            for k in range(TEAM):
                cols = pl.ds(pl.multiple_of((ids[1] ^ k) * units, 128), units)
                wide[:, cols] = ffn[k][:, i * units : (i + 1) * units].astype(F32)
            if i == 2:
                g_down[layer] = wide[:, :real]
            else:
                g_in[layer, i] = wide[:, :real]


def join_body(ids, ins, outs, scratch):
    n, half = outs[0].shape[0], outs[0].shape[1] // 2
    c = ids[2]
    for mb in range(n):
        rows = slice(mb * half, (mb + 1) * half)
        outs[0][mb, aligned(c * half, half)] = ins[0][rows]
        outs[0][mb, aligned((1 - c) * half, half)] = ins[1][rows]


def shards(tokens, cu_seqlens, attn_gain, mlp_gain, w_qkv, w_attn_out, w_ffn_in, w_ffn_out, out_grad):
    nz = lax.axis_size("z")
    z = lax.axis_index("z")
    t = lax.axis_index("y") * 2 + lax.axis_index("x")
    c = lax.axis_index("c")
    ids = jnp.stack([z, t, c]).astype(jnp.int32)
    micro, chip_rows, feat = tokens.shape
    layers, d_rows = w_qkv.shape[0], w_qkv.shape[2]
    hc = w_qkv.shape[3] // TEAM
    sub = chip_rows // 2
    real = w_ffn_in.shape[3]
    units = -(-real // (TEAM * 128)) * 128
    team_rows = TEAM * chip_rows
    per_chain = micro // CHAINS
    n = per_chain
    own = n * sub
    rows = LOCAL * own
    aw, fw = 4 * hc, 3 * units

    started = call(
        "start", start_body, ids,
        [tokens, out_grad, w_qkv, w_attn_out, w_ffn_in, w_ffn_out],
        [out((micro * sub, feat), BF)] * 2
        + [out((d_rows, aw), BF)] * (layers * TEAM)
        + [out((d_rows, fw), BF)] * (layers * TEAM),
        [pltpu.VMEM((d_rows, TEAM * units), BF)],
    )
    tok_own, grad_own = started[:2]
    packs = started[2:]

    def blocks_of(x):
        mine = [x] + [hop_team(x, k) for k in range(1, TEAM)]
        return mine + [hop_core(b) for b in mine]

    def chain_rows(x, i):
        return x[i * own : (i + 1) * own]

    tok_blocks = [blocks_of(chain_rows(tok_own, i)) for i in range(CHAINS)]

    def assemble(pieces, name):
        width = pieces[0].shape[1]
        got = [pieces[0]] + [hop_team(pieces[k], k) for k in range(1, TEAM)]
        plane = call("plane_" + name, plane_body, ids, got, [out((TEAM * d_rows, width), BF)])[0]
        planes = [plane] + [hop_z(plane, s) for s in range(1, nz)]
        return call("full_" + name, full_body, ids, planes, [out((nz * TEAM * d_rows, width), BF)])[0]

    owned = jnp.concatenate([attn_gain, mlp_gain, attn_gain, mlp_gain], axis=0).astype(F32)[: 4 * layers]
    spot = lax.broadcasted_iota(jnp.int32, (1, feat), 1) // d_rows == z * TEAM + t
    gains = jnp.where(spot, jnp.tile(owned, (1, feat // d_rows)), 0.0)
    gains = gains + hop_team(gains, 1)
    gains = gains + hop_team(gains, 2)
    gains = sum([gains] + [hop_z(gains, s) for s in range(1, nz)])

    attn_w, ffn_w = [None] * layers, [None] * layers
    for layer in range(layers):
        attn_w[layer] = assemble(packs[layer * TEAM : (layer + 1) * TEAM], "a" + str(layer))
        ffn_w[layer] = assemble(
            packs[(layers + layer) * TEAM : (layers + layer + 1) * TEAM], "f" + str(layer)
        )
    grad_blocks = [blocks_of(chain_rows(grad_own, i)) for i in range(CHAINS)]

    band_index = z * team_rows - BLK + jnp.arange(team_rows + 2 * BLK, dtype=jnp.int32)
    inside = (band_index >= 0) & (band_index < cu_seqlens[0, -1])
    docs = jnp.sum((band_index[None, :, None] >= cu_seqlens[:, None, 1:-1]).astype(jnp.int32), axis=2)
    docs = jnp.where(inside[None], docs, -1)
    block = jnp.arange(LOCAL, dtype=jnp.int32)
    true_block = ((block % TEAM) ^ t) * 2 + ((block // TEAM) ^ c)
    index = z * team_rows + true_block[:, None] * sub + jnp.arange(sub, dtype=jnp.int32)[None]
    begin = jnp.max(
        jnp.where(
            index[:, None, :, None] >= cu_seqlens[None, :, None, :-1], cu_seqlens[None, :, None, :-1], 0
        ),
        axis=3,
    )
    offsets = (index[:, None] - begin).astype(F32)
    lane = jnp.arange(hc, dtype=jnp.int32) % HD
    sign = jnp.where(lane < HD // 2, -1.0, 1.0)

    state = []
    for i in range(CHAINS):
        mbs = slice(i * n, (i + 1) * n)
        tables = []
        for layer in range(layers):
            base = 10000.0 if layer % 2 == 0 else 160000.0
            inv = base ** (-((lane % (HD // 2)).astype(F32) * 2.0 / HD))
            ang = offsets[:, mbs].reshape(rows, 1) * inv
            tables.append((jnp.cos(ang), jnp.sin(ang) * sign))
        state.append(
            {
                "tables": tables,
                "col": docs[mbs, :, None],
                "row": docs[mbs, None, :],
                "x": chain_rows(tok_own, i),
                "blocks": tok_blocks[i],
                "saved": [],
            }
        )

    partial_out = [out((rows // 2, feat), BF)] * 2
    band = pltpu.VMEM((team_rows + 2 * BLK, hc), BF)
    band32 = pltpu.VMEM((team_rows + 2 * BLK, hc), F32)

    def fold(parts, name):
        got = hop_core(parts[1])
        h = call(
            "fold_" + name, fold_body, ids, [parts[0], got],
            [out((own, feat), F32)] + [out((own, feat), BF)] * (TEAM - 1),
        )
        return [h[0]] + [hop_team(h[k], k) for k in range(1, TEAM)]

    def forward_attn(st, layer):
        windowed = layer % 2 == 0
        w = attn_w[layer]
        cos, sin = st["tables"][layer]
        a, qkv, lo, hi = call(
            "qkv", qkv_body(layer, layer == 0, n, sub), ids, st["blocks"] + [gains, w, cos, sin],
            [out((rows, feat), BF), out((rows, 3 * hc), BF)] + [out((n * BLK, 2 * hc), BF)] * 2,
            flops=2 * rows * feat * 3 * hc,
        )
        lo, hi = step_z(lo, 1), step_z(hi, -1)
        ctx, *parts = call(
            "attn", attn_body(windowed, n, sub), ids, [qkv, lo, hi, st["col"], st["row"], w],
            [out((rows, hc), BF)] + partial_out, [band] * 2, flops=4 * rows * feat * hc,
        )
        terms = fold(parts, "attn")
        mid, b = call(
            "mid", resid_body(layers + layer), ids, [st["x"]] + terms + [gains],
            [out((own, feat), F32), out((own, feat), BF)],
        )
        st["saved"].append([st["x"], a, qkv, lo, hi, ctx, mid])
        st["x"] = mid
        st["blocks"] = blocks_of(b)

    def forward_mlp(st, layer):
        b, gu, hid, *parts = call(
            "mlp", mlp_body, ids, st["blocks"] + [ffn_w[layer]],
            [out((rows, feat), BF), out((rows, 2 * units), F32), out((rows, units), BF)] + partial_out,
            flops=6 * rows * feat * units,
        )
        st["saved"][layer] += [b, gu, hid]
        terms = fold(parts, "mlp")
        if layer + 1 < layers:
            st["x"], a = call(
                "next", resid_body(layer + 1), ids, [st["x"]] + terms + [gains],
                [out((own, feat), F32), out((own, feat), BF)],
            )
            st["blocks"] = blocks_of(a)
        else:
            st["x"] = call("last", resid_body(None), ids, [st["x"]] + terms, [out((own, feat), BF)])[0]

    for layer in range(layers):
        for st in state:
            forward_attn(st, layer)
        for st in state:
            forward_mlp(st, layer)

    def join(parts, dtype):
        x = parts[0] if CHAINS == 1 else jnp.concatenate(parts, axis=0)
        return call("join", join_body, ids, [x, hop_core(x)], [out((micro, chip_rows, feat), dtype)])[0]

    hidden_out = join([st["x"] for st in state], BF)

    for i, st in enumerate(state):
        st["dy"] = chain_rows(grad_own, i)
        st["blocks"] = grad_blocks[i]

    def collect(ins, width, name):
        flops = 2 * rows * CHAINS * feat * width
        pieces = call(
            "wgrad_" + name, weight_grad_body, ids, ins, [out((TEAM * d_rows, width), BF)] * nz,
            [pltpu.VMEM((nz * TEAM * d_rows, width), BF)], flops=flops,
        )
        got = [pieces[0]] + [hop_z(pieces[s], s) for s in range(1, nz)]
        mine = call(
            "zsum_" + name, plane_sum_body, ids, got,
            [out((d_rows, width), F32)] + [out((d_rows, width), BF)] * (TEAM - 1),
            [pltpu.VMEM((TEAM * d_rows, width), F32)],
        )
        return [mine[0]] + [hop_team(mine[k], k) for k in range(1, TEAM)]

    gain_rows = [None] * (2 * layers)

    def backward_mlp(st, layer):
        b, gu, hid = st["saved"][layer][7:]
        dy, dgu, *parts = call(
            "mlp_back", mlp_back_body, ids, st["blocks"] + [gu, ffn_w[layer]],
            [out((rows, feat), BF), out((rows, 2 * units), BF)] + partial_out,
            flops=6 * rows * feat * units,
        )
        terms = fold(parts, "mlp_back")
        dg, dmid, dmb = call(
            "mid_back", norm_back_body(layers + layer), ids, terms + [st["saved"][layer][6], st["dy"], gains],
            [out((1, feat), F32), out((own, feat), F32), out((own, feat), BF)],
        )
        old = gain_rows[layers + layer]
        gain_rows[layers + layer] = dg if old is None else old + dg
        st["dy"] = dmid
        st["blocks"] = blocks_of(dmb)
        return [b, dgu, dy, hid]

    def backward_attn(st, layer):
        windowed = layer % 2 == 0
        w = attn_w[layer]
        cos, sin = st["tables"][layer]
        x_in, a, qkv, lo, hi, ctx = st["saved"][layer][:6]
        dm, dq, dkv, dlo, dhi = call(
            "attn_back", attn_back_body(windowed, n, sub), ids,
            st["blocks"] + [qkv, lo, hi, st["col"], st["row"], w, cos, sin],
            [out((rows, feat), BF), out((rows, hc), BF), out((rows, 2 * hc), F32)]
            + [out((n * BLK, 2 * hc), BF)] * 2,
            [band] * 2 + [pltpu.VMEM((rows, hc), BF), pltpu.VMEM((rows, hc), F32)] + [band32] * 2,
            flops=6 * rows * feat * hc,
        )
        from_next, from_prev = step_z(dlo, -1), step_z(dhi, 1)
        dqkv, *parts = call(
            "qkv_back", qkv_back_body(n, sub), ids, [dq, dkv, from_next, from_prev, w, cos, sin],
            [out((rows, 3 * hc), BF)] + partial_out, [pltpu.VMEM((rows, 2 * hc), F32)],
            flops=6 * rows * feat * hc,
        )
        terms = fold(parts, "qkv_back")
        low = [out((own, feat), BF)] if layer > 0 else []
        dg, st["dy"], *dyb = call(
            "in_back", norm_back_body(layer), ids, terms + [x_in, st["dy"], gains],
            [out((1, feat), F32), out((own, feat), F32)] + low,
        )
        old = gain_rows[layer]
        gain_rows[layer] = dg if old is None else old + dg
        if layer > 0:
            st["blocks"] = blocks_of(dyb[0])
        return [a, dqkv, dm, ctx]

    attn_parts, ffn_parts = [None] * layers, [None] * layers
    for layer in reversed(range(layers)):
        ins = sum([backward_mlp(st, layer) for st in state], [])
        ffn_parts[layer] = collect(ins, fw, "f" + str(layer))
        ins = sum([backward_attn(st, layer) for st in state], [])
        attn_parts[layer] = collect(ins, aw, "a" + str(layer))

    input_grad = join([st["dy"] for st in state], F32)

    dgain = jnp.concatenate(gain_rows + gain_rows, axis=0)[: 4 * layers]
    dgain = dgain + hop_core(dgain)
    dgain = dgain + hop_team(dgain, 1)
    dgain = dgain + hop_team(dgain, 2)
    dgain = sum([dgain] + [hop_z(dgain, s) for s in range(1, nz)])
    dgain = lax.dynamic_slice_in_dim(dgain, (z * TEAM + t) * d_rows, d_rows, axis=1)

    g_qkv, g_out, g_in, g_down = call(
        "finish", finish_body, ids, sum(attn_parts, []) + sum(ffn_parts, []),
        [out(w_qkv.shape, F32), out(w_attn_out.shape, F32), out(w_ffn_in.shape, F32), out(w_ffn_out.shape, F32)],
        [pltpu.VMEM((d_rows, TEAM * units), F32)],
    )
    return (
        hidden_out,
        input_grad,
        dgain[:layers],
        dgain[layers : 2 * layers],
        g_qkv,
        g_out,
        g_in,
        g_down,
    )


def solution(mesh):
    dp, tensor = mesh.devices.shape
    fine = Mesh(mesh.devices.reshape(dp // TEAM, 2, 2, tensor), ("z", "y", "x", "c"))
    rows = ("z", "y", "x")
    in_specs = (
        P(None, rows, None),
        P(),
        P(None, rows),
        P(None, rows),
        P(None, None, rows, "c"),
        P(None, rows, "c"),
        P(None, None, rows, "c"),
        P(None, rows, "c"),
        P(None, rows, None),
    )
    out_specs = (
        P(None, rows, None),
        P(None, rows, None),
        P(None, rows),
        P(None, rows),
        P(None, None, rows, "c"),
        P(None, rows, "c"),
        P(None, None, rows, "c"),
        P(None, rows, "c"),
    )
    return jax.shard_map(shards, mesh=fine, in_specs=in_specs, out_specs=out_specs, check_vma=False)
```

```python
import jax
import jax.numpy as jnp
from jax import lax
from jax.experimental import pallas as pl
from jax.experimental.pallas import tpu as pltpu
from jax.sharding import Mesh
from jax.sharding import PartitionSpec as P

HD = 64
HALF = 64
BLK = 128
TEAM = 4
LOCAL = 2 * TEAM
MASKED = -1e30
BF = jnp.bfloat16
F32 = jnp.float32
CHAINS = 1


def mm(a, b, ca, cb):
    return lax.dot_general(a, b, (((ca,), (cb,)), ((), ())), preferred_element_type=F32)


def hop_team(x, k):
    return lax.ppermute(x, ("y", "x"), [(i, i ^ k) for i in range(TEAM)])


def hop_core(x):
    return lax.ppermute(x, "c", [(0, 1), (1, 0)])


def hop_z(x, s):
    n = lax.axis_size("z")
    return lax.ppermute(x, "z", [(i, i ^ s if n == 4 else (i + s) % n) for i in range(n)])


def step_z(x, by):
    n = lax.axis_size("z")
    return lax.ppermute(x, "z", [(i, i + by) for i in range(n) if 0 <= i + by < n])


def out(shape, dtype):
    return jax.ShapeDtypeStruct(shape, dtype)


def call(name, body, ids, ins, outs, scratch=(), flops=0, after=()):
    ins, after = list(ins), list(after)

    def kernel(*refs):
        n_in, n_out = len(ins), len(outs)
        rest = refs[1 + n_in + len(after) :]
        body(refs[0], refs[1 : 1 + n_in], rest[:n_out], rest[n_out:])

    moved = sum(a.size * a.dtype.itemsize for a in ins) + sum(
        o.size * jnp.dtype(o.dtype).itemsize for o in outs
    )
    vmem = pl.BlockSpec(memory_space=pltpu.VMEM)
    results = pl.pallas_call(
        kernel,
        name=name,
        in_specs=[pl.BlockSpec(memory_space=pltpu.SMEM)] + [vmem] * len(ins)
        + [pl.BlockSpec(memory_space=pl.ANY)] * len(after),
        out_specs=[vmem] * len(outs),
        out_shape=list(outs),
        scratch_shapes=list(scratch),
        compiler_params=pltpu.CompilerParams(vmem_limit_bytes=24 * 1024 * 1024),
        cost_estimate=pl.CostEstimate(flops=flops, bytes_accessed=moved, transcendentals=0),
    )(ids, *ins, *after)
    return list(results)


def aligned(start, size):
    return pl.ds(pl.multiple_of(start, size), size)


def norm_parts(v):
    cent = v - jnp.mean(v, axis=-1, keepdims=True)
    rstd = lax.rsqrt(jnp.mean(cent * cent, axis=-1, keepdims=True) + 1e-05)
    return cent * rstd, rstd


def gelu_parts(gate):
    cdf = 0.5 * (1.0 + lax.erf(gate * 0.7071067811865476))
    return gate * cdf, cdf + gate * jnp.exp(-0.5 * gate * gate) * 0.3989422804014327


def swap_halves(v):
    width = v.shape[-1]
    lane = lax.broadcasted_iota(jnp.int32, v.shape, 1) % HD
    return jnp.where(
        lane < HD // 2, pltpu.roll(v, width - HD // 2, 1), pltpu.roll(v, HD // 2, 1)
    )


def true_rows(ids, n, sub, mb, b):
    blk = (ids[2] ^ (b % 2)) * TEAM + (ids[1] ^ (b // 2))
    return aligned((blk * n + mb) * sub, sub)


def tiles_of(refs, tile):
    rows = refs[0].shape[0]
    per = max(1, tile // rows)
    for first in range(0, len(refs), per):
        group = [r[...] for r in refs[first : first + per]]
        yield slice(first * rows, (first + per) * rows), (
            group[0] if per == 1 else jnp.concatenate(group, axis=0)
        )


def store_partial(p_refs, where, value):
    half = p_refs[0].shape[0]
    which = where.start // half
    p_refs[which][where.start - which * half : where.stop - which * half, :] = value.astype(BF)


def lane_picks(count):
    shape = (count, 128)
    row, lane = (lax.broadcasted_iota(jnp.int32, shape, d) for d in (0, 1))
    return jnp.where(row == lane, 1.0, 0.0).astype(BF)


def start_body(ids, ins, outs, scratch):
    tokens, grads, gains, w_qkv, w_out, w_in, w_down = ins
    t, c = ids[1], ids[2]
    n, half = tokens.shape[0], tokens.shape[1] // 2
    for src, dst in ((tokens, outs[0]), (grads, outs[1])):
        for mb in range(n):
            dst[mb * half : (mb + 1) * half] = src[mb, aligned(c * half, half)]
    packs = outs[2:]
    layers, hc = w_qkv.shape[0], w_qkv.shape[3] // TEAM
    real, units = w_in.shape[3], scratch[0].shape[1] // TEAM
    scratch[0][...] = jnp.zeros(scratch[0].shape, BF)
    for layer in range(layers):
        for k in range(TEAM):
            dst = packs[layer * TEAM + k]
            cols = aligned((t ^ k) * hc, hc)
            for i in range(3):
                dst[:, i * hc : (i + 1) * hc] = w_qkv[layer, i, :, cols]
            dst[:, 3 * hc : 4 * hc] = w_out[layer, :, cols]
            if layer == 0:
                dst[:, 4 * hc :] = mm(gains[...], lane_picks(gains.shape[0]), 0, 0).astype(BF)
        for i in range(3):
            scratch[0][:, :real] = w_down[layer] if i == 2 else w_in[layer, i]
            for k in range(TEAM):
                cols = pl.ds(pl.multiple_of((t ^ k) * units, 128), units)
                packs[(layers + layer) * TEAM + k][:, i * units : (i + 1) * units] = scratch[0][:, cols]


def plane_body(ids, ins, outs, scratch):
    rows = ins[0].shape[0]
    for k in range(TEAM):
        outs[0][aligned((ids[1] ^ k) * rows, rows)] = ins[k][...]


def full_body(ids, ins, outs, scratch):
    rows, nz = ins[0].shape[0], len(ins)
    for s in range(nz):
        src = ids[0] ^ s if nz == 4 else lax.rem(ids[0] - s + nz, nz)
        outs[0][aligned(src * rows, rows)] = ins[s][...]


def full_gains_body(ids, ins, outs, scratch):
    rows, nz = ins[0].shape[0], len(ins)
    width = outs[0].shape[1]
    for s in range(nz):
        src = ids[0] ^ s if nz == 4 else lax.rem(ids[0] - s + nz, nz)
        outs[0][aligned(src * rows, rows)] = ins[s][:, :width]
        scratch[0][aligned(src * rows, rows)] = ins[s][:, width:]
    outs[1][...] = mm(lane_picks(outs[1].shape[0]), scratch[0][...], 1, 1)


def add_body(ids, ins, outs, scratch):
    outs[0][...] = total_of(ins).astype(BF)


def qkv_body(row, raw, n, sub):
    def body(ids, ins, outs, scratch):
        blocks, (gains, w, cos, sin) = ins[:LOCAL], ins[LOCAL:]
        a_ref, qkv_ref, lo_ref, hi_ref = outs
        hc = w.shape[1] // 4
        for where, tile in tiles_of(blocks, 256):
            if raw:
                tile = (norm_parts(tile.astype(F32))[0] * gains[row : row + 1]).astype(BF)
            a_ref[where] = tile
            r = mm(tile, w[:, : 3 * hc], 1, 0)
            cs, sn = cos[where], sin[where]
            q, k = r[:, :hc], r[:, hc : 2 * hc]
            qkv_ref[where, :hc] = (q * cs + swap_halves(q) * sn).astype(BF)
            qkv_ref[where, hc : 2 * hc] = (k * cs + swap_halves(k) * sn).astype(BF)
            qkv_ref[where, 2 * hc :] = r[:, 2 * hc :].astype(BF)
        per = BLK // sub
        for mb in range(n):
            for i in range(per):
                dst = slice(mb * BLK + i * sub, mb * BLK + (i + 1) * sub)
                lo_ref[dst] = qkv_ref[true_rows(ids, n, sub, mb, LOCAL - per + i), hc:]
                hi_ref[dst] = qkv_ref[true_rows(ids, n, sub, mb, i), hc:]

    return body


def fill_band(ids, mb, n, sub, qkv, lo, hi, kb, vb):
    hc = kb.shape[1]
    edge = slice(mb * BLK, (mb + 1) * BLK)
    last = BLK + LOCAL * sub
    kb[:BLK], vb[:BLK] = lo[edge, :hc], lo[edge, hc:]
    kb[last:], vb[last:] = hi[edge, :hc], hi[edge, hc:]
    for b in range(LOCAL):
        src = true_rows(ids, n, sub, mb, b)
        dst = slice(BLK + b * sub, BLK + (b + 1) * sub)
        kb[dst] = qkv[src, hc : 2 * hc]
        vb[dst] = qkv[src, 2 * hc :]


def allowed_of(mb, i, col, row, windowed):
    ok = col[mb, BLK + i * BLK : 2 * BLK + i * BLK, :] == row[mb, :, i * BLK : (i + 3) * BLK]
    if windowed:
        shape = (BLK, 3 * BLK)
        gap = lax.broadcasted_iota(jnp.int32, shape, 1) - lax.broadcasted_iota(jnp.int32, shape, 0)
        ok = ok & (gap <= BLK + HALF) & (gap >= BLK - HALF)
    return ok


def take(ids, ref, n, sub, mb, i, lanes):
    per = BLK // sub
    return jnp.concatenate(
        [ref[true_rows(ids, n, sub, mb, per * i + e), lanes] for e in range(per)], axis=0
    )


def put(ids, ref, n, sub, mb, i, lanes, value):
    for e in range(BLK // sub):
        per = BLK // sub
        ref[true_rows(ids, n, sub, mb, per * i + e), lanes] = value[e * sub : (e + 1) * sub]


def probs_of(qh, k, ok):
    s = jnp.where(ok, 0.125 * mm(qh, k, 1, 1), MASKED)
    e = jnp.exp(s - jnp.max(s, axis=1, keepdims=True))
    return e / jnp.sum(e, axis=1, keepdims=True)


def attn_body(windowed, n, sub):
    def body(ids, ins, outs, scratch):
        qkv, lo, hi, col, row, w = ins
        ctx_ref = outs[0]
        kb, vb = scratch
        hc = kb.shape[1]
        head_of = lax.broadcasted_iota(jnp.int32, (BLK, hc), 1) // HD
        for mb in range(n):
            fill_band(ids, mb, n, sub, qkv, lo, hi, kb, vb)
            for i in range(LOCAL * sub // BLK):
                ok = allowed_of(mb, i, col, row, windowed)
                q = take(ids, qkv, n, sub, mb, i, slice(0, hc))
                band = slice(i * BLK, (i + 3) * BLK)
                k, v = kb[band], vb[band]
                ctx = jnp.zeros((BLK, hc), F32)
                for h in range(hc // HD):
                    qh = jnp.where(head_of == h, q, jnp.zeros_like(q))
                    p = probs_of(qh, k, ok).astype(BF)
                    ctx = jnp.where(head_of == h, mm(p, v, 1, 0), ctx)
                put(ids, ctx_ref, n, sub, mb, i, slice(0, hc), ctx.astype(BF))
        total = ctx_ref.shape[0]
        for first in range(0, total, 256):
            where = slice(first, first + 256)
            store_partial(outs[1:], where, mm(ctx_ref[where], w[:, 3 * hc :], 1, 1))

    return body


def fold_body(ids, ins, outs, scratch):
    rows = outs[0].shape[0]
    for k in range(TEAM):
        where = slice(k * rows, (k + 1) * rows)
        both = ins[0][where].astype(F32) + ins[1][where].astype(F32)
        outs[k][...] = both.astype(outs[k].dtype)


def total_of(refs):
    value = refs[0][...].astype(F32)
    for r in refs[1:]:
        value = value + r[...].astype(F32)
    return value


def resid_body(row):
    def body(ids, ins, outs, scratch):
        x = ins[0][...].astype(F32) + total_of(ins[1 : 1 + TEAM])
        if row is None:
            outs[0][...] = x.astype(BF)
        else:
            outs[0][...] = x
            outs[1][...] = (norm_parts(x)[0] * ins[-1][row : row + 1]).astype(BF)

    return body


def mlp_body(ids, ins, outs, scratch):
    blocks, w = ins[:LOCAL], ins[LOCAL]
    b_ref, gu_ref, hid_ref = outs[:3]
    units = w.shape[1] // 3
    for where, tile in tiles_of(blocks, 256):
        b_ref[where] = tile
        gu = mm(tile, w[:, : 2 * units], 1, 0)
        gu_ref[where] = gu
        hid = (gelu_parts(gu[:, :units])[0] * gu[:, units:]).astype(BF)
        hid_ref[where] = hid
        store_partial(outs[3:], where, mm(hid, w[:, 2 * units :], 1, 1))


def mlp_back_body(ids, ins, outs, scratch):
    blocks, (gu_ref, w) = ins[:LOCAL], ins[LOCAL:]
    dy_ref, dgu_ref = outs[:2]
    units = w.shape[1] // 3
    for where, tile in tiles_of(blocks, 256):
        dy_ref[where] = tile
        dhid = mm(tile, w[:, 2 * units :], 1, 0)
        act, slope = gelu_parts(gu_ref[where, :units])
        dgu_ref[where, :units] = (dhid * gu_ref[where, units:] * slope).astype(BF)
        dgu_ref[where, units:] = (dhid * act).astype(BF)
        store_partial(outs[2:], where, mm(dgu_ref[where], w[:, : 2 * units], 1, 1))


def norm_back_body(row):
    def body(ids, ins, outs, scratch):
        dout = total_of(ins[:TEAM])
        v, dy, gains = ins[TEAM:]
        xhat, rstd = norm_parts(v[...].astype(F32))
        outs[0][...] = jnp.sum(dout * xhat, axis=0, keepdims=True)
        dx = dout * gains[row : row + 1]
        m1 = jnp.mean(dx, axis=-1, keepdims=True)
        m2 = jnp.mean(dx * xhat, axis=-1, keepdims=True)
        dv = dy[...].astype(F32) + rstd * (dx - m1 - xhat * m2)
        outs[1][...] = dv
        if len(outs) > 2:
            outs[2][...] = dv.astype(BF)

    return body


def attn_back_body(windowed, n, sub):
    def body(ids, ins, outs, scratch):
        blocks, (qkv, lo, hi, col, row, w, cos, sin) = ins[:LOCAL], ins[LOCAL:]
        dm_ref, dq_ref, dkv_ref, dlo_ref, dhi_ref = outs
        kb, vb, dctx, dqs, dkb, dvb = scratch
        hc = kb.shape[1]
        for where, tile in tiles_of(blocks, 256):
            dm_ref[where] = tile
            dctx[where] = mm(tile, w[:, 3 * hc :], 1, 0).astype(BF)
        head_of = lax.broadcasted_iota(jnp.int32, (BLK, hc), 1) // HD
        last = BLK + LOCAL * sub
        for mb in range(n):
            fill_band(ids, mb, n, sub, qkv, lo, hi, kb, vb)
            dkb[...] = jnp.zeros(dkb.shape, F32)
            dvb[...] = jnp.zeros(dvb.shape, F32)
            for i in range(LOCAL * sub // BLK):
                ok = allowed_of(mb, i, col, row, windowed)
                q = take(ids, qkv, n, sub, mb, i, slice(0, hc))
                do = take(ids, dctx, n, sub, mb, i, slice(0, hc))
                band = slice(i * BLK, (i + 3) * BLK)
                k, v = kb[band], vb[band]
                dq = jnp.zeros((BLK, hc), F32)
                dk = dkb[band]
                dv = dvb[band]
                for h in range(hc // HD):
                    mine = head_of == h
                    qh = jnp.where(mine, q, jnp.zeros_like(q))
                    doh = jnp.where(mine, do, jnp.zeros_like(do))
                    p = probs_of(qh, k, ok)
                    dp = mm(doh, v, 1, 1)
                    ds = (p * (dp - jnp.sum(p * dp, axis=1, keepdims=True))).astype(BF)
                    dq = jnp.where(mine, mm(ds, k, 1, 0), dq)
                    dk = dk + mm(ds, qh, 0, 0)
                    dv = dv + mm(p.astype(BF), doh, 0, 0)
                put(ids, dqs, n, sub, mb, i, slice(0, hc), 0.125 * dq)
                dkb[band] = dk
                dvb[band] = dv
            edge = slice(mb * BLK, (mb + 1) * BLK)
            dlo_ref[edge, :hc] = (0.125 * dkb[:BLK]).astype(BF)
            dlo_ref[edge, hc:] = dvb[:BLK].astype(BF)
            dhi_ref[edge, :hc] = (0.125 * dkb[last:]).astype(BF)
            dhi_ref[edge, hc:] = dvb[last:].astype(BF)
            for b in range(LOCAL):
                src = slice(BLK + b * sub, BLK + (b + 1) * sub)
                dst = true_rows(ids, n, sub, mb, b)
                dkv_ref[dst, :hc] = 0.125 * dkb[src]
                dkv_ref[dst, hc:] = dvb[src]
        for first in range(0, dqs.shape[0], 256):
            where = slice(first, first + 256)
            g = dqs[where]
            dq_ref[where] = (g * cos[where] + swap_halves(g * sin[where])).astype(BF)

    return body


def qkv_back_body(n, sub):
    def body(ids, ins, outs, scratch):
        dq, dkv, from_next, from_prev, w, cos, sin = ins
        dqkv_ref = outs[0]
        acc = scratch[0]
        hc = w.shape[1] // 4
        acc[...] = dkv[...]
        per = BLK // sub
        for mb in range(n):
            for i in range(per):
                src = slice(mb * BLK + i * sub, mb * BLK + (i + 1) * sub)
                first = true_rows(ids, n, sub, mb, i)
                acc[first] = acc[first] + from_prev[src].astype(F32)
                end = true_rows(ids, n, sub, mb, LOCAL - per + i)
                acc[end] = acc[end] + from_next[src].astype(F32)
        for first in range(0, acc.shape[0], 256):
            where = slice(first, first + 256)
            g = acc[where, :hc]
            dqkv_ref[where, :hc] = dq[where]
            dqkv_ref[where, hc : 2 * hc] = (g * cos[where] + swap_halves(g * sin[where])).astype(BF)
            dqkv_ref[where, 2 * hc :] = acc[where, hc:].astype(BF)
            store_partial(outs[1:], where, mm(dqkv_ref[where], w[:, : 3 * hc], 1, 1))

    return body


def weight_grad_body(ids, ins, outs, scratch):
    full = scratch[0]
    chains = [ins[i : i + 4] for i in range(0, len(ins), 4)]
    cut = chains[0][1].shape[1]
    step = 256
    for first in range(0, full.shape[0], step):
        where = slice(first, first + step)
        full[where, :cut] = sum(mm(c[0][:, where], c[1][...], 0, 0) for c in chains).astype(BF)
        full[where, cut:] = sum(mm(c[2][:, where], c[3][...], 0, 0) for c in chains).astype(BF)
    nz = len(outs)
    span = outs[0].shape[0]
    for s in range(nz):
        dst = ids[0] ^ s if nz == 4 else lax.rem(ids[0] + s, nz)
        outs[s][...] = full[aligned(dst * span, span)]


def plane_sum_body(ids, ins, outs, scratch):
    scratch[0][...] = total_of(ins)
    rows = outs[0].shape[0]
    for k in range(TEAM):
        outs[k][...] = scratch[0][aligned((ids[1] ^ k) * rows, rows)].astype(outs[k].dtype)


def finish_body(ids, ins, outs, scratch):
    g_qkv, g_out, g_in, g_down = outs
    wide = scratch[0]
    layers, hc = g_qkv.shape[0], g_qkv.shape[3] // TEAM
    real, units = g_down.shape[2], wide.shape[1] // TEAM
    for layer in range(layers):
        attn = ins[layer * TEAM : (layer + 1) * TEAM]
        ffn = ins[(layers + layer) * TEAM : (layers + layer + 1) * TEAM]
        for k in range(TEAM):
            cols = aligned((ids[1] ^ k) * hc, hc)
            for i in range(3):
                g_qkv[layer, i, :, cols] = attn[k][:, i * hc : (i + 1) * hc].astype(F32)
            g_out[layer, :, cols] = attn[k][:, 3 * hc :].astype(F32)
        for i in range(3):
            for k in range(TEAM):
                cols = pl.ds(pl.multiple_of((ids[1] ^ k) * units, 128), units)
                wide[:, cols] = ffn[k][:, i * units : (i + 1) * units].astype(F32)
            if i == 2:
                g_down[layer] = wide[:, :real]
            else:
                g_in[layer, i] = wide[:, :real]


def join_body(ids, ins, outs, scratch):
    n, half = outs[0].shape[0], outs[0].shape[1] // 2
    c = ids[2]
    for mb in range(n):
        rows = slice(mb * half, (mb + 1) * half)
        outs[0][mb, aligned(c * half, half)] = ins[0][rows]
        outs[0][mb, aligned((1 - c) * half, half)] = ins[1][rows]


def shards(tokens, cu_seqlens, attn_gain, mlp_gain, w_qkv, w_attn_out, w_ffn_in, w_ffn_out, out_grad):
    nz = lax.axis_size("z")
    z = lax.axis_index("z")
    t = lax.axis_index("y") * 2 + lax.axis_index("x")
    c = lax.axis_index("c")
    ids = jnp.stack([z, t, c]).astype(jnp.int32)
    micro, chip_rows, feat = tokens.shape
    layers, d_rows = w_qkv.shape[0], w_qkv.shape[2]
    hc = w_qkv.shape[3] // TEAM
    sub = chip_rows // 2
    real = w_ffn_in.shape[3]
    units = -(-real // (TEAM * 128)) * 128
    team_rows = TEAM * chip_rows
    per_chain = micro // CHAINS
    n = per_chain
    own = n * sub
    rows = LOCAL * own
    aw, fw = 4 * hc, 3 * units

    owned = jnp.concatenate([attn_gain, mlp_gain, attn_gain, mlp_gain], axis=0)[: 4 * layers]
    started = call(
        "start", start_body, ids,
        [tokens, out_grad, owned, w_qkv, w_attn_out, w_ffn_in, w_ffn_out],
        [out((micro * sub, feat), BF)] * 2
        + [out((d_rows, aw + 128), BF)] * TEAM
        + [out((d_rows, aw), BF)] * ((layers - 1) * TEAM)
        + [out((d_rows, fw), BF)] * (layers * TEAM),
        [pltpu.VMEM((d_rows, TEAM * units), BF)],
    )
    tok_own, grad_own = started[:2]
    packs = started[2:]

    def blocks_of(x):
        mine = [x] + [hop_team(x, k) for k in range(1, TEAM)]
        return mine + [hop_core(b) for b in mine]

    def chain_rows(x, i):
        return x[i * own : (i + 1) * own]

    tok_blocks = [blocks_of(chain_rows(tok_own, i)) for i in range(CHAINS)]

    def plane_of(pieces, name, after=()):
        width = pieces[0].shape[1]
        got = [pieces[0]] + [hop_team(pieces[k], k) for k in range(1, TEAM)]
        return call("plane_" + name, plane_body, ids, got, [out((TEAM * d_rows, width), BF)], after=after)[0]

    def full_of(plane, name, relay=True):
        width = plane.shape[1]
        if nz == 4 and relay:
            far = hop_z(plane, 2)
            planes = [plane, hop_z(plane, 1), far, hop_z(far, 1)]
        else:
            far = plane
            planes = [plane] + [hop_z(plane, s) for s in range(1, nz)]
        full = call("full_" + name, full_body, ids, planes, [out((nz * TEAM * d_rows, width), BF)])[0]
        return full, far

    def pack(kind, layer):
        first = (kind * layers + layer) * TEAM
        return packs[first : first + TEAM]

    planes_a, planes_f = [plane_of(pack(0, 0), "a0")], [plane_of(pack(1, 0), "f0")]
    planes = [planes_a[0]] + [hop_z(planes_a[0], s) for s in range(1, nz)]
    wa0, gains = call(
        "full_a0", full_gains_body, ids, planes,
        [out((feat, aw), BF), out((4 * layers, feat), F32)], [pltpu.VMEM((feat, 128), BF)],
    )
    attn_w, ffn_w, far_f = [wa0], [], []
    for i in range(layers):
        if i > 0:
            planes_a.append(plane_of(pack(0, i), "a" + str(i), ffn_w[i - 1 :]))
            attn_w.append(full_of(planes_a[i], "a" + str(i), False)[0])
            planes_f.append(plane_of(pack(1, i), "f" + str(i), attn_w[i:]))
        w, far = full_of(planes_f[i], "f" + str(i))
        ffn_w.append(w)
        far_f.append(far)
    grad_blocks = [blocks_of(chain_rows(grad_own, i)) for i in range(CHAINS)]

    band_index = z * team_rows - BLK + jnp.arange(team_rows + 2 * BLK, dtype=jnp.int32)
    inside = (band_index >= 0) & (band_index < cu_seqlens[0, -1])
    docs = jnp.sum((band_index[None, :, None] >= cu_seqlens[:, None, 1:-1]).astype(jnp.int32), axis=2)
    docs = jnp.where(inside[None], docs, -1)
    block = jnp.arange(LOCAL, dtype=jnp.int32)
    true_block = ((block % TEAM) ^ t) * 2 + ((block // TEAM) ^ c)
    index = z * team_rows + true_block[:, None] * sub + jnp.arange(sub, dtype=jnp.int32)[None]
    begin = jnp.max(
        jnp.where(
            index[:, None, :, None] >= cu_seqlens[None, :, None, :-1], cu_seqlens[None, :, None, :-1], 0
        ),
        axis=3,
    )
    offsets = (index[:, None] - begin).astype(F32)
    lane = jnp.arange(hc, dtype=jnp.int32) % HD
    sign = jnp.where(lane < HD // 2, -1.0, 1.0)

    state = []
    for i in range(CHAINS):
        mbs = slice(i * n, (i + 1) * n)
        tables = []
        for layer in range(layers):
            base = 10000.0 if layer % 2 == 0 else 160000.0
            inv = base ** (-((lane % (HD // 2)).astype(F32) * 2.0 / HD))
            ang = offsets[:, mbs].reshape(rows, 1) * inv
            tables.append((jnp.cos(ang), jnp.sin(ang) * sign))
        state.append(
            {
                "tables": tables,
                "col": docs[mbs, :, None],
                "row": docs[mbs, None, :],
                "x": chain_rows(tok_own, i),
                "blocks": tok_blocks[i],
                "saved": [],
            }
        )

    partial_out = [out((rows // 2, feat), BF)] * 2
    band = pltpu.VMEM((team_rows + 2 * BLK, hc), BF)
    band32 = pltpu.VMEM((team_rows + 2 * BLK, hc), F32)

    def fold(parts, name, after=()):
        got = hop_core(parts[1])
        h = call(
            "fold_" + name, fold_body, ids, [parts[0], got],
            [out((own, feat), F32)] + [out((own, feat), BF)] * (TEAM - 1), after=after,
        )
        return [h[0]] + [hop_team(h[k], k) for k in range(1, TEAM)]

    def forward_attn(st, layer):
        windowed = layer % 2 == 0
        w = attn_w[layer]
        cos, sin = st["tables"][layer]
        a, qkv, lo, hi = call(
            "qkv", qkv_body(layer, layer == 0, n, sub), ids, st["blocks"] + [gains, w, cos, sin],
            [out((rows, feat), BF), out((rows, 3 * hc), BF)] + [out((n * BLK, 2 * hc), BF)] * 2,
            flops=2 * rows * feat * 3 * hc, after=[planes_f[0] if layer == 0 else far_f[layer]],
        )
        lo, hi = step_z(lo, 1), step_z(hi, -1)
        ctx, *parts = call(
            "attn", attn_body(windowed, n, sub), ids, [qkv, lo, hi, st["col"], st["row"], w],
            [out((rows, hc), BF)] + partial_out, [band] * 2, flops=4 * rows * feat * hc,
        )
        terms = fold(parts, "attn")
        mid, b = call(
            "mid", resid_body(layers + layer), ids, [st["x"]] + terms + [gains],
            [out((own, feat), F32), out((own, feat), BF)],
        )
        st["saved"].append([st["x"], a, qkv, lo, hi, ctx, mid])
        st["x"] = mid
        st["blocks"] = blocks_of(b)

    def forward_mlp(st, layer):
        b, gu, hid, *parts = call(
            "mlp", mlp_body, ids, st["blocks"] + [ffn_w[layer]],
            [out((rows, feat), BF), out((rows, 2 * units), F32), out((rows, units), BF)] + partial_out,
            flops=6 * rows * feat * units,
        )
        st["saved"][layer] += [b, gu, hid]
        terms = fold(parts, "mlp")
        if layer + 1 < layers:
            st["x"], a = call(
                "next", resid_body(layer + 1), ids, [st["x"]] + terms + [gains],
                [out((own, feat), F32), out((own, feat), BF)],
                after=[attn_w[layer + 1], planes_f[layer + 1]],
            )
            st["blocks"] = blocks_of(a)
        else:
            st["x"] = call("last", resid_body(None), ids, [st["x"]] + terms, [out((own, feat), BF)])[0]

    for layer in range(layers):
        for st in state:
            forward_attn(st, layer)
        for st in state:
            forward_mlp(st, layer)

    def join(parts, dtype):
        x = parts[0] if CHAINS == 1 else jnp.concatenate(parts, axis=0)
        return call("join", join_body, ids, [x, hop_core(x)], [out((micro, chip_rows, feat), dtype)])[0]

    hidden_out = join([st["x"] for st in state], BF)

    for i, st in enumerate(state):
        st["dy"] = chain_rows(grad_own, i)
        st["blocks"] = grad_blocks[i]

    def weight_pieces(ins, width, name):
        return call(
            "wgrad_" + name, weight_grad_body, ids, ins, [out((TEAM * d_rows, width), BF)] * nz,
            [pltpu.VMEM((nz * TEAM * d_rows, width), BF)], flops=2 * rows * CHAINS * feat * width,
        )

    def relay(pieces, name):
        if nz != 4:
            return [pieces[0]] + [hop_z(pieces[s], s) for s in range(1, nz)]
        near = hop_z(pieces[1], 1)
        far = call("relay_" + name, add_body, ids, [pieces[2], hop_z(pieces[3], 1)], [out(pieces[2].shape, BF)])[0]
        return [pieces[0], near, hop_z(far, 2)]

    def z_sum(got, name):
        width = got[0].shape[1]
        mine = call(
            "zsum_" + name, plane_sum_body, ids, got,
            [out((d_rows, width), F32)] + [out((d_rows, width), BF)] * (TEAM - 1),
            [pltpu.VMEM((TEAM * d_rows, width), F32)],
        )
        return [mine[0]] + [hop_team(mine[k], k) for k in range(1, TEAM)]

    gain_rows = [None] * (2 * layers)

    def add_gain(row, dg):
        gain_rows[row] = dg if gain_rows[row] is None else gain_rows[row] + dg

    attn_parts, ffn_parts = [None] * layers, [None] * layers
    st = state[0]
    wait_mlp, wait_fold, wait_mid = [], [], []
    for layer in reversed(range(layers)):
        w = attn_w[layer]
        cos, sin = st["tables"][layer]
        x_in, a, qkv, lo, hi, ctx, mid, b, gu, hid = st["saved"][layer]
        dy, dgu, *parts = call(
            "mlp_back", mlp_back_body, ids, st["blocks"] + [gu, ffn_w[layer]],
            [out((rows, feat), BF), out((rows, 2 * units), BF)] + partial_out,
            flops=6 * rows * feat * units, after=wait_mlp,
        )
        terms = fold(parts, "mlp_back", wait_fold)
        pieces = weight_pieces([b, dgu, dy, hid], fw, "f" + str(layer))
        dg, dmid, dmb = call(
            "mid_back", norm_back_body(layers + layer), ids, terms + [mid, st["dy"], gains],
            [out((1, feat), F32), out((own, feat), F32), out((own, feat), BF)],
            after=pieces + wait_mid,
        )
        add_gain(layers + layer, dg)
        relayed = relay(pieces, "f" + str(layer))
        dm, dq, dkv, dlo, dhi = call(
            "attn_back", attn_back_body(layer % 2 == 0, n, sub), ids,
            blocks_of(dmb) + [qkv, lo, hi, st["col"], st["row"], w, cos, sin],
            [out((rows, feat), BF), out((rows, hc), BF), out((rows, 2 * hc), F32)]
            + [out((n * BLK, 2 * hc), BF)] * 2,
            [band] * 2 + [pltpu.VMEM((rows, hc), BF), pltpu.VMEM((rows, hc), F32)] + [band32] * 2,
            flops=6 * rows * feat * hc,
        )
        from_next, from_prev = step_z(dlo, -1), step_z(dhi, 1)
        ffn_parts[layer] = z_sum(relayed, "f" + str(layer))
        dqkv, *parts = call(
            "qkv_back", qkv_back_body(n, sub), ids, [dq, dkv, from_next, from_prev, w, cos, sin],
            [out((rows, 3 * hc), BF)] + partial_out, [pltpu.VMEM((rows, 2 * hc), F32)],
            flops=6 * rows * feat * hc,
            after=ffn_parts[layer][:1] + ([st["x"]] if layer + 1 == layers else []),
        )
        pieces = weight_pieces([a, dqkv, dm, ctx], aw, "a" + str(layer))
        terms = fold(parts, "qkv_back", pieces if layer == 0 else [])
        low = [out((own, feat), BF)] if layer > 0 else []
        dg, st["dy"], *dyb = call(
            "in_back", norm_back_body(layer), ids, terms + [x_in, dmid, gains],
            [out((1, feat), F32), out((own, feat), F32)] + low, after=pieces + ffn_parts[layer],
        )
        add_gain(layer, dg)
        if layer > 0:
            st["blocks"] = blocks_of(dyb[0])
            relayed = relay(pieces, "a" + str(layer))
            attn_parts[layer] = z_sum(relayed, "a" + str(layer))
            wait_mlp = relayed[1:2]
            wait_fold = attn_parts[layer][:1]
            wait_mid = attn_parts[layer]
        else:
            got = [pieces[0]] + [hop_z(pieces[s], s) for s in range(1, nz)]
            attn_parts[layer] = z_sum(got, "a" + str(layer))

    input_grad = join([st["dy"] for st in state], F32)

    dgain = jnp.concatenate(gain_rows + gain_rows, axis=0)[: 4 * layers]
    dgain = dgain + hop_core(dgain)
    dgain = dgain + hop_team(dgain, 1)
    dgain = dgain + hop_team(dgain, 2)
    dgain = sum([dgain] + [hop_z(dgain, s) for s in range(1, nz)])
    dgain = lax.dynamic_slice_in_dim(dgain, (z * TEAM + t) * d_rows, d_rows, axis=1)

    g_qkv, g_out, g_in, g_down = call(
        "finish", finish_body, ids, sum(attn_parts, []) + sum(ffn_parts, []),
        [out(w_qkv.shape, F32), out(w_attn_out.shape, F32), out(w_ffn_in.shape, F32), out(w_ffn_out.shape, F32)],
        [pltpu.VMEM((d_rows, TEAM * units), F32)],
    )
    return (
        hidden_out,
        input_grad,
        dgain[:layers],
        dgain[layers : 2 * layers],
        g_qkv,
        g_out,
        g_in,
        g_down,
    )


def solution(mesh):
    dp, tensor = mesh.devices.shape
    fine = Mesh(mesh.devices.reshape(dp // TEAM, 2, 2, tensor), ("z", "y", "x", "c"))
    rows = ("z", "y", "x")
    in_specs = (
        P(None, rows, None),
        P(),
        P(None, rows),
        P(None, rows),
        P(None, None, rows, "c"),
        P(None, rows, "c"),
        P(None, None, rows, "c"),
        P(None, rows, "c"),
        P(None, rows, None),
    )
    out_specs = (
        P(None, rows, None),
        P(None, rows, None),
        P(None, rows),
        P(None, rows),
        P(None, None, rows, "c"),
        P(None, rows, "c"),
        P(None, None, rows, "c"),
        P(None, rows, "c"),
    )
    return jax.shard_map(shards, mesh=fine, in_specs=in_specs, out_specs=out_specs, check_vma=False)
```

```python
import jax
import jax.numpy as jnp
from jax import lax
from jax.experimental import pallas as pl
from jax.experimental.pallas import tpu as pltpu
from jax.sharding import Mesh
from jax.sharding import PartitionSpec as P

HD = 64
HALF = 64
BLK = 128
TEAM = 4
LOCAL = 2 * TEAM
MASKED = -1e30
BF = jnp.bfloat16
F32 = jnp.float32
CHAINS = 1


def mm(a, b, ca, cb):
    return lax.dot_general(a, b, (((ca,), (cb,)), ((), ())), preferred_element_type=F32)


def hop_team(x, k):
    return lax.ppermute(x, ("y", "x"), [(i, i ^ k) for i in range(TEAM)])


def hop_core(x):
    return lax.ppermute(x, "c", [(0, 1), (1, 0)])


def hop_z(x, s):
    n = lax.axis_size("z")
    return lax.ppermute(x, "z", [(i, i ^ s if n == 4 else (i + s) % n) for i in range(n)])


def step_z(x, by):
    n = lax.axis_size("z")
    return lax.ppermute(x, "z", [(i, i + by) for i in range(n) if 0 <= i + by < n])


def out(shape, dtype):
    return jax.ShapeDtypeStruct(shape, dtype)


def call(name, body, ids, ins, outs, scratch=(), flops=0, after=()):
    ins, after = list(ins), list(after)

    def kernel(*refs):
        n_in, n_out = len(ins), len(outs)
        rest = refs[1 + n_in + len(after) :]
        body(refs[0], refs[1 : 1 + n_in], rest[:n_out], rest[n_out:])

    moved = sum(a.size * a.dtype.itemsize for a in ins) + sum(
        o.size * jnp.dtype(o.dtype).itemsize for o in outs
    )
    vmem = pl.BlockSpec(memory_space=pltpu.VMEM)
    results = pl.pallas_call(
        kernel,
        name=name,
        in_specs=[pl.BlockSpec(memory_space=pltpu.SMEM)] + [vmem] * len(ins)
        + [pl.BlockSpec(memory_space=pl.ANY)] * len(after),
        out_specs=[vmem] * len(outs),
        out_shape=list(outs),
        scratch_shapes=list(scratch),
        compiler_params=pltpu.CompilerParams(vmem_limit_bytes=24 * 1024 * 1024),
        cost_estimate=pl.CostEstimate(flops=flops, bytes_accessed=moved, transcendentals=0),
    )(ids, *ins, *after)
    return list(results)


def aligned(start, size):
    return pl.ds(pl.multiple_of(start, size), size)


def norm_parts(v):
    cent = v - jnp.mean(v, axis=-1, keepdims=True)
    rstd = lax.rsqrt(jnp.mean(cent * cent, axis=-1, keepdims=True) + 1e-05)
    return cent * rstd, rstd


def gelu_parts(gate):
    cdf = 0.5 * (1.0 + lax.erf(gate * 0.7071067811865476))
    return gate * cdf, cdf + gate * jnp.exp(-0.5 * gate * gate) * 0.3989422804014327


def swap_halves(v):
    width = v.shape[-1]
    lane = lax.broadcasted_iota(jnp.int32, v.shape, 1) % HD
    return jnp.where(
        lane < HD // 2, pltpu.roll(v, width - HD // 2, 1), pltpu.roll(v, HD // 2, 1)
    )


def true_rows(ids, n, sub, mb, b):
    blk = (ids[2] ^ (b % 2)) * TEAM + (ids[1] ^ (b // 2))
    return aligned((blk * n + mb) * sub, sub)


def tiles_of(refs, tile):
    rows = refs[0].shape[0]
    per = max(1, tile // rows)
    for first in range(0, len(refs), per):
        group = [r[...] for r in refs[first : first + per]]
        yield slice(first * rows, (first + per) * rows), (
            group[0] if per == 1 else jnp.concatenate(group, axis=0)
        )


def store_partial(p_refs, where, value):
    half = p_refs[0].shape[0]
    which = where.start // half
    p_refs[which][where.start - which * half : where.stop - which * half, :] = value.astype(BF)


def start_attn_body(ids, ins, outs, scratch):
    w_qkv, w_out = ins
    layers, hc = w_qkv.shape[0], w_qkv.shape[3] // TEAM
    for layer in range(layers):
        for k in range(TEAM):
            cols = aligned((ids[1] ^ k) * hc, hc)
            if layer == 0:
                dst, rest, at = outs[k], outs[TEAM + k], 0
            else:
                dst = rest = outs[(layer + 1) * TEAM + k]
                at = 3 * hc
            for i in range(3):
                dst[:, i * hc : (i + 1) * hc] = w_qkv[layer, i, :, cols]
            rest[:, at : at + hc] = w_out[layer, :, cols]


def start_body(ids, ins, outs, scratch):
    tokens, grads, w_in, w_down, owned = ins
    t, c = ids[1], ids[2]
    n, half = tokens.shape[0], tokens.shape[1] // 2
    for src, dst in ((tokens, outs[0]), (grads, outs[1])):
        for mb in range(n):
            dst[mb * half : (mb + 1) * half] = src[mb, aligned(c * half, half)]
    spot = lax.broadcasted_iota(jnp.int32, owned.shape, 1) // w_in.shape[2] == ids[0] * TEAM + t
    outs[2][...] = jnp.where(spot, owned[...], 0.0)
    packs = outs[3:]
    real, units = w_in.shape[3], scratch[0].shape[1] // TEAM
    scratch[0][...] = jnp.zeros(scratch[0].shape, BF)
    for layer in range(w_in.shape[0]):
        for i in range(3):
            scratch[0][:, :real] = w_down[layer] if i == 2 else w_in[layer, i]
            for k in range(TEAM):
                cols = pl.ds(pl.multiple_of((t ^ k) * units, 128), units)
                packs[layer * TEAM + k][:, i * units : (i + 1) * units] = scratch[0][:, cols]


def plane_body(ids, ins, outs, scratch):
    rows = ins[0].shape[0]
    for k in range(TEAM):
        outs[0][aligned((ids[1] ^ k) * rows, rows)] = ins[k][...]


def full_body(ids, ins, outs, scratch):
    rows, nz = ins[0].shape[0], len(ins)
    for s in range(nz):
        src = ids[0] ^ s if nz == 4 else lax.rem(ids[0] - s + nz, nz)
        outs[0][aligned(src * rows, rows)] = ins[s][...]


def add_body(ids, ins, outs, scratch):
    outs[0][...] = total_of(ins).astype(BF)


def qkv_body(row, raw, n, sub):
    def body(ids, ins, outs, scratch):
        blocks, (gains, w, cos, sin) = ins[:LOCAL], ins[LOCAL:]
        a_ref, qkv_ref, lo_ref, hi_ref = outs
        hc = cos.shape[1]
        for where, tile in tiles_of(blocks, 256):
            if raw:
                tile = (norm_parts(tile.astype(F32))[0] * gains[row : row + 1]).astype(BF)
            a_ref[where] = tile
            r = mm(tile, w[:, : 3 * hc], 1, 0)
            cs, sn = cos[where], sin[where]
            q, k = r[:, :hc], r[:, hc : 2 * hc]
            qkv_ref[where, :hc] = (q * cs + swap_halves(q) * sn).astype(BF)
            qkv_ref[where, hc : 2 * hc] = (k * cs + swap_halves(k) * sn).astype(BF)
            qkv_ref[where, 2 * hc :] = r[:, 2 * hc :].astype(BF)
        per = BLK // sub
        for mb in range(n):
            for i in range(per):
                dst = slice(mb * BLK + i * sub, mb * BLK + (i + 1) * sub)
                lo_ref[dst] = qkv_ref[true_rows(ids, n, sub, mb, LOCAL - per + i), hc:]
                hi_ref[dst] = qkv_ref[true_rows(ids, n, sub, mb, i), hc:]

    return body


def fill_band(ids, mb, n, sub, qkv, lo, hi, kb, vb):
    hc = kb.shape[1]
    edge = slice(mb * BLK, (mb + 1) * BLK)
    last = BLK + LOCAL * sub
    kb[:BLK], vb[:BLK] = lo[edge, :hc], lo[edge, hc:]
    kb[last:], vb[last:] = hi[edge, :hc], hi[edge, hc:]
    for b in range(LOCAL):
        src = true_rows(ids, n, sub, mb, b)
        dst = slice(BLK + b * sub, BLK + (b + 1) * sub)
        kb[dst] = qkv[src, hc : 2 * hc]
        vb[dst] = qkv[src, 2 * hc :]


def keys_of(i, windowed):
    return slice(i * BLK + BLK - HALF, (i + 2) * BLK + HALF) if windowed else slice(i * BLK, (i + 3) * BLK)


def allowed_of(mb, i, col, row, windowed):
    keys = keys_of(0, windowed)
    width = keys.stop - keys.start
    ok = col[mb, BLK + i * BLK : 2 * BLK + i * BLK, :] == row[mb, :, i * BLK : i * BLK + width]
    if windowed:
        shape = (BLK, width)
        gap = lax.broadcasted_iota(jnp.int32, shape, 1) - lax.broadcasted_iota(jnp.int32, shape, 0)
        ok = ok & (gap <= 2 * HALF) & (gap >= 0)
    return ok


def take(ids, ref, n, sub, mb, i, lanes):
    per = BLK // sub
    return jnp.concatenate(
        [ref[true_rows(ids, n, sub, mb, per * i + e), lanes] for e in range(per)], axis=0
    )


def put(ids, ref, n, sub, mb, i, lanes, value):
    for e in range(BLK // sub):
        per = BLK // sub
        ref[true_rows(ids, n, sub, mb, per * i + e), lanes] = value[e * sub : (e + 1) * sub]


def probs_of(qh, k, ok):
    s = jnp.where(ok, mm(qh, k, 1, 1), MASKED)
    e = jnp.exp(s - jnp.max(s, axis=1, keepdims=True))
    return e * (1.0 / jnp.sum(e, axis=1, keepdims=True))


def attn_body(windowed, n, sub):
    def body(ids, ins, outs, scratch):
        qkv, lo, hi, col, row, w = ins
        ctx_ref = outs[0]
        kb, vb = scratch
        hc = kb.shape[1]
        head_of = lax.broadcasted_iota(jnp.int32, (BLK, hc), 1) // HD
        for mb in range(n):
            fill_band(ids, mb, n, sub, qkv, lo, hi, kb, vb)
            for i in range(LOCAL * sub // BLK):
                ok = allowed_of(mb, i, col, row, windowed)
                q = take(ids, qkv, n, sub, mb, i, slice(0, hc)) * jnp.asarray(0.125, BF)
                band = keys_of(i, windowed)
                k, v = kb[band], vb[band]
                ctx = jnp.zeros((BLK, hc), F32)
                for h in range(hc // HD):
                    qh = jnp.where(head_of == h, q, jnp.zeros_like(q))
                    p = probs_of(qh, k, ok).astype(BF)
                    ctx = jnp.where(head_of == h, mm(p, v, 1, 0), ctx)
                put(ids, ctx_ref, n, sub, mb, i, slice(0, hc), ctx.astype(BF))
        total = ctx_ref.shape[0]
        for first in range(0, total, 256):
            where = slice(first, first + 256)
            store_partial(outs[1:], where, mm(ctx_ref[where], w[:, w.shape[1] - hc :], 1, 1))

    return body


def fold_body(ids, ins, outs, scratch):
    rows = outs[0].shape[0]
    for k in range(TEAM):
        where = slice(k * rows, (k + 1) * rows)
        both = ins[0][where].astype(F32) + ins[1][where].astype(F32)
        outs[k][...] = both.astype(outs[k].dtype)


def total_of(refs):
    value = refs[0][...].astype(F32)
    for r in refs[1:]:
        value = value + r[...].astype(F32)
    return value


def resid_body(row):
    def body(ids, ins, outs, scratch):
        x = ins[0][...].astype(F32) + total_of(ins[1 : 1 + TEAM])
        if row is None:
            outs[0][...] = x.astype(BF)
        else:
            outs[0][...] = x
            outs[1][...] = (norm_parts(x)[0] * ins[-1][row : row + 1]).astype(BF)

    return body


def mlp_body(ids, ins, outs, scratch):
    blocks, w = ins[:LOCAL], ins[LOCAL]
    b_ref, gu_ref, hid_ref = outs[:3]
    units = w.shape[1] // 3
    for where, tile in tiles_of(blocks, 256):
        b_ref[where] = tile
        gu = mm(tile, w[:, : 2 * units], 1, 0)
        gu_ref[where] = gu
        hid = (gelu_parts(gu[:, :units])[0] * gu[:, units:]).astype(BF)
        hid_ref[where] = hid
        store_partial(outs[3:], where, mm(hid, w[:, 2 * units :], 1, 1))


def mlp_back_body(ids, ins, outs, scratch):
    blocks, (gu_ref, w) = ins[:LOCAL], ins[LOCAL:]
    dy_ref, dgu_ref = outs[:2]
    units = w.shape[1] // 3
    for where, tile in tiles_of(blocks, 256):
        dy_ref[where] = tile
        dhid = mm(tile, w[:, 2 * units :], 1, 0)
        act, slope = gelu_parts(gu_ref[where, :units])
        dgu_ref[where, :units] = (dhid * gu_ref[where, units:] * slope).astype(BF)
        dgu_ref[where, units:] = (dhid * act).astype(BF)
        store_partial(outs[2:], where, mm(dgu_ref[where], w[:, : 2 * units], 1, 1))


def norm_back_body(row):
    def body(ids, ins, outs, scratch):
        dout = total_of(ins[:TEAM])
        v, dy, gains = ins[TEAM:]
        xhat, rstd = norm_parts(v[...].astype(F32))
        outs[0][...] = jnp.sum(dout * xhat, axis=0, keepdims=True)
        dx = dout * gains[row : row + 1]
        m1 = jnp.mean(dx, axis=-1, keepdims=True)
        m2 = jnp.mean(dx * xhat, axis=-1, keepdims=True)
        dv = dy[...].astype(F32) + rstd * (dx - m1 - xhat * m2)
        outs[1][...] = dv
        if len(outs) > 2:
            outs[2][...] = dv.astype(BF)

    return body


def attn_back_body(windowed, n, sub):
    def body(ids, ins, outs, scratch):
        blocks, (qkv, lo, hi, col, row, w, cos, sin) = ins[:LOCAL], ins[LOCAL:]
        dm_ref, dq_ref, dkv_ref, dlo_ref, dhi_ref = outs
        kb, vb, dctx, dqs, dkb, dvb = scratch
        hc = kb.shape[1]
        for where, tile in tiles_of(blocks, 256):
            dm_ref[where] = tile
            dctx[where] = mm(tile, w[:, w.shape[1] - hc :], 1, 0).astype(BF)
        head_of = lax.broadcasted_iota(jnp.int32, (BLK, hc), 1) // HD
        last = BLK + LOCAL * sub
        for mb in range(n):
            fill_band(ids, mb, n, sub, qkv, lo, hi, kb, vb)
            dkb[...] = jnp.zeros(dkb.shape, F32)
            dvb[...] = jnp.zeros(dvb.shape, F32)
            for i in range(LOCAL * sub // BLK):
                ok = allowed_of(mb, i, col, row, windowed)
                q = take(ids, qkv, n, sub, mb, i, slice(0, hc)) * jnp.asarray(0.125, BF)
                do = take(ids, dctx, n, sub, mb, i, slice(0, hc))
                band = keys_of(i, windowed)
                k, v = kb[band], vb[band]
                dq = jnp.zeros((BLK, hc), F32)
                dk = dkb[band]
                dv = dvb[band]
                for h in range(hc // HD):
                    mine = head_of == h
                    qh = jnp.where(mine, q, jnp.zeros_like(q))
                    doh = jnp.where(mine, do, jnp.zeros_like(do))
                    p = probs_of(qh, k, ok)
                    dp = mm(doh, v, 1, 1)
                    ds = (p * (dp - jnp.sum(p * dp, axis=1, keepdims=True))).astype(BF)
                    dq = jnp.where(mine, mm(ds, k, 1, 0), dq)
                    dk = dk + mm(ds, qh, 0, 0)
                    dv = dv + mm(p.astype(BF), doh, 0, 0)
                put(ids, dqs, n, sub, mb, i, slice(0, hc), 0.125 * dq)
                dkb[band] = dk
                dvb[band] = dv
            edge = slice(mb * BLK, (mb + 1) * BLK)
            dlo_ref[edge, :hc] = dkb[:BLK].astype(BF)
            dlo_ref[edge, hc:] = dvb[:BLK].astype(BF)
            dhi_ref[edge, :hc] = dkb[last:].astype(BF)
            dhi_ref[edge, hc:] = dvb[last:].astype(BF)
            for b in range(LOCAL):
                src = slice(BLK + b * sub, BLK + (b + 1) * sub)
                dst = true_rows(ids, n, sub, mb, b)
                dkv_ref[dst, :hc] = dkb[src]
                dkv_ref[dst, hc:] = dvb[src]
        for first in range(0, dqs.shape[0], 256):
            where = slice(first, first + 256)
            g = dqs[where]
            dq_ref[where] = (g * cos[where] + swap_halves(g * sin[where])).astype(BF)

    return body


def qkv_back_body(n, sub):
    def body(ids, ins, outs, scratch):
        dq, dkv, from_next, from_prev, w, cos, sin = ins
        dqkv_ref = outs[0]
        acc = scratch[0]
        hc = cos.shape[1]
        acc[...] = dkv[...]
        per = BLK // sub
        for mb in range(n):
            for i in range(per):
                src = slice(mb * BLK + i * sub, mb * BLK + (i + 1) * sub)
                first = true_rows(ids, n, sub, mb, i)
                acc[first] = acc[first] + from_prev[src].astype(F32)
                end = true_rows(ids, n, sub, mb, LOCAL - per + i)
                acc[end] = acc[end] + from_next[src].astype(F32)
        for first in range(0, acc.shape[0], 256):
            where = slice(first, first + 256)
            g = acc[where, :hc]
            dqkv_ref[where, :hc] = dq[where]
            dqkv_ref[where, hc : 2 * hc] = (g * cos[where] + swap_halves(g * sin[where])).astype(BF)
            dqkv_ref[where, 2 * hc :] = acc[where, hc:].astype(BF)
            store_partial(outs[1:], where, mm(dqkv_ref[where], w[:, : 3 * hc], 1, 1))

    return body


def weight_grad_body(ids, ins, outs, scratch):
    full = scratch[0]
    chains = [ins[i : i + 4] for i in range(0, len(ins), 4)]
    cut = chains[0][1].shape[1]
    step = 256
    for first in range(0, full.shape[0], step):
        where = slice(first, first + step)
        full[where, :cut] = sum(mm(c[0][:, where], c[1][...], 0, 0) for c in chains).astype(BF)
        full[where, cut:] = sum(mm(c[2][:, where], c[3][...], 0, 0) for c in chains).astype(BF)
    nz = len(outs)
    span = outs[0].shape[0]
    for s in range(nz):
        dst = ids[0] ^ s if nz == 4 else lax.rem(ids[0] + s, nz)
        outs[s][...] = full[aligned(dst * span, span)]


def plane_sum_body(ids, ins, outs, scratch):
    scratch[0][...] = total_of(ins)
    rows = outs[0].shape[0]
    for k in range(TEAM):
        outs[k][...] = scratch[0][aligned((ids[1] ^ k) * rows, rows)].astype(outs[k].dtype)


def finish_body(ids, ins, outs, scratch):
    g_qkv, g_out, g_in, g_down = outs
    wide = scratch[0]
    layers, hc = g_qkv.shape[0], g_qkv.shape[3] // TEAM
    real, units = g_down.shape[2], wide.shape[1] // TEAM
    for layer in range(layers):
        attn = ins[layer * TEAM : (layer + 1) * TEAM]
        ffn = ins[(layers + layer) * TEAM : (layers + layer + 1) * TEAM]
        for k in range(TEAM):
            cols = aligned((ids[1] ^ k) * hc, hc)
            for i in range(3):
                g_qkv[layer, i, :, cols] = attn[k][:, i * hc : (i + 1) * hc].astype(F32)
            g_out[layer, :, cols] = attn[k][:, 3 * hc :].astype(F32)
        for i in range(3):
            for k in range(TEAM):
                cols = pl.ds(pl.multiple_of((ids[1] ^ k) * units, 128), units)
                wide[:, cols] = ffn[k][:, i * units : (i + 1) * units].astype(F32)
            if i == 2:
                g_down[layer] = wide[:, :real]
            else:
                g_in[layer, i] = wide[:, :real]


def join_body(ids, ins, outs, scratch):
    n, half = outs[0].shape[0], outs[0].shape[1] // 2
    c = ids[2]
    for mb in range(n):
        rows = slice(mb * half, (mb + 1) * half)
        outs[0][mb, aligned(c * half, half)] = ins[0][rows]
        outs[0][mb, aligned((1 - c) * half, half)] = ins[1][rows]


def shards(tokens, cu_seqlens, attn_gain, mlp_gain, w_qkv, w_attn_out, w_ffn_in, w_ffn_out, out_grad):
    nz = lax.axis_size("z")
    z = lax.axis_index("z")
    t = lax.axis_index("y") * 2 + lax.axis_index("x")
    c = lax.axis_index("c")
    ids = jnp.stack([z, t, c]).astype(jnp.int32)
    micro, chip_rows, feat = tokens.shape
    layers, d_rows = w_qkv.shape[0], w_qkv.shape[2]
    hc = w_qkv.shape[3] // TEAM
    sub = chip_rows // 2
    real = w_ffn_in.shape[3]
    units = -(-real // (TEAM * 128)) * 128
    team_rows = TEAM * chip_rows
    per_chain = micro // CHAINS
    n = per_chain
    own = n * sub
    rows = LOCAL * own
    aw, fw = 4 * hc, 3 * units

    owned = jnp.concatenate([attn_gain, mlp_gain, attn_gain, mlp_gain], axis=0)[: 4 * layers]
    owned = jnp.tile(owned.astype(F32), (1, feat // d_rows))
    packs_a = call(
        "start_attn", start_attn_body, ids, [w_qkv, w_attn_out],
        [out((d_rows, 3 * hc), BF)] * TEAM
        + [out((d_rows, hc), BF)] * TEAM
        + [out((d_rows, aw), BF)] * ((layers - 1) * TEAM),
    )

    def plane_of(pieces, name, after=()):
        width = pieces[0].shape[1]
        got = [pieces[0]] + [hop_team(pieces[k], k) for k in range(1, TEAM)]
        return call("plane_" + name, plane_body, ids, got, [out((TEAM * d_rows, width), BF)], after=after)[0]

    plane_qkv = plane_of(packs_a[:TEAM], "q0")
    tok_own, grad_own, gains, *packs_f = call(
        "start", start_body, ids, [tokens, out_grad, w_ffn_in, w_ffn_out, owned],
        [out((micro * sub, feat), BF)] * 2
        + [out((4 * layers, feat), F32)]
        + [out((d_rows, fw), BF)] * (layers * TEAM),
        [pltpu.VMEM((d_rows, TEAM * units), BF)], after=[plane_qkv],
    )
    plane_out = plane_of(packs_a[TEAM : 2 * TEAM], "o0")

    def blocks_of(x):
        mine = [x] + [hop_team(x, k) for k in range(1, TEAM)]
        return mine + [hop_core(b) for b in mine]

    def chain_rows(x, i):
        return x[i * own : (i + 1) * own]

    tok_blocks = [blocks_of(chain_rows(tok_own, i)) for i in range(CHAINS)]

    def full_of(plane, name, relay=True):
        width = plane.shape[1]
        if nz == 4 and relay:
            far = hop_z(plane, 2)
            planes = [plane, hop_z(plane, 1), far, hop_z(far, 1)]
        else:
            far = plane
            planes = [plane] + [hop_z(plane, s) for s in range(1, nz)]
        full = call("full_" + name, full_body, ids, planes, [out((nz * TEAM * d_rows, width), BF)])[0]
        return full, far

    gains = sum([gains] + [hop_team(gains, k) for k in range(1, TEAM)])
    gains = sum([gains] + [hop_z(gains, s) for s in range(1, nz)])

    def pack(kind, layer):
        if kind == 0:
            return packs_a[(layer + 1) * TEAM : (layer + 2) * TEAM]
        return packs_f[layer * TEAM : (layer + 1) * TEAM]

    w_q0 = full_of(plane_qkv, "q0", False)[0]
    w_o0 = full_of(plane_out, "o0", False)[0]
    planes_a, planes_f = [plane_out], [plane_of(pack(1, 0), "f0")]
    attn_w, ffn_w, far_f = [(w_q0, w_o0)], [], []
    for i in range(layers):
        if i > 0:
            planes_a.append(plane_of(pack(0, i), "a" + str(i), ffn_w[i - 1 :]))
            full = full_of(planes_a[i], "a" + str(i), False)[0]
            attn_w.append((full, full))
            planes_f.append(plane_of(pack(1, i), "f" + str(i), [full]))
        w, far = full_of(planes_f[i], "f" + str(i))
        ffn_w.append(w)
        far_f.append(far)
    grad_blocks = [blocks_of(chain_rows(grad_own, i)) for i in range(CHAINS)]

    band_index = z * team_rows - BLK + jnp.arange(team_rows + 2 * BLK, dtype=jnp.int32)
    inside = (band_index >= 0) & (band_index < cu_seqlens[0, -1])
    docs = jnp.sum((band_index[None, :, None] >= cu_seqlens[:, None, 1:-1]).astype(jnp.int32), axis=2)
    docs = jnp.where(inside[None], docs, -1)
    block = jnp.arange(LOCAL, dtype=jnp.int32)
    true_block = ((block % TEAM) ^ t) * 2 + ((block // TEAM) ^ c)
    index = z * team_rows + true_block[:, None] * sub + jnp.arange(sub, dtype=jnp.int32)[None]
    begin = jnp.max(
        jnp.where(
            index[:, None, :, None] >= cu_seqlens[None, :, None, :-1], cu_seqlens[None, :, None, :-1], 0
        ),
        axis=3,
    )
    offsets = (index[:, None] - begin).astype(F32)
    lane = jnp.arange(hc, dtype=jnp.int32) % HD
    sign = jnp.where(lane < HD // 2, -1.0, 1.0)

    state = []
    for i in range(CHAINS):
        mbs = slice(i * n, (i + 1) * n)
        tables = []
        for layer in range(layers):
            base = 10000.0 if layer % 2 == 0 else 160000.0
            inv = base ** (-((lane % (HD // 2)).astype(F32) * 2.0 / HD))
            ang = offsets[:, mbs].reshape(rows, 1) * inv
            tables.append((jnp.cos(ang), jnp.sin(ang) * sign))
        state.append(
            {
                "tables": tables,
                "col": docs[mbs, :, None],
                "row": [docs[mbs, None, BLK - HALF :], docs[mbs, None, :]],
                "x": chain_rows(tok_own, i),
                "blocks": tok_blocks[i],
                "saved": [],
            }
        )

    partial_out = [out((rows // 2, feat), BF)] * 2
    band = pltpu.VMEM((team_rows + 2 * BLK, hc), BF)
    band32 = pltpu.VMEM((team_rows + 2 * BLK, hc), F32)

    def fold(parts, name, after=()):
        got = hop_core(parts[1])
        h = call(
            "fold_" + name, fold_body, ids, [parts[0], got],
            [out((own, feat), F32)] + [out((own, feat), BF)] * (TEAM - 1), after=after,
        )
        return [h[0]] + [hop_team(h[k], k) for k in range(1, TEAM)]

    def forward_attn(st, layer):
        windowed = layer % 2 == 0
        w3, wo = attn_w[layer]
        cos, sin = st["tables"][layer]
        a, qkv, lo, hi = call(
            "qkv", qkv_body(layer, layer == 0, n, sub), ids, st["blocks"] + [gains, w3, cos, sin],
            [out((rows, feat), BF), out((rows, 3 * hc), BF)] + [out((n * BLK, 2 * hc), BF)] * 2,
            flops=2 * rows * feat * 3 * hc, after=[planes_f[0]] if layer == 0 else [],
        )
        lo, hi = step_z(lo, 1), step_z(hi, -1)
        ctx, *parts = call(
            "attn", attn_body(windowed, n, sub), ids, [qkv, lo, hi, st["col"], st["row"][layer % 2], wo],
            [out((rows, hc), BF)] + partial_out, [band] * 2, flops=4 * rows * feat * hc,
            after=[far_f[layer]] if layer > 0 else [],
        )
        terms = fold(parts, "attn")
        mid, b = call(
            "mid", resid_body(layers + layer), ids, [st["x"]] + terms + [gains],
            [out((own, feat), F32), out((own, feat), BF)],
        )
        st["saved"].append([st["x"], a, qkv, lo, hi, ctx, mid])
        st["x"] = mid
        st["blocks"] = blocks_of(b)

    def forward_mlp(st, layer):
        b, gu, hid, *parts = call(
            "mlp", mlp_body, ids, st["blocks"] + [ffn_w[layer]],
            [out((rows, feat), BF), out((rows, 2 * units), F32), out((rows, units), BF)] + partial_out,
            flops=6 * rows * feat * units,
        )
        st["saved"][layer] += [b, gu, hid]
        terms = fold(parts, "mlp")
        if layer + 1 < layers:
            st["x"], a = call(
                "next", resid_body(layer + 1), ids, [st["x"]] + terms + [gains],
                [out((own, feat), F32), out((own, feat), BF)],
                after=[attn_w[layer + 1][0], planes_f[layer + 1]],
            )
            st["blocks"] = blocks_of(a)
        else:
            st["x"] = call("last", resid_body(None), ids, [st["x"]] + terms, [out((own, feat), BF)])[0]

    for layer in range(layers):
        for st in state:
            forward_attn(st, layer)
        for st in state:
            forward_mlp(st, layer)

    def join(parts, dtype):
        x = parts[0] if CHAINS == 1 else jnp.concatenate(parts, axis=0)
        return call("join", join_body, ids, [x, hop_core(x)], [out((micro, chip_rows, feat), dtype)])[0]

    hidden_out = join([st["x"] for st in state], BF)

    for i, st in enumerate(state):
        st["dy"] = chain_rows(grad_own, i)
        st["blocks"] = grad_blocks[i]

    def weight_pieces(ins, width, name):
        return call(
            "wgrad_" + name, weight_grad_body, ids, ins, [out((TEAM * d_rows, width), BF)] * nz,
            [pltpu.VMEM((nz * TEAM * d_rows, width), BF)], flops=2 * rows * CHAINS * feat * width,
        )

    def relay(pieces, name):
        if nz != 4:
            return [pieces[0]] + [hop_z(pieces[s], s) for s in range(1, nz)]
        near = hop_z(pieces[1], 1)
        far = call("relay_" + name, add_body, ids, [pieces[2], hop_z(pieces[3], 1)], [out(pieces[2].shape, BF)])[0]
        return [pieces[0], near, hop_z(far, 2)]

    def z_sum(got, name):
        width = got[0].shape[1]
        mine = call(
            "zsum_" + name, plane_sum_body, ids, got,
            [out((d_rows, width), F32)] + [out((d_rows, width), BF)] * (TEAM - 1),
            [pltpu.VMEM((TEAM * d_rows, width), F32)],
        )
        return [mine[0]] + [hop_team(mine[k], k) for k in range(1, TEAM)]

    gain_rows = [None] * (2 * layers)

    def add_gain(row, dg):
        gain_rows[row] = dg if gain_rows[row] is None else gain_rows[row] + dg

    attn_parts, ffn_parts = [None] * layers, [None] * layers
    st = state[0]
    wait_mlp, wait_fold, wait_mid, wait_attn = [], [], [], []
    for layer in reversed(range(layers)):
        w3, wo = attn_w[layer]
        cos, sin = st["tables"][layer]
        x_in, a, qkv, lo, hi, ctx, mid, b, gu, hid = st["saved"][layer]
        dy, dgu, *parts = call(
            "mlp_back", mlp_back_body, ids, st["blocks"] + [gu, ffn_w[layer]],
            [out((rows, feat), BF), out((rows, 2 * units), BF)] + partial_out,
            flops=6 * rows * feat * units, after=wait_mlp,
        )
        terms = fold(parts, "mlp_back", wait_fold)
        pieces = weight_pieces([b, dgu, dy, hid], fw, "f" + str(layer))
        dg, dmid, dmb = call(
            "mid_back", norm_back_body(layers + layer), ids, terms + [mid, st["dy"], gains],
            [out((1, feat), F32), out((own, feat), F32), out((own, feat), BF)],
            after=pieces + wait_mid,
        )
        add_gain(layers + layer, dg)
        relayed = relay(pieces, "f" + str(layer))
        dm, dq, dkv, dlo, dhi = call(
            "attn_back", attn_back_body(layer % 2 == 0, n, sub), ids,
            blocks_of(dmb) + [qkv, lo, hi, st["col"], st["row"][layer % 2], wo, cos, sin],
            [out((rows, feat), BF), out((rows, hc), BF), out((rows, 2 * hc), F32)]
            + [out((n * BLK, 2 * hc), BF)] * 2,
            [band] * 2 + [pltpu.VMEM((rows, hc), BF), pltpu.VMEM((rows, hc), F32)] + [band32] * 2,
            flops=6 * rows * feat * hc,
        )
        from_next, from_prev = step_z(dlo, -1), step_z(dhi, 1)
        ffn_parts[layer] = z_sum(relayed, "f" + str(layer))
        dqkv, *parts = call(
            "qkv_back", qkv_back_body(n, sub), ids, [dq, dkv, from_next, from_prev, w3, cos, sin],
            [out((rows, 3 * hc), BF)] + partial_out, [pltpu.VMEM((rows, 2 * hc), F32)],
            flops=6 * rows * feat * hc,
            after=ffn_parts[layer][:1] + wait_attn + ([st["x"]] if layer + 1 == layers else []),
        )
        pieces = weight_pieces([a, dqkv, dm, ctx], aw, "a" + str(layer))
        terms = fold(parts, "qkv_back", pieces if layer == 0 else [])
        if layer == 0:
            got = [pieces[0]] + [hop_z(pieces[s], s) for s in range(1, nz)]
            pieces = got
        low = [out((own, feat), BF)] if layer > 0 else []
        dg, st["dy"], *dyb = call(
            "in_back", norm_back_body(layer), ids, terms + [x_in, dmid, gains],
            [out((1, feat), F32), out((own, feat), F32)] + low, after=pieces,
        )
        add_gain(layer, dg)
        if layer > 0:
            st["blocks"] = blocks_of(dyb[0])
            relayed = relay(pieces, "a" + str(layer))
            attn_parts[layer] = z_sum(relayed, "a" + str(layer))
            wait_mlp = relayed[1:2]
            wait_fold = ffn_parts[layer]
            wait_mid = attn_parts[layer][:1]
            wait_attn = attn_parts[layer]
        else:
            attn_parts[layer] = z_sum(got, "a" + str(layer))

    input_grad = join([st["dy"] for st in state], F32)

    dgain = jnp.concatenate(gain_rows + gain_rows, axis=0)[: 4 * layers]
    dgain = dgain + hop_core(dgain)
    dgain = sum([dgain] + [hop_team(dgain, k) for k in range(1, TEAM)])
    dgain = sum([dgain] + [hop_z(dgain, s) for s in range(1, nz)])
    dgain = lax.dynamic_slice_in_dim(dgain, (z * TEAM + t) * d_rows, d_rows, axis=1)

    g_qkv, g_out, g_in, g_down = call(
        "finish", finish_body, ids, sum(attn_parts, []) + sum(ffn_parts, []),
        [out(w_qkv.shape, F32), out(w_attn_out.shape, F32), out(w_ffn_in.shape, F32), out(w_ffn_out.shape, F32)],
        [pltpu.VMEM((d_rows, TEAM * units), F32)],
    )
    return (
        hidden_out,
        input_grad,
        dgain[:layers],
        dgain[layers : 2 * layers],
        g_qkv,
        g_out,
        g_in,
        g_down,
    )


def solution(mesh):
    dp, tensor = mesh.devices.shape
    fine = Mesh(mesh.devices.reshape(dp // TEAM, 2, 2, tensor), ("z", "y", "x", "c"))
    rows = ("z", "y", "x")
    in_specs = (
        P(None, rows, None),
        P(),
        P(None, rows),
        P(None, rows),
        P(None, None, rows, "c"),
        P(None, rows, "c"),
        P(None, None, rows, "c"),
        P(None, rows, "c"),
        P(None, rows, None),
    )
    out_specs = (
        P(None, rows, None),
        P(None, rows, None),
        P(None, rows),
        P(None, rows),
        P(None, None, rows, "c"),
        P(None, rows, "c"),
        P(None, None, rows, "c"),
        P(None, rows, "c"),
    )
    return jax.shard_map(shards, mesh=fine, in_specs=in_specs, out_specs=out_specs, check_vma=False)
```

```python
import jax
import jax.numpy as jnp
from jax import lax
from jax.experimental import pallas as pl
from jax.experimental.pallas import tpu as pltpu
from jax.sharding import Mesh
from jax.sharding import PartitionSpec as P

HD = 64
HALF = 64
BLK = 128
TEAM = 4
LOCAL = 2 * TEAM
MASKED = -1e30
BF = jnp.bfloat16
F32 = jnp.float32
CHAINS = 1


def mm(a, b, ca, cb):
    return lax.dot_general(a, b, (((ca,), (cb,)), ((), ())), preferred_element_type=F32)


def hop_team(x, k):
    return lax.ppermute(x, ("y", "x"), [(i, i ^ k) for i in range(TEAM)])


def hop_core(x):
    return lax.ppermute(x, "c", [(0, 1), (1, 0)])


def hop_z(x, s):
    n = lax.axis_size("z")
    return lax.ppermute(x, "z", [(i, i ^ s if n == 4 else (i + s) % n) for i in range(n)])


def step_z(x, by):
    n = lax.axis_size("z")
    return lax.ppermute(x, "z", [(i, i + by) for i in range(n) if 0 <= i + by < n])


def out(shape, dtype):
    return jax.ShapeDtypeStruct(shape, dtype)


def call(name, body, ids, ins, outs, scratch=(), flops=0, after=()):
    ins, after = list(ins), list(after)

    def kernel(*refs):
        n_in, n_out = len(ins), len(outs)
        rest = refs[1 + n_in + len(after) :]
        body(refs[0], refs[1 : 1 + n_in], rest[:n_out], rest[n_out:])

    moved = sum(a.size * a.dtype.itemsize for a in ins) + sum(
        o.size * jnp.dtype(o.dtype).itemsize for o in outs
    )
    vmem = pl.BlockSpec(memory_space=pltpu.VMEM)
    results = pl.pallas_call(
        kernel,
        name=name,
        in_specs=[pl.BlockSpec(memory_space=pltpu.SMEM)] + [vmem] * len(ins)
        + [pl.BlockSpec(memory_space=pl.ANY)] * len(after),
        out_specs=[vmem] * len(outs),
        out_shape=list(outs),
        scratch_shapes=list(scratch),
        compiler_params=pltpu.CompilerParams(vmem_limit_bytes=12 * 1024 * 1024),
        cost_estimate=pl.CostEstimate(flops=flops, bytes_accessed=moved, transcendentals=0),
    )(ids, *ins, *after)
    return list(results)


def aligned(start, size):
    return pl.ds(pl.multiple_of(start, size), size)


def norm_parts(v):
    cent = v - jnp.mean(v, axis=-1, keepdims=True)
    rstd = lax.rsqrt(jnp.mean(cent * cent, axis=-1, keepdims=True) + 1e-05)
    return cent * rstd, rstd


def gelu_parts(gate):
    cdf = 0.5 * (1.0 + lax.erf(gate * 0.7071067811865476))
    return gate * cdf, cdf + gate * jnp.exp(-0.5 * gate * gate) * 0.3989422804014327


def swap_halves(v):
    width = v.shape[-1]
    lane = lax.broadcasted_iota(jnp.int32, v.shape, 1) % HD
    return jnp.where(
        lane < HD // 2, pltpu.roll(v, width - HD // 2, 1), pltpu.roll(v, HD // 2, 1)
    )


def true_rows(ids, n, sub, mb, b):
    blk = (ids[2] ^ (b % 2)) * TEAM + (ids[1] ^ (b // 2))
    return aligned((blk * n + mb) * sub, sub)


def tiles_of(refs, tile):
    rows = refs[0].shape[0]
    per = max(1, tile // rows)
    for first in range(0, len(refs), per):
        group = [r[...] for r in refs[first : first + per]]
        yield slice(first * rows, (first + per) * rows), (
            group[0] if per == 1 else jnp.concatenate(group, axis=0)
        )


def store_partial(p_refs, where, value):
    half = p_refs[0].shape[0]
    which = where.start // half
    p_refs[which][where.start - which * half : where.stop - which * half, :] = value.astype(BF)


def start_attn_body(ids, ins, outs, scratch):
    w_qkv, w_out = ins
    layers, hc = w_qkv.shape[0], w_qkv.shape[3] // TEAM
    for layer in range(layers):
        for k in range(TEAM):
            cols = aligned((ids[1] ^ k) * hc, hc)
            if layer == 0:
                dst, rest, at = outs[k], outs[TEAM + k], 0
            else:
                dst = rest = outs[(layer + 1) * TEAM + k]
                at = 3 * hc
            for i in range(3):
                dst[:, i * hc : (i + 1) * hc] = w_qkv[layer, i, :, cols]
            rest[:, at : at + hc] = w_out[layer, :, cols]


def start_body(ids, ins, outs, scratch):
    tokens, grads, w_in, w_down, owned = ins
    t, c = ids[1], ids[2]
    n, half = tokens.shape[0], tokens.shape[1] // 2
    for src, dst in ((tokens, outs[0]), (grads, outs[1])):
        for mb in range(n):
            dst[mb * half : (mb + 1) * half] = src[mb, aligned(c * half, half)]
    spot = lax.broadcasted_iota(jnp.int32, owned.shape, 1) // w_in.shape[2] == ids[0] * TEAM + t
    outs[2][...] = jnp.where(spot, owned[...], 0.0)
    packs = outs[3:]
    real, units = w_in.shape[3], scratch[0].shape[1] // TEAM
    scratch[0][...] = jnp.zeros(scratch[0].shape, BF)
    for layer in range(w_in.shape[0]):
        for i in range(3):
            scratch[0][:, :real] = w_down[layer] if i == 2 else w_in[layer, i]
            for k in range(TEAM):
                cols = pl.ds(pl.multiple_of((t ^ k) * units, 128), units)
                packs[layer * TEAM + k][:, i * units : (i + 1) * units] = scratch[0][:, cols]


def plane_body(ids, ins, outs, scratch):
    rows = ins[0].shape[0]
    for k in range(TEAM):
        outs[0][aligned((ids[1] ^ k) * rows, rows)] = ins[k][...]


def full_body(ids, ins, outs, scratch):
    rows, nz = ins[0].shape[0], len(ins)
    for s in range(nz):
        src = ids[0] ^ s if nz == 4 else lax.rem(ids[0] - s + nz, nz)
        outs[0][aligned(src * rows, rows)] = ins[s][...]


def add_body(ids, ins, outs, scratch):
    outs[0][...] = total_of(ins).astype(BF)


def qkv_body(row, raw, n, sub):
    def body(ids, ins, outs, scratch):
        blocks, (gains, w, cos, sin) = ins[:LOCAL], ins[LOCAL:]
        a_ref, qkv_ref, lo_ref, hi_ref = outs
        hc = cos.shape[1]
        for where, tile in tiles_of(blocks, 256):
            if raw:
                tile = (norm_parts(tile.astype(F32))[0] * gains[row : row + 1]).astype(BF)
            a_ref[where] = tile
            r = mm(tile, w[:, : 3 * hc], 1, 0)
            cs, sn = cos[where], sin[where]
            q, k = r[:, :hc], r[:, hc : 2 * hc]
            qkv_ref[where, :hc] = (q * cs + swap_halves(q) * sn).astype(BF)
            qkv_ref[where, hc : 2 * hc] = (k * cs + swap_halves(k) * sn).astype(BF)
            qkv_ref[where, 2 * hc :] = r[:, 2 * hc :].astype(BF)
        per = BLK // sub
        for mb in range(n):
            for i in range(per):
                dst = slice(mb * BLK + i * sub, mb * BLK + (i + 1) * sub)
                lo_ref[dst] = qkv_ref[true_rows(ids, n, sub, mb, LOCAL - per + i), hc:]
                hi_ref[dst] = qkv_ref[true_rows(ids, n, sub, mb, i), hc:]

    return body


def fill_band(ids, mb, n, sub, qkv, lo, hi, kb, vb):
    hc = kb.shape[1]
    edge = slice(mb * BLK, (mb + 1) * BLK)
    last = BLK + LOCAL * sub
    kb[:BLK], vb[:BLK] = lo[edge, :hc], lo[edge, hc:]
    kb[last:], vb[last:] = hi[edge, :hc], hi[edge, hc:]
    for b in range(LOCAL):
        src = true_rows(ids, n, sub, mb, b)
        dst = slice(BLK + b * sub, BLK + (b + 1) * sub)
        kb[dst] = qkv[src, hc : 2 * hc]
        vb[dst] = qkv[src, 2 * hc :]


def keys_of(i, windowed):
    return slice(i * BLK + BLK - HALF, (i + 2) * BLK + HALF) if windowed else slice(i * BLK, (i + 3) * BLK)


def allowed_of(mb, i, col, row, windowed):
    keys = keys_of(0, windowed)
    width = keys.stop - keys.start
    ok = col[mb, BLK + i * BLK : 2 * BLK + i * BLK, :] == row[mb, :, i * BLK : i * BLK + width]
    if windowed:
        shape = (BLK, width)
        gap = lax.broadcasted_iota(jnp.int32, shape, 1) - lax.broadcasted_iota(jnp.int32, shape, 0)
        ok = ok & (gap <= 2 * HALF) & (gap >= 0)
    return ok


def take(ids, ref, n, sub, mb, i, lanes):
    per = BLK // sub
    return jnp.concatenate(
        [ref[true_rows(ids, n, sub, mb, per * i + e), lanes] for e in range(per)], axis=0
    )


def put(ids, ref, n, sub, mb, i, lanes, value):
    for e in range(BLK // sub):
        per = BLK // sub
        ref[true_rows(ids, n, sub, mb, per * i + e), lanes] = value[e * sub : (e + 1) * sub]


def probs_of(qh, k, ok):
    s = jnp.where(ok, mm(qh, k, 1, 1), MASKED)
    e = jnp.exp(s - jnp.max(s, axis=1, keepdims=True))
    return e * (1.0 / jnp.sum(e, axis=1, keepdims=True))


def attn_body(windowed, n, sub):
    def body(ids, ins, outs, scratch):
        qkv, lo, hi, col, row, w = ins
        ctx_ref = outs[0]
        kb, vb = scratch
        hc = kb.shape[1]
        head_of = lax.broadcasted_iota(jnp.int32, (BLK, hc), 1) // HD
        for mb in range(n):
            fill_band(ids, mb, n, sub, qkv, lo, hi, kb, vb)
            for i in range(LOCAL * sub // BLK):
                ok = allowed_of(mb, i, col, row, windowed)
                q = take(ids, qkv, n, sub, mb, i, slice(0, hc)) * jnp.asarray(0.125, BF)
                band = keys_of(i, windowed)
                k, v = kb[band], vb[band]
                ctx = jnp.zeros((BLK, hc), F32)
                for h in range(hc // HD):
                    qh = jnp.where(head_of == h, q, jnp.zeros_like(q))
                    p = probs_of(qh, k, ok).astype(BF)
                    ctx = jnp.where(head_of == h, mm(p, v, 1, 0), ctx)
                put(ids, ctx_ref, n, sub, mb, i, slice(0, hc), ctx.astype(BF))
        total = ctx_ref.shape[0]
        for first in range(0, total, 256):
            where = slice(first, first + 256)
            store_partial(outs[1:], where, mm(ctx_ref[where], w[:, w.shape[1] - hc :], 1, 1))

    return body


def fold_body(ids, ins, outs, scratch):
    rows = outs[0].shape[0]
    for k in range(TEAM):
        where = slice(k * rows, (k + 1) * rows)
        both = ins[0][where].astype(F32) + ins[1][where].astype(F32)
        outs[k][...] = both.astype(outs[k].dtype)


def total_of(refs):
    value = refs[0][...].astype(F32)
    for r in refs[1:]:
        value = value + r[...].astype(F32)
    return value


def resid_body(row):
    def body(ids, ins, outs, scratch):
        x = ins[0][...].astype(F32) + total_of(ins[1 : 1 + TEAM])
        if row is None:
            outs[0][...] = x.astype(BF)
        else:
            outs[0][...] = x
            outs[1][...] = (norm_parts(x)[0] * ins[-1][row : row + 1]).astype(BF)

    return body


def mlp_body(ids, ins, outs, scratch):
    blocks, w = ins[:LOCAL], ins[LOCAL]
    b_ref, gu_ref, hid_ref = outs[:3]
    units = w.shape[1] // 3
    for where, tile in tiles_of(blocks, 256):
        b_ref[where] = tile
        gu = mm(tile, w[:, : 2 * units], 1, 0)
        gu_ref[where] = gu
        hid = (gelu_parts(gu[:, :units])[0] * gu[:, units:]).astype(BF)
        hid_ref[where] = hid
        store_partial(outs[3:], where, mm(hid, w[:, 2 * units :], 1, 1))


def mlp_back_body(ids, ins, outs, scratch):
    blocks, (gu_ref, w) = ins[:LOCAL], ins[LOCAL:]
    dy_ref, dgu_ref = outs[:2]
    units = w.shape[1] // 3
    for where, tile in tiles_of(blocks, 256):
        dy_ref[where] = tile
        dhid = mm(tile, w[:, 2 * units :], 1, 0)
        act, slope = gelu_parts(gu_ref[where, :units])
        dgu_ref[where, :units] = (dhid * gu_ref[where, units:] * slope).astype(BF)
        dgu_ref[where, units:] = (dhid * act).astype(BF)
        store_partial(outs[2:], where, mm(dgu_ref[where], w[:, : 2 * units], 1, 1))


def norm_back_body(row):
    def body(ids, ins, outs, scratch):
        dout = total_of(ins[:TEAM])
        v, dy, gains = ins[TEAM:]
        xhat, rstd = norm_parts(v[...].astype(F32))
        outs[0][...] = jnp.sum(dout * xhat, axis=0, keepdims=True)
        dx = dout * gains[row : row + 1]
        m1 = jnp.mean(dx, axis=-1, keepdims=True)
        m2 = jnp.mean(dx * xhat, axis=-1, keepdims=True)
        dv = dy[...].astype(F32) + rstd * (dx - m1 - xhat * m2)
        outs[1][...] = dv
        if len(outs) > 2:
            outs[2][...] = dv.astype(BF)

    return body


def attn_back_body(windowed, n, sub):
    def body(ids, ins, outs, scratch):
        blocks, (qkv, lo, hi, col, row, w, cos, sin) = ins[:LOCAL], ins[LOCAL:]
        dm_ref, dq_ref, dkv_ref, dlo_ref, dhi_ref = outs
        kb, vb, dctx, dqs, dkb, dvb = scratch
        hc = kb.shape[1]
        for where, tile in tiles_of(blocks, 256):
            dm_ref[where] = tile
            dctx[where] = mm(tile, w[:, w.shape[1] - hc :], 1, 0).astype(BF)
        head_of = lax.broadcasted_iota(jnp.int32, (BLK, hc), 1) // HD
        last = BLK + LOCAL * sub
        for mb in range(n):
            fill_band(ids, mb, n, sub, qkv, lo, hi, kb, vb)
            dkb[...] = jnp.zeros(dkb.shape, F32)
            dvb[...] = jnp.zeros(dvb.shape, F32)
            for i in range(LOCAL * sub // BLK):
                ok = allowed_of(mb, i, col, row, windowed)
                q = take(ids, qkv, n, sub, mb, i, slice(0, hc)) * jnp.asarray(0.125, BF)
                do = take(ids, dctx, n, sub, mb, i, slice(0, hc))
                band = keys_of(i, windowed)
                k, v = kb[band], vb[band]
                dq = jnp.zeros((BLK, hc), F32)
                dk = dkb[band]
                dv = dvb[band]
                for h in range(hc // HD):
                    mine = head_of == h
                    qh = jnp.where(mine, q, jnp.zeros_like(q))
                    doh = jnp.where(mine, do, jnp.zeros_like(do))
                    p = probs_of(qh, k, ok)
                    dp = mm(doh, v, 1, 1)
                    ds = (p * (dp - jnp.sum(p * dp, axis=1, keepdims=True))).astype(BF)
                    dq = jnp.where(mine, mm(ds, k, 1, 0), dq)
                    dk = dk + mm(ds, qh, 0, 0)
                    dv = dv + mm(p.astype(BF), doh, 0, 0)
                put(ids, dqs, n, sub, mb, i, slice(0, hc), 0.125 * dq)
                dkb[band] = dk
                dvb[band] = dv
            edge = slice(mb * BLK, (mb + 1) * BLK)
            dlo_ref[edge, :hc] = dkb[:BLK].astype(BF)
            dlo_ref[edge, hc:] = dvb[:BLK].astype(BF)
            dhi_ref[edge, :hc] = dkb[last:].astype(BF)
            dhi_ref[edge, hc:] = dvb[last:].astype(BF)
            for b in range(LOCAL):
                src = slice(BLK + b * sub, BLK + (b + 1) * sub)
                dst = true_rows(ids, n, sub, mb, b)
                dkv_ref[dst, :hc] = dkb[src]
                dkv_ref[dst, hc:] = dvb[src]
        for first in range(0, dqs.shape[0], 256):
            where = slice(first, first + 256)
            g = dqs[where]
            dq_ref[where] = (g * cos[where] + swap_halves(g * sin[where])).astype(BF)

    return body


def qkv_back_body(n, sub):
    def body(ids, ins, outs, scratch):
        dq, dkv, from_next, from_prev, w, cos, sin = ins
        dqkv_ref = outs[0]
        acc = scratch[0]
        hc = cos.shape[1]
        acc[...] = dkv[...]
        per = BLK // sub
        for mb in range(n):
            for i in range(per):
                src = slice(mb * BLK + i * sub, mb * BLK + (i + 1) * sub)
                first = true_rows(ids, n, sub, mb, i)
                acc[first] = acc[first] + from_prev[src].astype(F32)
                end = true_rows(ids, n, sub, mb, LOCAL - per + i)
                acc[end] = acc[end] + from_next[src].astype(F32)
        for first in range(0, acc.shape[0], 256):
            where = slice(first, first + 256)
            g = acc[where, :hc]
            dqkv_ref[where, :hc] = dq[where]
            dqkv_ref[where, hc : 2 * hc] = (g * cos[where] + swap_halves(g * sin[where])).astype(BF)
            dqkv_ref[where, 2 * hc :] = acc[where, hc:].astype(BF)
            store_partial(outs[1:], where, mm(dqkv_ref[where], w[:, : 3 * hc], 1, 1))

    return body


def weight_grad_body(ids, ins, outs, scratch):
    full = scratch[0]
    chains = [ins[i : i + 4] for i in range(0, len(ins), 4)]
    cut = chains[0][1].shape[1]
    step = 256
    for first in range(0, full.shape[0], step):
        where = slice(first, first + step)
        full[where, :cut] = sum(mm(c[0][:, where], c[1][...], 0, 0) for c in chains).astype(BF)
        full[where, cut:] = sum(mm(c[2][:, where], c[3][...], 0, 0) for c in chains).astype(BF)
    nz = len(outs)
    span = outs[0].shape[0]
    for s in range(nz):
        dst = ids[0] ^ s if nz == 4 else lax.rem(ids[0] + s, nz)
        outs[s][...] = full[aligned(dst * span, span)]


def plane_sum_body(ids, ins, outs, scratch):
    scratch[0][...] = total_of(ins)
    rows = outs[0].shape[0]
    for k in range(TEAM):
        outs[k][...] = scratch[0][aligned((ids[1] ^ k) * rows, rows)].astype(outs[k].dtype)


def finish_body(ids, ins, outs, scratch):
    g_qkv, g_out, g_in, g_down = outs
    wide = scratch[0]
    layers, hc = g_qkv.shape[0], g_qkv.shape[3] // TEAM
    real, units = g_down.shape[2], wide.shape[1] // TEAM
    for layer in range(layers):
        attn = ins[layer * TEAM : (layer + 1) * TEAM]
        ffn = ins[(layers + layer) * TEAM : (layers + layer + 1) * TEAM]
        for k in range(TEAM):
            cols = aligned((ids[1] ^ k) * hc, hc)
            for i in range(3):
                g_qkv[layer, i, :, cols] = attn[k][:, i * hc : (i + 1) * hc].astype(F32)
            g_out[layer, :, cols] = attn[k][:, 3 * hc :].astype(F32)
        for i in range(3):
            for k in range(TEAM):
                cols = pl.ds(pl.multiple_of((ids[1] ^ k) * units, 128), units)
                wide[:, cols] = ffn[k][:, i * units : (i + 1) * units].astype(F32)
            if i == 2:
                g_down[layer] = wide[:, :real]
            else:
                g_in[layer, i] = wide[:, :real]


def join_body(ids, ins, outs, scratch):
    n, half = outs[0].shape[0], outs[0].shape[1] // 2
    c = ids[2]
    for mb in range(n):
        rows = slice(mb * half, (mb + 1) * half)
        outs[0][mb, aligned(c * half, half)] = ins[0][rows]
        outs[0][mb, aligned((1 - c) * half, half)] = ins[1][rows]


def shards(tokens, cu_seqlens, attn_gain, mlp_gain, w_qkv, w_attn_out, w_ffn_in, w_ffn_out, out_grad):
    nz = lax.axis_size("z")
    z = lax.axis_index("z")
    t = lax.axis_index("y") * 2 + lax.axis_index("x")
    c = lax.axis_index("c")
    ids = jnp.stack([z, t, c]).astype(jnp.int32)
    micro, chip_rows, feat = tokens.shape
    layers, d_rows = w_qkv.shape[0], w_qkv.shape[2]
    hc = w_qkv.shape[3] // TEAM
    sub = chip_rows // 2
    real = w_ffn_in.shape[3]
    units = -(-real // (TEAM * 128)) * 128
    team_rows = TEAM * chip_rows
    per_chain = micro // CHAINS
    n = per_chain
    own = n * sub
    rows = LOCAL * own
    aw, fw = 4 * hc, 3 * units

    owned = jnp.concatenate([attn_gain, mlp_gain, attn_gain, mlp_gain], axis=0)[: 4 * layers]
    owned = jnp.tile(owned.astype(F32), (1, feat // d_rows))
    packs_a = call(
        "start_attn", start_attn_body, ids, [w_qkv, w_attn_out],
        [out((d_rows, 3 * hc), BF)] * TEAM
        + [out((d_rows, hc), BF)] * TEAM
        + [out((d_rows, aw), BF)] * ((layers - 1) * TEAM),
    )

    def plane_of(pieces, name, after=()):
        width = pieces[0].shape[1]
        got = [pieces[0]] + [hop_team(pieces[k], k) for k in range(1, TEAM)]
        return call("plane_" + name, plane_body, ids, got, [out((TEAM * d_rows, width), BF)], after=after)[0]

    plane_qkv = plane_of(packs_a[:TEAM], "q0")
    tok_own, grad_own, gains, *packs_f = call(
        "start", start_body, ids, [tokens, out_grad, w_ffn_in, w_ffn_out, owned],
        [out((micro * sub, feat), BF)] * 2
        + [out((4 * layers, feat), F32)]
        + [out((d_rows, fw), BF)] * (layers * TEAM),
        [pltpu.VMEM((d_rows, TEAM * units), BF)], after=[plane_qkv],
    )
    plane_out = plane_of(packs_a[TEAM : 2 * TEAM], "o0")

    def blocks_of(x):
        mine = [x] + [hop_team(x, k) for k in range(1, TEAM)]
        return mine + [hop_core(b) for b in mine]

    def chain_rows(x, i):
        return x[i * own : (i + 1) * own]

    tok_blocks = [blocks_of(chain_rows(tok_own, i)) for i in range(CHAINS)]

    def full_of(plane, name, relay=True):
        width = plane.shape[1]
        if nz == 4 and relay:
            far = hop_z(plane, 2)
            planes = [plane, hop_z(plane, 1), far, hop_z(far, 1)]
        else:
            far = plane
            planes = [plane] + [hop_z(plane, s) for s in range(1, nz)]
        full = call("full_" + name, full_body, ids, planes, [out((nz * TEAM * d_rows, width), BF)])[0]
        return full, far

    gains = sum([gains] + [hop_team(gains, k) for k in range(1, TEAM)])
    gains = sum([gains] + [hop_z(gains, s) for s in range(1, nz)])

    def pack(kind, layer):
        if kind == 0:
            return packs_a[(layer + 1) * TEAM : (layer + 2) * TEAM]
        return packs_f[layer * TEAM : (layer + 1) * TEAM]

    w_q0 = full_of(plane_qkv, "q0", False)[0]
    w_o0 = full_of(plane_out, "o0", False)[0]
    planes_a, planes_f = [plane_out], [plane_of(pack(1, 0), "f0")]
    attn_w, ffn_w, far_f = [(w_q0, w_o0)], [], []
    for i in range(layers):
        if i > 0:
            planes_a.append(plane_of(pack(0, i), "a" + str(i), ffn_w[i - 1 :]))
            full = full_of(planes_a[i], "a" + str(i), False)[0]
            attn_w.append((full, full))
            planes_f.append(plane_of(pack(1, i), "f" + str(i), [full]))
        w, far = full_of(planes_f[i], "f" + str(i))
        ffn_w.append(w)
        far_f.append(far)
    grad_blocks = [blocks_of(chain_rows(grad_own, i)) for i in range(CHAINS)]

    band_index = z * team_rows - BLK + jnp.arange(team_rows + 2 * BLK, dtype=jnp.int32)
    inside = (band_index >= 0) & (band_index < cu_seqlens[0, -1])
    docs = jnp.sum((band_index[None, :, None] >= cu_seqlens[:, None, 1:-1]).astype(jnp.int32), axis=2)
    docs = jnp.where(inside[None], docs, -1)
    block = jnp.arange(LOCAL, dtype=jnp.int32)
    true_block = ((block % TEAM) ^ t) * 2 + ((block // TEAM) ^ c)
    index = z * team_rows + true_block[:, None] * sub + jnp.arange(sub, dtype=jnp.int32)[None]
    begin = jnp.max(
        jnp.where(
            index[:, None, :, None] >= cu_seqlens[None, :, None, :-1], cu_seqlens[None, :, None, :-1], 0
        ),
        axis=3,
    )
    offsets = (index[:, None] - begin).astype(F32)
    lane = jnp.arange(hc, dtype=jnp.int32) % HD
    sign = jnp.where(lane < HD // 2, -1.0, 1.0)

    state = []
    for i in range(CHAINS):
        mbs = slice(i * n, (i + 1) * n)
        tables = []
        for layer in range(layers):
            base = 10000.0 if layer % 2 == 0 else 160000.0
            inv = base ** (-((lane % (HD // 2)).astype(F32) * 2.0 / HD))
            ang = offsets[:, mbs].reshape(rows, 1) * inv
            tables.append((jnp.cos(ang), jnp.sin(ang) * sign))
        state.append(
            {
                "tables": tables,
                "col": docs[mbs, :, None],
                "row": [docs[mbs, None, BLK - HALF :], docs[mbs, None, :]],
                "x": chain_rows(tok_own, i),
                "blocks": tok_blocks[i],
                "saved": [],
            }
        )

    partial_out = [out((rows // 2, feat), BF)] * 2
    band = pltpu.VMEM((team_rows + 2 * BLK, hc), BF)
    band32 = pltpu.VMEM((team_rows + 2 * BLK, hc), F32)

    def fold(parts, name, after=()):
        got = hop_core(parts[1])
        h = call(
            "fold_" + name, fold_body, ids, [parts[0], got],
            [out((own, feat), F32)] + [out((own, feat), BF)] * (TEAM - 1), after=after,
        )
        return [h[0]] + [hop_team(h[k], k) for k in range(1, TEAM)]

    def forward_attn(st, layer):
        windowed = layer % 2 == 0
        w3, wo = attn_w[layer]
        cos, sin = st["tables"][layer]
        a, qkv, lo, hi = call(
            "qkv", qkv_body(layer, layer == 0, n, sub), ids, st["blocks"] + [gains, w3, cos, sin],
            [out((rows, feat), BF), out((rows, 3 * hc), BF)] + [out((n * BLK, 2 * hc), BF)] * 2,
            flops=2 * rows * feat * 3 * hc, after=[planes_f[0]] if layer == 0 else [],
        )
        lo, hi = step_z(lo, 1), step_z(hi, -1)
        ctx, *parts = call(
            "attn", attn_body(windowed, n, sub), ids, [qkv, lo, hi, st["col"], st["row"][layer % 2], wo],
            [out((rows, hc), BF)] + partial_out, [band] * 2, flops=4 * rows * feat * hc,
            after=[far_f[layer]] if layer > 0 else [],
        )
        terms = fold(parts, "attn")
        mid, b = call(
            "mid", resid_body(layers + layer), ids, [st["x"]] + terms + [gains],
            [out((own, feat), F32), out((own, feat), BF)],
        )
        st["saved"].append([st["x"], a, qkv, lo, hi, ctx, mid])
        st["x"] = mid
        st["blocks"] = blocks_of(b)

    def forward_mlp(st, layer):
        b, gu, hid, *parts = call(
            "mlp", mlp_body, ids, st["blocks"] + [ffn_w[layer]],
            [out((rows, feat), BF), out((rows, 2 * units), F32), out((rows, units), BF)] + partial_out,
            flops=6 * rows * feat * units,
        )
        st["saved"][layer] += [b, gu, hid]
        terms = fold(parts, "mlp")
        if layer + 1 < layers:
            st["x"], a = call(
                "next", resid_body(layer + 1), ids, [st["x"]] + terms + [gains],
                [out((own, feat), F32), out((own, feat), BF)],
                after=[attn_w[layer + 1][0], planes_f[layer + 1]],
            )
            st["blocks"] = blocks_of(a)
        else:
            st["x"] = call("last", resid_body(None), ids, [st["x"]] + terms, [out((own, feat), BF)])[0]

    for layer in range(layers):
        for st in state:
            forward_attn(st, layer)
        for st in state:
            forward_mlp(st, layer)

    def join(parts, dtype):
        x = parts[0] if CHAINS == 1 else jnp.concatenate(parts, axis=0)
        return call("join", join_body, ids, [x, hop_core(x)], [out((micro, chip_rows, feat), dtype)])[0]

    hidden_out = join([st["x"] for st in state], BF)

    for i, st in enumerate(state):
        st["dy"] = chain_rows(grad_own, i)
        st["blocks"] = grad_blocks[i]

    def weight_pieces(ins, width, name):
        return call(
            "wgrad_" + name, weight_grad_body, ids, ins, [out((TEAM * d_rows, width), BF)] * nz,
            [pltpu.VMEM((nz * TEAM * d_rows, width), BF)], flops=2 * rows * CHAINS * feat * width,
        )

    def relay(pieces, name):
        if nz != 4:
            return [pieces[0]] + [hop_z(pieces[s], s) for s in range(1, nz)]
        near = hop_z(pieces[1], 1)
        far = call("relay_" + name, add_body, ids, [pieces[2], hop_z(pieces[3], 1)], [out(pieces[2].shape, BF)])[0]
        return [pieces[0], near, hop_z(far, 2)]

    def z_sum(got, name):
        width = got[0].shape[1]
        mine = call(
            "zsum_" + name, plane_sum_body, ids, got,
            [out((d_rows, width), F32)] + [out((d_rows, width), BF)] * (TEAM - 1),
            [pltpu.VMEM((TEAM * d_rows, width), F32)],
        )
        return [mine[0]] + [hop_team(mine[k], k) for k in range(1, TEAM)]

    gain_rows = [None] * (2 * layers)

    def add_gain(row, dg):
        gain_rows[row] = dg if gain_rows[row] is None else gain_rows[row] + dg

    attn_parts, ffn_parts = [None] * layers, [None] * layers
    st = state[0]
    wait_mlp, wait_fold, wait_mid, wait_attn = [], [], [], []
    for layer in reversed(range(layers)):
        w3, wo = attn_w[layer]
        cos, sin = st["tables"][layer]
        x_in, a, qkv, lo, hi, ctx, mid, b, gu, hid = st["saved"][layer]
        dy, dgu, *parts = call(
            "mlp_back", mlp_back_body, ids, st["blocks"] + [gu, ffn_w[layer]],
            [out((rows, feat), BF), out((rows, 2 * units), BF)] + partial_out,
            flops=6 * rows * feat * units, after=wait_mlp,
        )
        terms = fold(parts, "mlp_back", wait_fold)
        pieces = weight_pieces([b, dgu, dy, hid], fw, "f" + str(layer))
        dg, dmid, dmb = call(
            "mid_back", norm_back_body(layers + layer), ids, terms + [mid, st["dy"], gains],
            [out((1, feat), F32), out((own, feat), F32), out((own, feat), BF)],
            after=pieces + wait_mid,
        )
        add_gain(layers + layer, dg)
        relayed = relay(pieces, "f" + str(layer))
        dm, dq, dkv, dlo, dhi = call(
            "attn_back", attn_back_body(layer % 2 == 0, n, sub), ids,
            blocks_of(dmb) + [qkv, lo, hi, st["col"], st["row"][layer % 2], wo, cos, sin],
            [out((rows, feat), BF), out((rows, hc), BF), out((rows, 2 * hc), F32)]
            + [out((n * BLK, 2 * hc), BF)] * 2,
            [band] * 2 + [pltpu.VMEM((rows, hc), BF), pltpu.VMEM((rows, hc), F32)] + [band32] * 2,
            flops=6 * rows * feat * hc,
        )
        from_next, from_prev = step_z(dlo, -1), step_z(dhi, 1)
        ffn_parts[layer] = z_sum(relayed, "f" + str(layer))
        dqkv, *parts = call(
            "qkv_back", qkv_back_body(n, sub), ids, [dq, dkv, from_next, from_prev, w3, cos, sin],
            [out((rows, 3 * hc), BF)] + partial_out, [pltpu.VMEM((rows, 2 * hc), F32)],
            flops=6 * rows * feat * hc,
            after=ffn_parts[layer][:1] + wait_attn + ([st["x"]] if layer + 1 == layers else []),
        )
        pieces = weight_pieces([a, dqkv, dm, ctx], aw, "a" + str(layer))
        terms = fold(parts, "qkv_back", pieces if layer == 0 else [])
        if layer == 0:
            got = [pieces[0]] + [hop_z(pieces[s], s) for s in range(1, nz)]
            pieces = got
        low = [out((own, feat), BF)] if layer > 0 else []
        dg, st["dy"], *dyb = call(
            "in_back", norm_back_body(layer), ids, terms + [x_in, dmid, gains],
            [out((1, feat), F32), out((own, feat), F32)] + low, after=pieces,
        )
        add_gain(layer, dg)
        if layer > 0:
            st["blocks"] = blocks_of(dyb[0])
            relayed = relay(pieces, "a" + str(layer))
            attn_parts[layer] = z_sum(relayed, "a" + str(layer))
            wait_mlp = relayed[1:2]
            wait_fold = ffn_parts[layer]
            wait_mid = attn_parts[layer][:1]
            wait_attn = attn_parts[layer]
        else:
            attn_parts[layer] = z_sum(got, "a" + str(layer))

    input_grad = join([st["dy"] for st in state], F32)

    dgain = jnp.concatenate(gain_rows + gain_rows, axis=0)[: 4 * layers]
    dgain = dgain + hop_core(dgain)
    dgain = sum([dgain] + [hop_team(dgain, k) for k in range(1, TEAM)])
    dgain = sum([dgain] + [hop_z(dgain, s) for s in range(1, nz)])
    dgain = lax.dynamic_slice_in_dim(dgain, (z * TEAM + t) * d_rows, d_rows, axis=1)

    g_qkv, g_out, g_in, g_down = call(
        "finish", finish_body, ids, sum(attn_parts, []) + sum(ffn_parts, []),
        [out(w_qkv.shape, F32), out(w_attn_out.shape, F32), out(w_ffn_in.shape, F32), out(w_ffn_out.shape, F32)],
        [pltpu.VMEM((d_rows, TEAM * units), F32)],
    )
    return (
        hidden_out,
        input_grad,
        dgain[:layers],
        dgain[layers : 2 * layers],
        g_qkv,
        g_out,
        g_in,
        g_down,
    )


def solution(mesh):
    dp, tensor = mesh.devices.shape
    fine = Mesh(mesh.devices.reshape(dp // TEAM, 2, 2, tensor), ("z", "y", "x", "c"))
    rows = ("z", "y", "x")
    in_specs = (
        P(None, rows, None),
        P(),
        P(None, rows),
        P(None, rows),
        P(None, None, rows, "c"),
        P(None, rows, "c"),
        P(None, None, rows, "c"),
        P(None, rows, "c"),
        P(None, rows, None),
    )
    out_specs = (
        P(None, rows, None),
        P(None, rows, None),
        P(None, rows),
        P(None, rows),
        P(None, None, rows, "c"),
        P(None, rows, "c"),
        P(None, None, rows, "c"),
        P(None, rows, "c"),
    )
    return jax.shard_map(shards, mesh=fine, in_specs=in_specs, out_specs=out_specs, check_vma=False)
```

```python
import jax
import jax.numpy as jnp
from jax import lax
from jax.experimental import pallas as pl
from jax.experimental.pallas import tpu as pltpu
from jax.sharding import Mesh
from jax.sharding import PartitionSpec as P

HD = 64
HALF = 64
BLK = 128
TEAM = 4
LOCAL = 2 * TEAM
MASKED = -1e30
BF = jnp.bfloat16
F32 = jnp.float32
CHAINS = 1


def mm(a, b, ca, cb):
    return lax.dot_general(a, b, (((ca,), (cb,)), ((), ())), preferred_element_type=F32)


def hop_team(x, k):
    return lax.ppermute(x, ("y", "x"), [(i, i ^ k) for i in range(TEAM)])


def hop_core(x):
    return lax.ppermute(x, "c", [(0, 1), (1, 0)])


def hop_z(x, s):
    n = lax.axis_size("z")
    return lax.ppermute(x, "z", [(i, i ^ s if n == 4 else (i + s) % n) for i in range(n)])


def step_z(x, by):
    n = lax.axis_size("z")
    return lax.ppermute(x, "z", [(i, i + by) for i in range(n) if 0 <= i + by < n])


def out(shape, dtype):
    return jax.ShapeDtypeStruct(shape, dtype)


def call(name, body, ids, ins, outs, scratch=(), flops=0, after=()):
    ins, after = list(ins), list(after)

    def kernel(*refs):
        n_in, n_out = len(ins), len(outs)
        rest = refs[1 + n_in + len(after) :]
        body(refs[0], refs[1 : 1 + n_in], rest[:n_out], rest[n_out:])

    moved = sum(a.size * a.dtype.itemsize for a in ins) + sum(
        o.size * jnp.dtype(o.dtype).itemsize for o in outs
    )
    vmem = pl.BlockSpec(memory_space=pltpu.VMEM)
    results = pl.pallas_call(
        kernel,
        name=name,
        in_specs=[pl.BlockSpec(memory_space=pltpu.SMEM)] + [vmem] * len(ins)
        + [pl.BlockSpec(memory_space=pl.ANY)] * len(after),
        out_specs=[vmem] * len(outs),
        out_shape=list(outs),
        scratch_shapes=list(scratch),
        compiler_params=pltpu.CompilerParams(vmem_limit_bytes=8 * 1024 * 1024),
        cost_estimate=pl.CostEstimate(flops=flops, bytes_accessed=moved, transcendentals=0),
    )(ids, *ins, *after)
    return list(results)


def aligned(start, size):
    return pl.ds(pl.multiple_of(start, size), size)


def norm_parts(v):
    cent = v - jnp.mean(v, axis=-1, keepdims=True)
    rstd = lax.rsqrt(jnp.mean(cent * cent, axis=-1, keepdims=True) + 1e-05)
    return cent * rstd, rstd


def gelu_parts(gate):
    cdf = 0.5 * (1.0 + lax.erf(gate * 0.7071067811865476))
    return gate * cdf, cdf + gate * jnp.exp(-0.5 * gate * gate) * 0.3989422804014327


def swap_halves(v):
    width = v.shape[-1]
    lane = lax.broadcasted_iota(jnp.int32, v.shape, 1) % HD
    return jnp.where(
        lane < HD // 2, pltpu.roll(v, width - HD // 2, 1), pltpu.roll(v, HD // 2, 1)
    )


def true_rows(ids, n, sub, mb, b):
    blk = (ids[2] ^ (b % 2)) * TEAM + (ids[1] ^ (b // 2))
    return aligned((blk * n + mb) * sub, sub)


def tiles_of(refs, tile):
    rows = refs[0].shape[0]
    per = max(1, tile // rows)
    for first in range(0, len(refs), per):
        group = [r[...] for r in refs[first : first + per]]
        yield slice(first * rows, (first + per) * rows), (
            group[0] if per == 1 else jnp.concatenate(group, axis=0)
        )


def store_partial(p_refs, where, value):
    half = p_refs[0].shape[0]
    which = where.start // half
    p_refs[which][where.start - which * half : where.stop - which * half, :] = value.astype(BF)


def start_attn_body(ids, ins, outs, scratch):
    w_qkv, w_out = ins
    layers, hc = w_qkv.shape[0], w_qkv.shape[3] // TEAM
    for layer in range(layers):
        for k in range(TEAM):
            cols = aligned((ids[1] ^ k) * hc, hc)
            if layer == 0:
                dst, rest, at = outs[k], outs[TEAM + k], 0
            else:
                dst = rest = outs[(layer + 1) * TEAM + k]
                at = 3 * hc
            for i in range(3):
                dst[:, i * hc : (i + 1) * hc] = w_qkv[layer, i, :, cols]
            rest[:, at : at + hc] = w_out[layer, :, cols]


def start_body(ids, ins, outs, scratch):
    tokens, grads, w_in, w_down, owned = ins
    t, c = ids[1], ids[2]
    n, half = tokens.shape[0], tokens.shape[1] // 2
    for src, dst in ((tokens, outs[0]), (grads, outs[1])):
        for mb in range(n):
            dst[mb * half : (mb + 1) * half] = src[mb, aligned(c * half, half)]
    spot = lax.broadcasted_iota(jnp.int32, owned.shape, 1) // w_in.shape[2] == ids[0] * TEAM + t
    outs[2][...] = jnp.where(spot, owned[...], 0.0)
    packs = outs[3:]
    real, units = w_in.shape[3], scratch[0].shape[1] // TEAM
    scratch[0][...] = jnp.zeros(scratch[0].shape, BF)
    for layer in range(w_in.shape[0]):
        for i in range(3):
            scratch[0][:, :real] = w_down[layer] if i == 2 else w_in[layer, i]
            for k in range(TEAM):
                cols = pl.ds(pl.multiple_of((t ^ k) * units, 128), units)
                packs[layer * TEAM + k][:, i * units : (i + 1) * units] = scratch[0][:, cols]


def plane_body(ids, ins, outs, scratch):
    rows = ins[0].shape[0]
    for k in range(TEAM):
        outs[0][aligned((ids[1] ^ k) * rows, rows)] = ins[k][...]


def full_body(ids, ins, outs, scratch):
    rows, nz = ins[0].shape[0], len(ins)
    for s in range(nz):
        src = ids[0] ^ s if nz == 4 else lax.rem(ids[0] - s + nz, nz)
        outs[0][aligned(src * rows, rows)] = ins[s][...]


def add_body(ids, ins, outs, scratch):
    outs[0][...] = total_of(ins).astype(BF)


def qkv_body(row, raw, n, sub):
    def body(ids, ins, outs, scratch):
        blocks, (gains, w, cos, sin) = ins[:LOCAL], ins[LOCAL:]
        a_ref, qkv_ref, lo_ref, hi_ref = outs
        hc = cos.shape[1]
        for where, tile in tiles_of(blocks, 256):
            if raw:
                tile = (norm_parts(tile.astype(F32))[0] * gains[row : row + 1]).astype(BF)
            a_ref[where] = tile
            r = mm(tile, w[:, : 3 * hc], 1, 0)
            cs, sn = cos[where], sin[where]
            q, k = r[:, :hc], r[:, hc : 2 * hc]
            qkv_ref[where, :hc] = (q * cs + swap_halves(q) * sn).astype(BF)
            qkv_ref[where, hc : 2 * hc] = (k * cs + swap_halves(k) * sn).astype(BF)
            qkv_ref[where, 2 * hc :] = r[:, 2 * hc :].astype(BF)
        per = BLK // sub
        for mb in range(n):
            for i in range(per):
                dst = slice(mb * BLK + i * sub, mb * BLK + (i + 1) * sub)
                lo_ref[dst] = qkv_ref[true_rows(ids, n, sub, mb, LOCAL - per + i), hc:]
                hi_ref[dst] = qkv_ref[true_rows(ids, n, sub, mb, i), hc:]

    return body


def fill_band(ids, mb, n, sub, qkv, lo, hi, kb, vb):
    hc = kb.shape[1]
    edge = slice(mb * BLK, (mb + 1) * BLK)
    last = BLK + LOCAL * sub
    kb[:BLK], vb[:BLK] = lo[edge, :hc], lo[edge, hc:]
    kb[last:], vb[last:] = hi[edge, :hc], hi[edge, hc:]
    for b in range(LOCAL):
        src = true_rows(ids, n, sub, mb, b)
        dst = slice(BLK + b * sub, BLK + (b + 1) * sub)
        kb[dst] = qkv[src, hc : 2 * hc]
        vb[dst] = qkv[src, 2 * hc :]


def keys_of(i, windowed):
    return slice(i * BLK + BLK - HALF, (i + 2) * BLK + HALF) if windowed else slice(i * BLK, (i + 3) * BLK)


def allowed_of(mb, i, col, row, windowed):
    keys = keys_of(0, windowed)
    width = keys.stop - keys.start
    ok = col[mb, BLK + i * BLK : 2 * BLK + i * BLK, :] == row[mb, :, i * BLK : i * BLK + width]
    if windowed:
        shape = (BLK, width)
        gap = lax.broadcasted_iota(jnp.int32, shape, 1) - lax.broadcasted_iota(jnp.int32, shape, 0)
        ok = ok & (gap <= 2 * HALF) & (gap >= 0)
    return ok


def take(ids, ref, n, sub, mb, i, lanes):
    per = BLK // sub
    return jnp.concatenate(
        [ref[true_rows(ids, n, sub, mb, per * i + e), lanes] for e in range(per)], axis=0
    )


def put(ids, ref, n, sub, mb, i, lanes, value):
    for e in range(BLK // sub):
        per = BLK // sub
        ref[true_rows(ids, n, sub, mb, per * i + e), lanes] = value[e * sub : (e + 1) * sub]


def probs_of(qh, k, ok):
    s = jnp.where(ok, mm(qh, k, 1, 1), MASKED)
    e = jnp.exp(s - jnp.max(s, axis=1, keepdims=True))
    return e * (1.0 / jnp.sum(e, axis=1, keepdims=True))


def attn_body(windowed, n, sub):
    def body(ids, ins, outs, scratch):
        qkv, lo, hi, col, row, w = ins
        ctx_ref = outs[0]
        kb, vb = scratch
        hc = kb.shape[1]
        head_of = lax.broadcasted_iota(jnp.int32, (BLK, hc), 1) // HD
        for mb in range(n):
            fill_band(ids, mb, n, sub, qkv, lo, hi, kb, vb)
            for i in range(LOCAL * sub // BLK):
                ok = allowed_of(mb, i, col, row, windowed)
                q = take(ids, qkv, n, sub, mb, i, slice(0, hc)) * jnp.asarray(0.125, BF)
                band = keys_of(i, windowed)
                k, v = kb[band], vb[band]
                ctx = jnp.zeros((BLK, hc), F32)
                for h in range(hc // HD):
                    qh = jnp.where(head_of == h, q, jnp.zeros_like(q))
                    p = probs_of(qh, k, ok).astype(BF)
                    ctx = jnp.where(head_of == h, mm(p, v, 1, 0), ctx)
                put(ids, ctx_ref, n, sub, mb, i, slice(0, hc), ctx.astype(BF))
        total = ctx_ref.shape[0]
        for first in range(0, total, 256):
            where = slice(first, first + 256)
            store_partial(outs[1:], where, mm(ctx_ref[where], w[:, w.shape[1] - hc :], 1, 1))

    return body


def fold_body(ids, ins, outs, scratch):
    rows = outs[0].shape[0]
    for k in range(TEAM):
        where = slice(k * rows, (k + 1) * rows)
        both = ins[0][where].astype(F32) + ins[1][where].astype(F32)
        outs[k][...] = both.astype(outs[k].dtype)


def total_of(refs):
    value = refs[0][...].astype(F32)
    for r in refs[1:]:
        value = value + r[...].astype(F32)
    return value


def resid_body(row):
    def body(ids, ins, outs, scratch):
        x = ins[0][...].astype(F32) + total_of(ins[1 : 1 + TEAM])
        if row is None:
            outs[0][...] = x.astype(BF)
        else:
            outs[0][...] = x
            outs[1][...] = (norm_parts(x)[0] * ins[-1][row : row + 1]).astype(BF)

    return body


def mlp_body(ids, ins, outs, scratch):
    blocks, w = ins[:LOCAL], ins[LOCAL]
    b_ref, gu_ref, hid_ref = outs[:3]
    units = w.shape[1] // 3
    for where, tile in tiles_of(blocks, 256):
        b_ref[where] = tile
        gu = mm(tile, w[:, : 2 * units], 1, 0)
        gu_ref[where] = gu
        hid = (gelu_parts(gu[:, :units])[0] * gu[:, units:]).astype(BF)
        hid_ref[where] = hid
        store_partial(outs[3:], where, mm(hid, w[:, 2 * units :], 1, 1))


def mlp_back_body(ids, ins, outs, scratch):
    blocks, (gu_ref, w) = ins[:LOCAL], ins[LOCAL:]
    dy_ref, dgu_ref = outs[:2]
    units = w.shape[1] // 3
    for where, tile in tiles_of(blocks, 256):
        dy_ref[where] = tile
        dhid = mm(tile, w[:, 2 * units :], 1, 0)
        act, slope = gelu_parts(gu_ref[where, :units])
        dgu_ref[where, :units] = (dhid * gu_ref[where, units:] * slope).astype(BF)
        dgu_ref[where, units:] = (dhid * act).astype(BF)
        store_partial(outs[2:], where, mm(dgu_ref[where], w[:, : 2 * units], 1, 1))


def norm_back_body(row):
    def body(ids, ins, outs, scratch):
        dout = total_of(ins[:TEAM])
        v, dy, gains = ins[TEAM:]
        xhat, rstd = norm_parts(v[...].astype(F32))
        outs[0][...] = jnp.sum(dout * xhat, axis=0, keepdims=True)
        dx = dout * gains[row : row + 1]
        m1 = jnp.mean(dx, axis=-1, keepdims=True)
        m2 = jnp.mean(dx * xhat, axis=-1, keepdims=True)
        dv = dy[...].astype(F32) + rstd * (dx - m1 - xhat * m2)
        outs[1][...] = dv
        if len(outs) > 2:
            outs[2][...] = dv.astype(BF)

    return body


def attn_back_body(windowed, n, sub):
    def body(ids, ins, outs, scratch):
        blocks, (qkv, lo, hi, col, row, w, cos, sin) = ins[:LOCAL], ins[LOCAL:]
        dm_ref, dq_ref, dkv_ref, dlo_ref, dhi_ref = outs
        kb, vb, dctx, dqs, dkb, dvb = scratch
        hc = kb.shape[1]
        for where, tile in tiles_of(blocks, 256):
            dm_ref[where] = tile
            dctx[where] = mm(tile, w[:, w.shape[1] - hc :], 1, 0).astype(BF)
        head_of = lax.broadcasted_iota(jnp.int32, (BLK, hc), 1) // HD
        last = BLK + LOCAL * sub
        for mb in range(n):
            fill_band(ids, mb, n, sub, qkv, lo, hi, kb, vb)
            dkb[...] = jnp.zeros(dkb.shape, F32)
            dvb[...] = jnp.zeros(dvb.shape, F32)
            for i in range(LOCAL * sub // BLK):
                ok = allowed_of(mb, i, col, row, windowed)
                q = take(ids, qkv, n, sub, mb, i, slice(0, hc)) * jnp.asarray(0.125, BF)
                do = take(ids, dctx, n, sub, mb, i, slice(0, hc))
                band = keys_of(i, windowed)
                k, v = kb[band], vb[band]
                dq = jnp.zeros((BLK, hc), F32)
                dk = dkb[band]
                dv = dvb[band]
                for h in range(hc // HD):
                    mine = head_of == h
                    qh = jnp.where(mine, q, jnp.zeros_like(q))
                    doh = jnp.where(mine, do, jnp.zeros_like(do))
                    p = probs_of(qh, k, ok)
                    dp = mm(doh, v, 1, 1)
                    ds = (p * (dp - jnp.sum(p * dp, axis=1, keepdims=True))).astype(BF)
                    dq = jnp.where(mine, mm(ds, k, 1, 0), dq)
                    dk = dk + mm(ds, qh, 0, 0)
                    dv = dv + mm(p.astype(BF), doh, 0, 0)
                put(ids, dqs, n, sub, mb, i, slice(0, hc), 0.125 * dq)
                dkb[band] = dk
                dvb[band] = dv
            edge = slice(mb * BLK, (mb + 1) * BLK)
            dlo_ref[edge, :hc] = dkb[:BLK].astype(BF)
            dlo_ref[edge, hc:] = dvb[:BLK].astype(BF)
            dhi_ref[edge, :hc] = dkb[last:].astype(BF)
            dhi_ref[edge, hc:] = dvb[last:].astype(BF)
            for b in range(LOCAL):
                src = slice(BLK + b * sub, BLK + (b + 1) * sub)
                dst = true_rows(ids, n, sub, mb, b)
                dkv_ref[dst, :hc] = dkb[src]
                dkv_ref[dst, hc:] = dvb[src]
        for first in range(0, dqs.shape[0], 256):
            where = slice(first, first + 256)
            g = dqs[where]
            dq_ref[where] = (g * cos[where] + swap_halves(g * sin[where])).astype(BF)

    return body


def qkv_back_body(n, sub):
    def body(ids, ins, outs, scratch):
        dq, dkv, from_next, from_prev, w, cos, sin = ins
        dqkv_ref = outs[0]
        acc = scratch[0]
        hc = cos.shape[1]
        acc[...] = dkv[...]
        per = BLK // sub
        for mb in range(n):
            for i in range(per):
                src = slice(mb * BLK + i * sub, mb * BLK + (i + 1) * sub)
                first = true_rows(ids, n, sub, mb, i)
                acc[first] = acc[first] + from_prev[src].astype(F32)
                end = true_rows(ids, n, sub, mb, LOCAL - per + i)
                acc[end] = acc[end] + from_next[src].astype(F32)
        for first in range(0, acc.shape[0], 256):
            where = slice(first, first + 256)
            g = acc[where, :hc]
            dqkv_ref[where, :hc] = dq[where]
            dqkv_ref[where, hc : 2 * hc] = (g * cos[where] + swap_halves(g * sin[where])).astype(BF)
            dqkv_ref[where, 2 * hc :] = acc[where, hc:].astype(BF)
            store_partial(outs[1:], where, mm(dqkv_ref[where], w[:, : 3 * hc], 1, 1))

    return body


def weight_grad_body(ids, ins, outs, scratch):
    full = scratch[0]
    chains = [ins[i : i + 4] for i in range(0, len(ins), 4)]
    cut = chains[0][1].shape[1]
    step = 256
    for first in range(0, full.shape[0], step):
        where = slice(first, first + step)
        full[where, :cut] = sum(mm(c[0][:, where], c[1][...], 0, 0) for c in chains).astype(BF)
        full[where, cut:] = sum(mm(c[2][:, where], c[3][...], 0, 0) for c in chains).astype(BF)
    nz = len(outs)
    span = outs[0].shape[0]
    for s in range(nz):
        dst = ids[0] ^ s if nz == 4 else lax.rem(ids[0] + s, nz)
        outs[s][...] = full[aligned(dst * span, span)]


def plane_sum_body(ids, ins, outs, scratch):
    scratch[0][...] = total_of(ins)
    rows = outs[0].shape[0]
    for k in range(TEAM):
        outs[k][...] = scratch[0][aligned((ids[1] ^ k) * rows, rows)].astype(outs[k].dtype)


def finish_body(ids, ins, outs, scratch):
    g_qkv, g_out, g_in, g_down = outs
    wide = scratch[0]
    layers, hc = g_qkv.shape[0], g_qkv.shape[3] // TEAM
    real, units = g_down.shape[2], wide.shape[1] // TEAM
    for layer in range(layers):
        attn = ins[layer * TEAM : (layer + 1) * TEAM]
        ffn = ins[(layers + layer) * TEAM : (layers + layer + 1) * TEAM]
        for k in range(TEAM):
            cols = aligned((ids[1] ^ k) * hc, hc)
            for i in range(3):
                g_qkv[layer, i, :, cols] = attn[k][:, i * hc : (i + 1) * hc].astype(F32)
            g_out[layer, :, cols] = attn[k][:, 3 * hc :].astype(F32)
        for i in range(3):
            for k in range(TEAM):
                cols = pl.ds(pl.multiple_of((ids[1] ^ k) * units, 128), units)
                wide[:, cols] = ffn[k][:, i * units : (i + 1) * units].astype(F32)
            if i == 2:
                g_down[layer] = wide[:, :real]
            else:
                g_in[layer, i] = wide[:, :real]


def join_body(ids, ins, outs, scratch):
    n, half = outs[0].shape[0], outs[0].shape[1] // 2
    c = ids[2]
    for mb in range(n):
        rows = slice(mb * half, (mb + 1) * half)
        outs[0][mb, aligned(c * half, half)] = ins[0][rows]
        outs[0][mb, aligned((1 - c) * half, half)] = ins[1][rows]


def shards(tokens, cu_seqlens, attn_gain, mlp_gain, w_qkv, w_attn_out, w_ffn_in, w_ffn_out, out_grad):
    nz = lax.axis_size("z")
    z = lax.axis_index("z")
    t = lax.axis_index("y") * 2 + lax.axis_index("x")
    c = lax.axis_index("c")
    ids = jnp.stack([z, t, c]).astype(jnp.int32)
    micro, chip_rows, feat = tokens.shape
    layers, d_rows = w_qkv.shape[0], w_qkv.shape[2]
    hc = w_qkv.shape[3] // TEAM
    sub = chip_rows // 2
    real = w_ffn_in.shape[3]
    units = -(-real // (TEAM * 128)) * 128
    team_rows = TEAM * chip_rows
    per_chain = micro // CHAINS
    n = per_chain
    own = n * sub
    rows = LOCAL * own
    aw, fw = 4 * hc, 3 * units

    owned = jnp.concatenate([attn_gain, mlp_gain, attn_gain, mlp_gain], axis=0)[: 4 * layers]
    owned = jnp.tile(owned.astype(F32), (1, feat // d_rows))
    packs_a = call(
        "start_attn", start_attn_body, ids, [w_qkv, w_attn_out],
        [out((d_rows, 3 * hc), BF)] * TEAM
        + [out((d_rows, hc), BF)] * TEAM
        + [out((d_rows, aw), BF)] * ((layers - 1) * TEAM),
    )

    def plane_of(pieces, name, after=()):
        width = pieces[0].shape[1]
        got = [pieces[0]] + [hop_team(pieces[k], k) for k in range(1, TEAM)]
        return call("plane_" + name, plane_body, ids, got, [out((TEAM * d_rows, width), BF)], after=after)[0]

    plane_qkv = plane_of(packs_a[:TEAM], "q0")
    tok_own, grad_own, gains, *packs_f = call(
        "start", start_body, ids, [tokens, out_grad, w_ffn_in, w_ffn_out, owned],
        [out((micro * sub, feat), BF)] * 2
        + [out((4 * layers, feat), F32)]
        + [out((d_rows, fw), BF)] * (layers * TEAM),
        [pltpu.VMEM((d_rows, TEAM * units), BF)], after=[plane_qkv],
    )
    plane_out = plane_of(packs_a[TEAM : 2 * TEAM], "o0")

    def blocks_of(x):
        mine = [x] + [hop_team(x, k) for k in range(1, TEAM)]
        return mine + [hop_core(b) for b in mine]

    def chain_rows(x, i):
        return x[i * own : (i + 1) * own]

    tok_blocks = [blocks_of(chain_rows(tok_own, i)) for i in range(CHAINS)]

    def full_of(plane, name, relay=True):
        width = plane.shape[1]
        if nz == 4 and relay:
            far = hop_z(plane, 2)
            planes = [plane, hop_z(plane, 1), far, hop_z(far, 1)]
        else:
            far = plane
            planes = [plane] + [hop_z(plane, s) for s in range(1, nz)]
        full = call("full_" + name, full_body, ids, planes, [out((nz * TEAM * d_rows, width), BF)])[0]
        return full, far

    gains = sum([gains] + [hop_team(gains, k) for k in range(1, TEAM)])
    gains = sum([gains] + [hop_z(gains, s) for s in range(1, nz)])

    def pack(kind, layer):
        if kind == 0:
            return packs_a[(layer + 1) * TEAM : (layer + 2) * TEAM]
        return packs_f[layer * TEAM : (layer + 1) * TEAM]

    w_q0 = full_of(plane_qkv, "q0", False)[0]
    w_o0 = full_of(plane_out, "o0", False)[0]
    planes_a, planes_f = [plane_out], [plane_of(pack(1, 0), "f0")]
    attn_w, ffn_w, far_f = [(w_q0, w_o0)], [], []
    for i in range(layers):
        if i > 0:
            planes_a.append(plane_of(pack(0, i), "a" + str(i), ffn_w[i - 1 :]))
            full = full_of(planes_a[i], "a" + str(i), False)[0]
            attn_w.append((full, full))
            planes_f.append(plane_of(pack(1, i), "f" + str(i), [full]))
        w, far = full_of(planes_f[i], "f" + str(i))
        ffn_w.append(w)
        far_f.append(far)
    grad_blocks = [blocks_of(chain_rows(grad_own, i)) for i in range(CHAINS)]

    band_index = z * team_rows - BLK + jnp.arange(team_rows + 2 * BLK, dtype=jnp.int32)
    inside = (band_index >= 0) & (band_index < cu_seqlens[0, -1])
    docs = jnp.sum((band_index[None, :, None] >= cu_seqlens[:, None, 1:-1]).astype(jnp.int32), axis=2)
    docs = jnp.where(inside[None], docs, -1)
    block = jnp.arange(LOCAL, dtype=jnp.int32)
    true_block = ((block % TEAM) ^ t) * 2 + ((block // TEAM) ^ c)
    index = z * team_rows + true_block[:, None] * sub + jnp.arange(sub, dtype=jnp.int32)[None]
    begin = jnp.max(
        jnp.where(
            index[:, None, :, None] >= cu_seqlens[None, :, None, :-1], cu_seqlens[None, :, None, :-1], 0
        ),
        axis=3,
    )
    offsets = (index[:, None] - begin).astype(F32)
    lane = jnp.arange(hc, dtype=jnp.int32) % HD
    sign = jnp.where(lane < HD // 2, -1.0, 1.0)

    state = []
    for i in range(CHAINS):
        mbs = slice(i * n, (i + 1) * n)
        tables = []
        for layer in range(layers):
            base = 10000.0 if layer % 2 == 0 else 160000.0
            inv = base ** (-((lane % (HD // 2)).astype(F32) * 2.0 / HD))
            ang = offsets[:, mbs].reshape(rows, 1) * inv
            tables.append((jnp.cos(ang), jnp.sin(ang) * sign))
        state.append(
            {
                "tables": tables,
                "col": docs[mbs, :, None],
                "row": [docs[mbs, None, BLK - HALF :], docs[mbs, None, :]],
                "x": chain_rows(tok_own, i),
                "blocks": tok_blocks[i],
                "saved": [],
            }
        )

    partial_out = [out((rows // 2, feat), BF)] * 2
    band = pltpu.VMEM((team_rows + 2 * BLK, hc), BF)
    band32 = pltpu.VMEM((team_rows + 2 * BLK, hc), F32)

    def fold(parts, name, after=()):
        got = hop_core(parts[1])
        h = call(
            "fold_" + name, fold_body, ids, [parts[0], got],
            [out((own, feat), F32)] + [out((own, feat), BF)] * (TEAM - 1), after=after,
        )
        return [h[0]] + [hop_team(h[k], k) for k in range(1, TEAM)]

    def forward_attn(st, layer):
        windowed = layer % 2 == 0
        w3, wo = attn_w[layer]
        cos, sin = st["tables"][layer]
        a, qkv, lo, hi = call(
            "qkv", qkv_body(layer, layer == 0, n, sub), ids, st["blocks"] + [gains, w3, cos, sin],
            [out((rows, feat), BF), out((rows, 3 * hc), BF)] + [out((n * BLK, 2 * hc), BF)] * 2,
            flops=2 * rows * feat * 3 * hc, after=[planes_f[0]] if layer == 0 else [],
        )
        lo, hi = step_z(lo, 1), step_z(hi, -1)
        ctx, *parts = call(
            "attn", attn_body(windowed, n, sub), ids, [qkv, lo, hi, st["col"], st["row"][layer % 2], wo],
            [out((rows, hc), BF)] + partial_out, [band] * 2, flops=4 * rows * feat * hc,
            after=[far_f[layer]] if layer > 0 else [],
        )
        terms = fold(parts, "attn")
        mid, b = call(
            "mid", resid_body(layers + layer), ids, [st["x"]] + terms + [gains],
            [out((own, feat), F32), out((own, feat), BF)],
        )
        st["saved"].append([st["x"], a, qkv, lo, hi, ctx, mid])
        st["x"] = mid
        st["blocks"] = blocks_of(b)

    def forward_mlp(st, layer):
        b, gu, hid, *parts = call(
            "mlp", mlp_body, ids, st["blocks"] + [ffn_w[layer]],
            [out((rows, feat), BF), out((rows, 2 * units), F32), out((rows, units), BF)] + partial_out,
            flops=6 * rows * feat * units,
        )
        st["saved"][layer] += [b, gu, hid]
        terms = fold(parts, "mlp")
        if layer + 1 < layers:
            st["x"], a = call(
                "next", resid_body(layer + 1), ids, [st["x"]] + terms + [gains],
                [out((own, feat), F32), out((own, feat), BF)],
                after=[attn_w[layer + 1][0], planes_f[layer + 1]],
            )
            st["blocks"] = blocks_of(a)
        else:
            st["x"] = call("last", resid_body(None), ids, [st["x"]] + terms, [out((own, feat), BF)])[0]

    for layer in range(layers):
        for st in state:
            forward_attn(st, layer)
        for st in state:
            forward_mlp(st, layer)

    def join(parts, dtype):
        x = parts[0] if CHAINS == 1 else jnp.concatenate(parts, axis=0)
        return call("join", join_body, ids, [x, hop_core(x)], [out((micro, chip_rows, feat), dtype)])[0]

    hidden_out = join([st["x"] for st in state], BF)

    for i, st in enumerate(state):
        st["dy"] = chain_rows(grad_own, i)
        st["blocks"] = grad_blocks[i]

    def weight_pieces(ins, width, name):
        return call(
            "wgrad_" + name, weight_grad_body, ids, ins, [out((TEAM * d_rows, width), BF)] * nz,
            [pltpu.VMEM((nz * TEAM * d_rows, width), BF)], flops=2 * rows * CHAINS * feat * width,
        )

    def relay(pieces, name):
        if nz != 4:
            return [pieces[0]] + [hop_z(pieces[s], s) for s in range(1, nz)]
        near = hop_z(pieces[1], 1)
        far = call("relay_" + name, add_body, ids, [pieces[2], hop_z(pieces[3], 1)], [out(pieces[2].shape, BF)])[0]
        return [pieces[0], near, hop_z(far, 2)]

    def z_sum(got, name):
        width = got[0].shape[1]
        mine = call(
            "zsum_" + name, plane_sum_body, ids, got,
            [out((d_rows, width), F32)] + [out((d_rows, width), BF)] * (TEAM - 1),
            [pltpu.VMEM((TEAM * d_rows, width), F32)],
        )
        return [mine[0]] + [hop_team(mine[k], k) for k in range(1, TEAM)]

    gain_rows = [None] * (2 * layers)

    def add_gain(row, dg):
        gain_rows[row] = dg if gain_rows[row] is None else gain_rows[row] + dg

    attn_parts, ffn_parts = [None] * layers, [None] * layers
    st = state[0]
    wait_mlp, wait_fold, wait_mid, wait_attn = [], [], [], []
    for layer in reversed(range(layers)):
        w3, wo = attn_w[layer]
        cos, sin = st["tables"][layer]
        x_in, a, qkv, lo, hi, ctx, mid, b, gu, hid = st["saved"][layer]
        dy, dgu, *parts = call(
            "mlp_back", mlp_back_body, ids, st["blocks"] + [gu, ffn_w[layer]],
            [out((rows, feat), BF), out((rows, 2 * units), BF)] + partial_out,
            flops=6 * rows * feat * units, after=wait_mlp,
        )
        terms = fold(parts, "mlp_back", wait_fold)
        pieces = weight_pieces([b, dgu, dy, hid], fw, "f" + str(layer))
        dg, dmid, dmb = call(
            "mid_back", norm_back_body(layers + layer), ids, terms + [mid, st["dy"], gains],
            [out((1, feat), F32), out((own, feat), F32), out((own, feat), BF)],
            after=pieces + wait_mid,
        )
        add_gain(layers + layer, dg)
        relayed = relay(pieces, "f" + str(layer))
        dm, dq, dkv, dlo, dhi = call(
            "attn_back", attn_back_body(layer % 2 == 0, n, sub), ids,
            blocks_of(dmb) + [qkv, lo, hi, st["col"], st["row"][layer % 2], wo, cos, sin],
            [out((rows, feat), BF), out((rows, hc), BF), out((rows, 2 * hc), F32)]
            + [out((n * BLK, 2 * hc), BF)] * 2,
            [band] * 2 + [pltpu.VMEM((rows, hc), BF), pltpu.VMEM((rows, hc), F32)] + [band32] * 2,
            flops=6 * rows * feat * hc,
        )
        from_next, from_prev = step_z(dlo, -1), step_z(dhi, 1)
        ffn_parts[layer] = z_sum(relayed, "f" + str(layer))
        dqkv, *parts = call(
            "qkv_back", qkv_back_body(n, sub), ids, [dq, dkv, from_next, from_prev, w3, cos, sin],
            [out((rows, 3 * hc), BF)] + partial_out, [pltpu.VMEM((rows, 2 * hc), F32)],
            flops=6 * rows * feat * hc,
            after=ffn_parts[layer][:1] + wait_attn + ([st["x"]] if layer + 1 == layers else []),
        )
        pieces = weight_pieces([a, dqkv, dm, ctx], aw, "a" + str(layer))
        terms = fold(parts, "qkv_back", pieces if layer == 0 else [])
        if layer == 0:
            got = [pieces[0]] + [hop_z(pieces[s], s) for s in range(1, nz)]
            pieces = got
        low = [out((own, feat), BF)] if layer > 0 else []
        dg, st["dy"], *dyb = call(
            "in_back", norm_back_body(layer), ids, terms + [x_in, dmid, gains],
            [out((1, feat), F32), out((own, feat), F32)] + low, after=pieces,
        )
        add_gain(layer, dg)
        if layer > 0:
            st["blocks"] = blocks_of(dyb[0])
            relayed = relay(pieces, "a" + str(layer))
            attn_parts[layer] = z_sum(relayed, "a" + str(layer))
            wait_mlp = relayed[1:2]
            wait_fold = ffn_parts[layer]
            wait_mid = attn_parts[layer][:1]
            wait_attn = attn_parts[layer]
        else:
            attn_parts[layer] = z_sum(got, "a" + str(layer))

    input_grad = join([st["dy"] for st in state], F32)

    dgain = jnp.concatenate(gain_rows + gain_rows, axis=0)[: 4 * layers]
    dgain = dgain + hop_core(dgain)
    dgain = sum([dgain] + [hop_team(dgain, k) for k in range(1, TEAM)])
    dgain = sum([dgain] + [hop_z(dgain, s) for s in range(1, nz)])
    dgain = lax.dynamic_slice_in_dim(dgain, (z * TEAM + t) * d_rows, d_rows, axis=1)

    g_qkv, g_out, g_in, g_down = call(
        "finish", finish_body, ids, sum(attn_parts, []) + sum(ffn_parts, []),
        [out(w_qkv.shape, F32), out(w_attn_out.shape, F32), out(w_ffn_in.shape, F32), out(w_ffn_out.shape, F32)],
        [pltpu.VMEM((d_rows, TEAM * units), F32)],
    )
    return (
        hidden_out,
        input_grad,
        dgain[:layers],
        dgain[layers : 2 * layers],
        g_qkv,
        g_out,
        g_in,
        g_down,
    )


def solution(mesh):
    dp, tensor = mesh.devices.shape
    fine = Mesh(mesh.devices.reshape(dp // TEAM, 2, 2, tensor), ("z", "y", "x", "c"))
    rows = ("z", "y", "x")
    in_specs = (
        P(None, rows, None),
        P(),
        P(None, rows),
        P(None, rows),
        P(None, None, rows, "c"),
        P(None, rows, "c"),
        P(None, None, rows, "c"),
        P(None, rows, "c"),
        P(None, rows, None),
    )
    out_specs = (
        P(None, rows, None),
        P(None, rows, None),
        P(None, rows),
        P(None, rows),
        P(None, None, rows, "c"),
        P(None, rows, "c"),
        P(None, None, rows, "c"),
        P(None, rows, "c"),
    )
    return jax.shard_map(shards, mesh=fine, in_specs=in_specs, out_specs=out_specs, check_vma=False)
```
